32 devices in a mesh: batch: 4 (over y, x), seq: 2 (over core), tensor: 4 (over z).
Axes of the slice: x: 2, y: 2, z: 4, core: 2. Of those that a mesh axis runs over, the one named last changes fastest.
Arguments:
- layer_in: bfloat16 [4, 1024, 2304], P('batch', 'seq'), may hold values from -6 to 6
- cotangent: bfloat16 [4, 1024, 2304], P('batch', 'seq'), may hold values from -6 to 6
- qkv_weight: float32 [2304, 4, 1024], P(('batch', 'seq'), 'tensor')
- out_weight: float32 [2048, 2304], P('tensor', ('batch', 'seq')), may hold values from -0.125 to 0.125
- gate_up_weight: float32 [2304, 2, 9216], P(('batch', 'seq'), None, 'tensor'), may hold values from -0.125 to 0.125
- down_weight: float32 [9216, 2304], P('tensor', ('batch', 'seq')), may hold values from -0.0625 to 0.0625
- norm_gains: float32 [4, 2304], P(None, ('batch', 'seq')), may hold values from -0.1 to 0.1
- qkv_first: float32 [2304, 4, 1024], P(('batch', 'seq'), 'tensor'), may hold values from -40 to 40
- out_first: float32 [2048, 2304], P('tensor', ('batch', 'seq')), may hold values from -112 to 112
- gate_up_first: float32 [2304, 2, 9216], P(('batch', 'seq'), None, 'tensor'), may hold values from -40 to 40
- down_first: float32 [9216, 2304], P('tensor', ('batch', 'seq')), may hold values from -80 to 80
- gains_first: float32 [4, 2304], P(None, ('batch', 'seq')), may hold values from -80 to 80
- qkv_second: float32 [2304, 4, 1024], P(('batch', 'seq'), 'tensor'), may hold values from 51.2 to 204.8
- out_second: float32 [2048, 2304], P('tensor', ('batch', 'seq')), may hold values from 409.6 to 1638.4
- gate_up_second: float32 [2304, 2, 9216], P(('batch', 'seq'), None, 'tensor'), may hold values from 51.2 to 204.8
- down_second: float32 [9216, 2304], P('tensor', ('batch', 'seq')), may hold values from 204.8 to 819.2
- gains_second: float32 [4, 2304], P(None, ('batch', 'seq')), may hold values from 102.4 to 409.6
Outputs:
- layer_out: bfloat16 [4, 1024, 2304], P('batch', 'seq')
- input_grad: float32 [4, 1024, 2304], P('batch', 'seq')
- qkv_grad: float32 [2304, 4, 1024], P(('batch', 'seq'), 'tensor')
- out_grad: float32 [2048, 2304], P('tensor', ('batch', 'seq'))
- gate_up_grad: float32 [2304, 2, 9216], P(('batch', 'seq'), None, 'tensor')
- down_grad: float32 [9216, 2304], P('tensor', ('batch', 'seq'))
- gains_grad: float32 [4, 2304], P(None, ('batch', 'seq'))
- qkv_weight_new: float32 [2304, 4, 1024], P(('batch', 'seq'), 'tensor')
- out_weight_new: float32 [2048, 2304], P('tensor', ('batch', 'seq'))
- gate_up_weight_new: float32 [2304, 2, 9216], P(('batch', 'seq'), None, 'tensor')
- down_weight_new: float32 [9216, 2304], P('tensor', ('batch', 'seq'))
- norm_gains_new: float32 [4, 2304], P(None, ('batch', 'seq'))
- qkv_first_new: float32 [2304, 4, 1024], P(('batch', 'seq'), 'tensor')
- out_first_new: float32 [2048, 2304], P('tensor', ('batch', 'seq'))
- gate_up_first_new: float32 [2304, 2, 9216], P(('batch', 'seq'), None, 'tensor')
- down_first_new: float32 [9216, 2304], P('tensor', ('batch', 'seq'))
- gains_first_new: float32 [4, 2304], P(None, ('batch', 'seq'))
- qkv_second_new: float32 [2304, 4, 1024], P(('batch', 'seq'), 'tensor')
- out_second_new: float32 [2048, 2304], P('tensor', ('batch', 'seq'))
- gate_up_second_new: float32 [2304, 2, 9216], P(('batch', 'seq'), None, 'tensor')
- down_second_new: float32 [9216, 2304], P('tensor', ('batch', 'seq'))
- gains_second_new: float32 [4, 2304], P(None, ('batch', 'seq'))
The draws below stay inside these ranges and needn't reach their ends.
All inputs are finite; a program needn't handle non-finite values.
Results may differ from the reference program's by a relative error of at most 0.025.
Values may be sent and summed in bfloat16 or wider, within the bound.
No kernel may reach another device: no remote copies, remote signals or barrier semaphores. Data moves between devices by JAX's collectives and lax.ppermute only.
A program may use at most 320 MiB of HBM per device.

```python
import math
import jax
import jax.numpy as jnp
from jax import lax

D = 2304
HEADS = 8
KV_HEADS = 4
HEAD_DIM = 256
FF = 9216
TOK_DEV = 512
WIN_BLOCKS = 4
STEP = 10
GROUP = 2
SEQS = 4
LENGTH = 1024
WINDOW = 2048


def draw_qkv_weight(key, part):
    columns = (GROUP + 2) * HEAD_DIM
    unscaled = jnp.clip(jax.random.normal(key, (D, KV_HEADS, columns), jnp.float32), -4.0, 4.0)
    return unscaled * D ** (-0.5)


def level_of(key, shape, pieces, least, largest):
    loudness, own = 1.0, jax.random.fold_in(key, 6)
    for axis_at, parts in pieces:
        draws = jnp.exp(jax.random.uniform(jax.random.fold_in(own, axis_at), (parts,), jnp.float32, least / len(pieces), largest / len(pieces)))
        loudness = loudness * jnp.repeat(draws, shape[axis_at] // parts).reshape([-1 if axis == axis_at else 1 for axis in range(len(shape))])
    return loudness


def centred(stream_key, dims, width, limit, pieces=(), kind=jnp.bfloat16):
    level = level_of(stream_key, dims, pieces, -0.22, 0.18) if pieces else 1.0
    array = jax.random.normal(stream_key, dims, jnp.float32) * width * level
    return jnp.minimum(jnp.maximum(array, -limit), limit).astype(kind)


def setup_inputs(seed: int = 0) -> dict:
    key_of = jax.random.split(jax.random.key(seed), 18)
    return {
        "layer_in": centred(key_of[0], (SEQS, LENGTH, D), 1.0, 6.0, ((0, 4), (1, 2))),
        "cotangent": centred(key_of[1], (SEQS, LENGTH, D), 1.0, 6.0, ((0, 4), (1, 2))),
        "qkv_weight": draw_qkv_weight(jax.random.fold_in(key_of[17], 71), 0),
        "out_weight": centred(key_of[3], (HEADS * HEAD_DIM, D), (HEADS * HEAD_DIM) ** -0.5, 0.125, ((0, 4), (1, 8)), jnp.float32),
        "gate_up_weight": centred(key_of[4], (D, 2, FF), D ** -0.5, 0.125, ((0, 8), (2, 4)), jnp.float32),
        "down_weight": centred(key_of[5], (FF, D), FF ** -0.5, 0.0625, ((0, 4), (1, 8)), jnp.float32),
        "norm_gains": jnp.clip(jax.random.uniform(key_of[6], (4, D), jnp.float32, -0.1, 0.1) * level_of(key_of[6], (4, D), ((1, 8),), -0.4, 0.0), -0.1, 0.1),
        "qkv_first": centred(key_of[7], (D, KV_HEADS, (GROUP + 2) * HEAD_DIM), (0.1 * (SEQS * LENGTH) ** 0.5), 40.0, ((0, 8), (1, 4)), jnp.float32),
        "out_first": centred(key_of[8], (HEADS * HEAD_DIM, D), (0.28 * (SEQS * LENGTH) ** 0.5), 112.0, ((0, 4), (1, 8)), jnp.float32),
        "gate_up_first": centred(key_of[9], (D, 2, FF), (0.1 * (SEQS * LENGTH) ** 0.5), 40.0, ((0, 8), (2, 4)), jnp.float32),
        "down_first": centred(key_of[10], (FF, D), (0.2 * (SEQS * LENGTH) ** 0.5), 80.0, ((0, 4), (1, 8)), jnp.float32),
        "gains_first": centred(key_of[11], (4, D), (0.2 * (SEQS * LENGTH) ** 0.5), 80.0, ((1, 8),), jnp.float32),
        "qkv_second": jnp.clip(jnp.exp(math.log(204.8) - 1.3862944 * jax.random.uniform(key_of[12], (D, KV_HEADS, (GROUP + 2) * HEAD_DIM), jnp.float32) ** level_of(key_of[12], (D, KV_HEADS, (GROUP + 2) * HEAD_DIM), ((0, 8), (1, 4)), -0.2, 0.2)), 51.2, 204.8),
        "out_second": jnp.clip(jnp.exp(math.log(1638.4) - 1.3862944 * jax.random.uniform(key_of[13], (HEADS * HEAD_DIM, D), jnp.float32) ** level_of(key_of[13], (HEADS * HEAD_DIM, D), ((0, 4), (1, 8)), -0.2, 0.2)), 409.6, 1638.4),
        "gate_up_second": jnp.clip(jnp.exp(math.log(204.8) - 1.3862944 * jax.random.uniform(key_of[14], (D, 2, FF), jnp.float32) ** level_of(key_of[14], (D, 2, FF), ((0, 8), (2, 4)), -0.2, 0.2)), 51.2, 204.8),
        "down_second": jnp.clip(jnp.exp(math.log(819.2) - 1.3862944 * jax.random.uniform(key_of[15], (FF, D), jnp.float32) ** level_of(key_of[15], (FF, D), ((0, 4), (1, 8)), -0.2, 0.2)), 204.8, 819.2),
        "gains_second": jnp.clip(jnp.exp(math.log(409.6) - 1.3862944 * jax.random.uniform(key_of[16], (4, D), jnp.float32) ** level_of(key_of[16], (4, D), ((1, 8),), -0.2, 0.2)), 102.4, 409.6),
    }


norm_eps = 1e-06
soft_cap = 50.0
learn_rate = 0.02
decay_rate = 0.1
beta_first = 0.9
beta_second = 0.95
adam_eps = 1e-08
gelu_coef = 0.7978845608028654

def rounded(values):
    return lax.optimization_barrier(values.astype(jnp.bfloat16))

def rms_norm(values, gain):
    scale = lax.rsqrt(lax.optimization_barrier(jnp.mean(values * values, axis=-1, keepdims=True)) + norm_eps)
    return values * scale * (1.0 + gain)

def norm_back(values, gain, upstream):
    _, pullback = jax.vjp(rms_norm, values, gain)
    return pullback(upstream)

def gelu_tanh(values):
    inner = gelu_coef * (values + 0.044715 * values * values * values)
    return 0.5 * values * (1.0 + jnp.tanh(inner))

def geglu(gate, up_part):
    return gelu_tanh(gate) * up_part

def rope_tables(positions, head_size):
    half = head_size // 2
    exponent = jnp.arange(half, dtype=jnp.float32) * (2.0 / head_size)
    freqs = 10000.0 ** (-exponent)
    angles = positions.astype(jnp.float32)[:, None] * freqs[None, :]
    return (jnp.cos(angles), jnp.sin(angles))

def rotate(values, cosine, sine):
    half = values.shape[-1] // 2
    first = values[..., :half]
    second = values[..., half:]
    cosine = cosine[:, None, :]
    sine = sine[:, None, :]
    return jnp.concatenate([first * cosine - second * sine, second * cosine + first * sine], axis=-1)

def adam_step(weight, grad, first, second, decay):
    first_new = beta_first * first + (1.0 - beta_first) * grad
    second_new = beta_second * second + (1.0 - beta_second) * grad * grad
    first_hat = first_new / (1.0 - beta_first ** STEP)
    second_hat = second_new / (1.0 - beta_second ** STEP)
    weight_new = weight - learn_rate * (first_hat / (jnp.sqrt(second_hat) + adam_eps) + decay * weight)
    return (weight_new, first_new, second_new)

def reference(layer_in, cotangent, qkv_weight, out_weight, gate_up_weight, down_weight, norm_gains, qkv_first, out_first, gate_up_first, down_first, gains_first, qkv_second, out_second, gate_up_second, down_second, gains_second):
    qkv_rounded = rounded(qkv_weight).reshape(D, KV_HEADS * (GROUP + 2) * HEAD_DIM)
    out_rounded = rounded(out_weight)
    gate_up_rounded = rounded(gate_up_weight).reshape(D, 2 * FF)
    down_rounded = rounded(down_weight)
    gains_rounded = rounded(norm_gains).astype(jnp.float32)
    score_scale = HEAD_DIM ** (-0.5)
    offsets = jnp.arange(LENGTH, dtype=jnp.int32)
    cosine, sine = rope_tables(offsets, HEAD_DIM)
    pad_rows = WIN_BLOCKS * TOK_DEV
    ext_rows = (WIN_BLOCKS + 1) * TOK_DEV
    block_count = LENGTH // TOK_DEV
    block_ids = jnp.arange(block_count, dtype=jnp.int32)

    def block_mask(start):
        query_pos = start + jnp.arange(TOK_DEV, dtype=jnp.int32)
        key_pos = start - pad_rows + jnp.arange(ext_rows, dtype=jnp.int32)
        spread = query_pos[:, None] - key_pos[None, :]
        return (spread >= 0) & (spread < WINDOW) & (key_pos >= 0)[None, :]

    def padded(values):
        return jnp.concatenate([jnp.zeros((pad_rows, HEAD_DIM), values.dtype), values], axis=0)

    def scores_of(query_block, key_block):
        raw = jnp.einsum('igd,jd->gij', query_block.astype(jnp.float32), key_block.astype(jnp.float32)) * score_scale
        return soft_cap * jnp.tanh(raw / soft_cap)

    def group_forward(operands):
        query_group, key_group, value_group = operands
        keys_pad = padded(key_group)
        values_pad = padded(value_group)

        def one_block(block):
            start = block * TOK_DEV
            query_block = lax.dynamic_slice_in_dim(query_group, start, TOK_DEV, 0)
            key_block = lax.dynamic_slice_in_dim(keys_pad, start, ext_rows, 0)
            value_block = lax.dynamic_slice_in_dim(values_pad, start, ext_rows, 0)
            allowed = block_mask(start)[None]
            capped = scores_of(query_block, key_block)
            totals = lax.optimization_barrier(jnp.sum(jnp.where(allowed, jnp.exp(capped), 0.0), axis=-1))
            log_sums = jnp.log(totals)
            probs = rounded(jnp.where(allowed, jnp.exp(capped - log_sums[:, :, None]), 0.0))
            attended = rounded(jnp.einsum('gij,jd->igd', probs.astype(jnp.float32), value_block.astype(jnp.float32)))
            return (attended, log_sums)
        attended, log_sums = lax.map(one_block, block_ids)
        attended = attended.reshape(LENGTH, GROUP, HEAD_DIM)
        log_sums = log_sums.transpose(1, 0, 2).reshape(GROUP, LENGTH)
        return (attended, log_sums)

    def group_backward(operands):
        query_group, key_group, value_group, attended, grad_att, log_sums = operands
        keys_pad = padded(key_group)
        values_pad = padded(value_group)

        def one_block(carry, block):
            grad_keys_pad, grad_values_pad = carry
            start = block * TOK_DEV
            query_block = lax.dynamic_slice_in_dim(query_group, start, TOK_DEV, 0)
            key_block = lax.dynamic_slice_in_dim(keys_pad, start, ext_rows, 0)
            value_block = lax.dynamic_slice_in_dim(values_pad, start, ext_rows, 0)
            att_block = lax.dynamic_slice_in_dim(attended, start, TOK_DEV, 0)
            grad_block = lax.dynamic_slice_in_dim(grad_att, start, TOK_DEV, 0)
            lse_block = lax.dynamic_slice_in_dim(log_sums, start, TOK_DEV, 1)
            allowed = block_mask(start)[None]
            capped = scores_of(query_block, key_block)
            probs = jnp.where(allowed, jnp.exp(capped - lse_block[:, :, None]), 0.0)
            probs_rounded = rounded(probs).astype(jnp.float32)
            grad_float = grad_block.astype(jnp.float32)
            delta = lax.optimization_barrier(jnp.sum(grad_float * att_block.astype(jnp.float32), axis=-1)).T
            grad_probs = jnp.einsum('igd,jd->gij', grad_float, value_block.astype(jnp.float32))
            grad_scores = rounded(probs * (grad_probs - delta[:, :, None]) * (1.0 - (capped / soft_cap) ** 2)).astype(jnp.float32)
            grad_values = jnp.einsum('gij,igd->jd', probs_rounded, grad_float)
            grad_queries = jnp.einsum('gij,jd->igd', grad_scores, key_block.astype(jnp.float32)) * score_scale
            grad_keys = jnp.einsum('gij,igd->jd', grad_scores, query_block.astype(jnp.float32)) * score_scale
            old_keys = lax.dynamic_slice_in_dim(grad_keys_pad, start, ext_rows, 0)
            old_values = lax.dynamic_slice_in_dim(grad_values_pad, start, ext_rows, 0)
            grad_keys_pad = lax.dynamic_update_slice_in_dim(grad_keys_pad, old_keys + grad_keys, start, 0)
            grad_values_pad = lax.dynamic_update_slice_in_dim(grad_values_pad, old_values + grad_values, start, 0)
            return ((grad_keys_pad, grad_values_pad), grad_queries)
        start_pads = (jnp.zeros((pad_rows + LENGTH, HEAD_DIM), jnp.float32), jnp.zeros((pad_rows + LENGTH, HEAD_DIM), jnp.float32))
        (grad_keys_pad, grad_values_pad), grad_queries = lax.scan(one_block, start_pads, block_ids)
        grad_queries = grad_queries.reshape(LENGTH, GROUP, HEAD_DIM)
        return (grad_queries, grad_keys_pad[pad_rows:], grad_values_pad[pad_rows:])

    def one_sequence(totals, operands):
        seq_in, seq_cot = operands
        stream = seq_in.astype(jnp.float32)
        attn_in = rounded(rms_norm(stream, gains_rounded[0]))
        projected = jnp.dot(attn_in, qkv_rounded, preferred_element_type=jnp.float32).reshape(LENGTH, KV_HEADS, GROUP + 2, HEAD_DIM)
        queries = rounded(rotate(projected[:, :, :GROUP].reshape(LENGTH, HEADS, HEAD_DIM), cosine, sine))
        keys = rounded(rotate(projected[:, :, GROUP], cosine, sine))
        values = rounded(projected[:, :, GROUP + 1])
        query_groups = queries.reshape(LENGTH, KV_HEADS, GROUP, HEAD_DIM).transpose(1, 0, 2, 3)
        key_groups = keys.transpose(1, 0, 2)
        value_groups = values.transpose(1, 0, 2)
        attended, log_sums = lax.map(group_forward, (query_groups, key_groups, value_groups))
        att_flat = attended.transpose(1, 0, 2, 3).reshape(LENGTH, HEADS * HEAD_DIM)
        attn_out = jnp.dot(att_flat, out_rounded, preferred_element_type=jnp.float32)
        mid_stream = stream + rms_norm(attn_out, gains_rounded[1])
        ffn_in = rounded(rms_norm(mid_stream, gains_rounded[2]))
        gate_up = jnp.dot(ffn_in, gate_up_rounded, preferred_element_type=jnp.float32).reshape(LENGTH, 2, FF)
        hidden = rounded(geglu(gate_up[:, 0], gate_up[:, 1]))
        ffn_out = jnp.dot(hidden, down_rounded, preferred_element_type=jnp.float32)
        seq_out = (mid_stream + rms_norm(ffn_out, gains_rounded[3])).astype(jnp.bfloat16)
        grad_top = seq_cot.astype(jnp.float32)
        grad_ffn_out, gain_three = norm_back(ffn_out, gains_rounded[3], grad_top)
        grad_ffn = rounded(grad_ffn_out)
        grad_hidden = jnp.dot(grad_ffn, down_rounded.T, preferred_element_type=jnp.float32)
        _, geglu_pull = jax.vjp(geglu, gate_up[:, 0], gate_up[:, 1])
        grad_gate, grad_up = geglu_pull(grad_hidden)
        grad_gate_up = rounded(jnp.stack([grad_gate, grad_up], axis=1).reshape(LENGTH, 2 * FF))
        grad_ffn_in = jnp.dot(grad_gate_up, gate_up_rounded.T, preferred_element_type=jnp.float32)
        grad_mid_norm, gain_two = norm_back(mid_stream, gains_rounded[2], grad_ffn_in)
        grad_mid = grad_top + grad_mid_norm
        grad_attn_out, gain_one = norm_back(attn_out, gains_rounded[1], grad_mid)
        grad_attn = rounded(grad_attn_out)
        grad_att_flat = rounded(jnp.dot(grad_attn, out_rounded.T, preferred_element_type=jnp.float32))
        grad_att_groups = grad_att_flat.reshape(LENGTH, KV_HEADS, GROUP, HEAD_DIM).transpose(1, 0, 2, 3)
        grad_queries, grad_keys, grad_values = lax.map(group_backward, (query_groups, key_groups, value_groups, attended, grad_att_groups, log_sums))
        grad_queries = grad_queries.transpose(1, 0, 2, 3).reshape(LENGTH, HEADS, HEAD_DIM)
        grad_queries = rotate(grad_queries, cosine, -sine).reshape(LENGTH, KV_HEADS, GROUP, HEAD_DIM)
        grad_keys = rotate(grad_keys.transpose(1, 0, 2), cosine, -sine)
        grad_values = grad_values.transpose(1, 0, 2)
        grad_proj = rounded(jnp.concatenate([grad_queries, grad_keys[:, :, None], grad_values[:, :, None]], axis=2).reshape(LENGTH, KV_HEADS * (GROUP + 2) * HEAD_DIM))
        grad_attn_in = jnp.dot(grad_proj, qkv_rounded.T, preferred_element_type=jnp.float32)
        grad_stream_norm, gain_zero = norm_back(stream, gains_rounded[0], grad_attn_in)
        seq_grad = grad_mid + grad_stream_norm
        totals = (totals[0] + jnp.dot(attn_in.T, grad_proj, preferred_element_type=jnp.float32), totals[1] + jnp.dot(att_flat.T, grad_attn, preferred_element_type=jnp.float32), totals[2] + jnp.dot(ffn_in.T, grad_gate_up, preferred_element_type=jnp.float32), totals[3] + jnp.dot(hidden.T, grad_ffn, preferred_element_type=jnp.float32), totals[4] + jnp.stack([gain_zero, gain_one, gain_two, gain_three]))
        return (totals, (seq_out, seq_grad))
    zeros = (jnp.zeros((D, KV_HEADS * (GROUP + 2) * HEAD_DIM), jnp.float32), jnp.zeros((HEADS * HEAD_DIM, D), jnp.float32), jnp.zeros((D, 2 * FF), jnp.float32), jnp.zeros((FF, D), jnp.float32), jnp.zeros((4, D), jnp.float32))
    totals, outputs = lax.scan(one_sequence, zeros, (layer_in, cotangent))
    layer_out, input_grad = outputs
    qkv_grad = totals[0].reshape(D, KV_HEADS, (GROUP + 2) * HEAD_DIM)
    out_grad = totals[1]
    gate_up_grad = totals[2].reshape(D, 2, FF)
    down_grad = totals[3]
    gains_grad = totals[4]
    qkv_new, qkv_first_new, qkv_second_new = adam_step(qkv_weight, qkv_grad, qkv_first, qkv_second, decay_rate)
    out_new, out_first_new, out_second_new = adam_step(out_weight, out_grad, out_first, out_second, decay_rate)
    gate_up_new, gate_up_first_new, gate_up_second_new = adam_step(gate_up_weight, gate_up_grad, gate_up_first, gate_up_second, decay_rate)
    down_new, down_first_new, down_second_new = adam_step(down_weight, down_grad, down_first, down_second, decay_rate)
    gains_new, gains_first_new, gains_second_new = adam_step(norm_gains, gains_grad, gains_first, gains_second, 0.0)
    return (layer_out, input_grad, qkv_grad, out_grad, gate_up_grad, down_grad, gains_grad, qkv_new, out_new, gate_up_new, down_new, gains_new, qkv_first_new, out_first_new, gate_up_first_new, down_first_new, gains_first_new, qkv_second_new, out_second_new, gate_up_second_new, down_second_new, gains_second_new)
```

```python
import jax
import jax.numpy as jnp
from jax import lax
from jax.experimental import pallas as pl
from jax.experimental.pallas import tpu as pltpu
from jax.sharding import PartitionSpec as P

HEAD_DIM = 256
WIN_BLOCKS = 4
STEP = 10
GROUP = 2


norm_eps = 1e-06
soft_cap = 50.0
learn_rate = 0.02
decay_rate = 0.1
beta_first = 0.9
beta_second = 0.95
adam_eps = 1e-08
gelu_coef = 0.7978845608028654


def from_behind(value, axis, steps):
    count = lax.axis_size(axis)
    initial, last = (max(0, -steps), min(count, count - steps))
    return lax.ppermute(value, axis, [(source, source + steps) for source in range(initial, last)])


def rms_norm(values, gain):
    scale = lax.rsqrt(jnp.mean(values * values, axis=-1, keepdims=True) + norm_eps)
    return values * scale * (1.0 + gain)


def norm_back(values, gain, upstream):
    _, pullback = jax.vjp(rms_norm, values, gain)
    return pullback(upstream)


def gelu_tanh(values):
    inner = gelu_coef * (values + 0.044715 * values * values * values)
    return 0.5 * values * (1.0 + jnp.tanh(inner))


def geglu(gate, up_part):
    return gelu_tanh(gate) * up_part


def rope_tables(positions, head_size):
    half = head_size // 2
    exponent = jnp.arange(half, dtype=jnp.float32) * (2.0 / head_size)
    freqs = 10000.0 ** (-exponent)
    angles = positions.astype(jnp.float32)[:, None] * freqs[None, :]
    return (jnp.cos(angles), jnp.sin(angles))


def rotate(values, cosine, sine):
    half = values.shape[-1] // 2
    first = values[..., :half]
    second = values[..., half:]
    cosine = cosine[:, None, :]
    sine = sine[:, None, :]
    return jnp.concatenate(
        [first * cosine - second * sine, second * cosine + first * sine], axis=-1
    )


def adam_step(weight, grad, first, second, decay):
    first_new = beta_first * first + (1.0 - beta_first) * grad
    second_new = beta_second * second + (1.0 - beta_second) * grad * grad
    first_hat = first_new / (1.0 - beta_first**STEP)
    second_hat = second_new / (1.0 - beta_second**STEP)
    weight_new = weight - learn_rate * (
        first_hat / (jnp.sqrt(second_hat) + adam_eps) + decay * weight
    )
    return (weight_new, first_new, second_new)


def rows_product(left, right):
    return lax.dot_general(
        left, right, (((0,), (0,)), ((), ())), preferred_element_type=jnp.float32
    )


def cols_product(left, right):
    return lax.dot_general(
        left, right, (((1,), (1,)), ((), ())), preferred_element_type=jnp.float32
    )


def capped_scores(query_groups, ext_keys):
    raw = jnp.einsum(
        "icgd,jcd->cgij", query_groups, ext_keys, preferred_element_type=jnp.float32
    ) * query_groups.shape[-1] ** (-0.5)
    return soft_cap * jnp.tanh(raw / soft_cap)


def tensor_sum(part):
    return lax.psum(part, "tensor")


def swap(value, axis, bit):
    count = lax.axis_size(axis)
    return lax.ppermute(value, axis, [(source, source ^ bit) for source in range(count)])


def gather_begin(shard):
    half = shard.shape[0] // 2
    low, high = shard[:half], shard[half:]
    return low, high, swap(low, "batch", 1), swap(high, "batch", 2)


def gather_end(state):
    low, high, low_one, high_two = state
    low_far = swap(jnp.stack([low, low_one]), "batch", 2)
    high_far = swap(jnp.stack([high, high_two]), "batch", 1)
    near = jnp.stack(
        [
            jnp.concatenate([low, high]),
            jnp.concatenate([low_one, high_far[0]]),
            jnp.concatenate([low_far[0], high_two]),
            jnp.concatenate([low_far[1], high_far[1]]),
        ]
    )
    return near, swap(near, "seq", 1)


def own_blocks(wide):
    tokens, width = wide.shape
    chip, core = lax.axis_index("batch"), lax.axis_index("seq")
    split = wide.reshape(tokens, 8, width // 8)
    halves = []
    for owner in (core, 1 - core):
        parts = [
            lax.dynamic_index_in_dim(split, (chip ^ k) * 2 + owner, 1, keepdims=False)
            for k in range(4)
        ]
        halves.append(jnp.concatenate(parts, axis=1))
    return halves


def both_cores(wide):
    mine, theirs = own_blocks(wide)
    return jnp.concatenate([mine, swap(theirs, "seq", 1)], axis=0)


def weight_local(wide, narrow):
    local = rows_product(wide, narrow).astype(jnp.bfloat16)
    return local.reshape(4, -1, local.shape[1])


def scatter_begin(local):
    half = local.shape[1] // 2
    state = []
    for part, first, second in ((local[:, :half], 1, 2), (local[:, half:], 2, 1)):
        got = swap(jnp.stack([part[first], part[3]]), "batch", first)
        far = part[second].astype(jnp.float32) + got[1].astype(jnp.float32)
        state.append((part[0], got[0], far.astype(jnp.bfloat16)))
    return state


def scatter_end(state):
    total = []
    for (own, got, far), second in zip(state, (2, 1)):
        got_far = swap(far, "batch", second)
        near = own.astype(jnp.float32) + got.astype(jnp.float32)
        total.append(near + got_far.astype(jnp.float32))
    return jnp.concatenate(total, axis=0)


def everywhere_sum(value):
    for axis, bit in (("seq", 1), ("batch", 1), ("batch", 2), ("tensor", 1), ("tensor", 2)):
        value = value + swap(value, axis, bit)
    return value


def spec_any():
    return pl.BlockSpec(memory_space=pl.ANY)


def spec_vmem():
    return pl.BlockSpec(memory_space=pltpu.VMEM)


def spec_smem():
    return pl.BlockSpec(memory_space=pltpu.SMEM)


def kernel_params():
    return pltpu.CompilerParams(vmem_limit_bytes=56 * 1024 * 1024)


def cost(flops, moved):
    return pl.CostEstimate(flops=flops, bytes_accessed=moved, transcendentals=0)


def shaped(shape, kind):
    return jax.ShapeDtypeStruct(shape, kind)


def dot_nn(left, right):
    return lax.dot_general(
        left, right, (((1,), (0,)), ((), ())), preferred_element_type=jnp.float32
    )


def dot_nt(left, right):
    return lax.dot_general(
        left, right, (((1,), (1,)), ((), ())), preferred_element_type=jnp.float32
    )


def dot_tn(left, right):
    return lax.dot_general(
        left, right, (((0,), (0,)), ((), ())), preferred_element_type=jnp.float32
    )


def row_scale(values):
    return lax.rsqrt(jnp.mean(values * values, axis=-1, keepdims=True) + norm_eps)


def norm_pull(values, scale, gain, upstream):
    normed = values * scale
    inner = upstream * (1.0 + gain)
    pulled = scale * (inner - normed * jnp.mean(normed * inner, axis=-1, keepdims=True))
    return pulled, upstream * normed


def fetch_rows(place, near, far, target, sems, column, columns):
    chip, core = place[0], place[1]
    rows = near.shape[1]
    copies = []
    for k in range(4):
        for which, source in enumerate((near, far)):
            row = ((k ^ chip) * 2 + (which ^ core)) * rows
            copies.append(
                pltpu.make_async_copy(
                    source.at[k, :, pl.ds(column, columns)],
                    target.at[pl.ds(pl.multiple_of(row, 16), rows), :],
                    sems.at[k * 2 + which],
                )
            )
    for copy in copies:
        copy.start()
    return copies


def rope(values, cosine, sine):
    half = HEAD_DIM // 2
    first, second = values[:, :half], values[:, half:]
    return jnp.concatenate(
        [first * cosine - second * sine, second * cosine + first * sine], axis=1
    )


def arrange_kernel(place, near, far, result, sems):
    for copy in fetch_rows(place, near, far, result, sems, 0, result.shape[1]):
        copy.wait()


def arrange(place, near, far):
    return pl.pallas_call(
        arrange_kernel,
        in_specs=[spec_smem(), spec_any(), spec_any()],
        out_specs=spec_vmem(),
        out_shape=shaped((8 * near.shape[1], near.shape[2]), jnp.bfloat16),
        scratch_shapes=[pltpu.SemaphoreType.DMA((8,))],
        compiler_params=kernel_params(),
        cost_estimate=cost(0, 4 * near.size * 4),
        name="arrange",
    )(place, near, far)


def project_kernel(place, x, near, far, cosine, sine, *rest):
    queries, pair, attn_in, gains, weight, sems = rest[-6:]
    copies = fetch_rows(place, near, far, weight, sems, 0, weight.shape[1])
    for copy in copies:
        copy.wait()
    width = (GROUP + 2) * HEAD_DIM
    tail = weight[:, width + GROUP * HEAD_DIM :].astype(jnp.float32)
    gains[...] = jnp.transpose(tail)[:8]
    gain = 1.0 + gains[0:1, :]
    chunk = 16

    @pl.loop(0, x.shape[0] // chunk, unroll=2)
    def _(step):
        rows = pl.ds(pl.multiple_of(step * chunk, chunk), chunk)
        stream = x[rows, :].astype(jnp.float32)
        attn_in[rows, :] = (stream * row_scale(stream) * gain).astype(jnp.bfloat16)

    for member in range(GROUP + 2):
        columns = slice(member * HEAD_DIM, (member + 1) * HEAD_DIM)
        part = dot_nn(attn_in[...], weight[:, columns])
        if member < GROUP:
            queries[:, columns] = rope(part, cosine[...], sine[...]).astype(jnp.bfloat16)
        elif member == GROUP:
            pair[0] = rope(part, cosine[...], sine[...]).astype(jnp.bfloat16)
        else:
            pair[1] = part.astype(jnp.bfloat16)


def project(place, x, near, far, cosine, sine, *earlier):
    tokens, width = x.shape
    bf16 = jnp.bfloat16
    return pl.pallas_call(
        project_kernel,
        in_specs=[spec_smem(), spec_vmem(), spec_any(), spec_any(), spec_vmem(), spec_vmem()]
        + [spec_any()] * len(earlier),
        out_specs=[spec_vmem()] * 4,
        out_shape=[
            shaped((tokens, GROUP * HEAD_DIM), bf16),
            shaped((2, tokens, HEAD_DIM), bf16),
            shaped((tokens, width), bf16),
            shaped((8, width), jnp.float32),
        ],
        scratch_shapes=[pltpu.VMEM((width, near.shape[2]), bf16), pltpu.SemaphoreType.DMA((8,))],
        compiler_params=kernel_params(),
        cost_estimate=cost(2 * tokens * width * 1024, 12_000_000),
        name="project",
    )(place, x, near, far, cosine, sine, *earlier)


def chunk_scores(query, key, behind, row, core):
    raw = dot_nt(query, key) * (HEAD_DIM**-0.5 / soft_cap)
    bent = jnp.tanh(raw)
    powers = jnp.exp(soft_cap * bent)
    if behind:
        powers = jnp.where(core > 0, powers, 0.0)
    else:
        at = row + lax.broadcasted_iota(jnp.int32, powers.shape, 0)
        powers = jnp.where(at >= lax.broadcasted_iota(jnp.int32, powers.shape, 1), powers, 0.0)
    return bent, powers


def attend_kernel(place, queries, pair, behind, near, far, attended, result, weight, sems):
    width = (GROUP + 2) * HEAD_DIM
    copies = fetch_rows(place, near, far, weight, sems, width, GROUP * HEAD_DIM)
    core = place[1]
    chunk = 128
    tokens = queries.shape[0]
    for start in range(0, tokens, chunk):
        rows = slice(start, start + chunk)
        keys = start + chunk
        for head in range(GROUP):
            columns = slice(head * HEAD_DIM, (head + 1) * HEAD_DIM)
            query = queries[rows, columns]
            _, old = chunk_scores(query, behind[0], True, start, core)
            _, new = chunk_scores(query, pair[0, :keys], False, start, core)
            total = jnp.sum(old, axis=-1, keepdims=True) + jnp.sum(new, axis=-1, keepdims=True)
            share = 1.0 / total
            value = dot_nn((old * share).astype(jnp.bfloat16), behind[1])
            value += dot_nn((new * share).astype(jnp.bfloat16), pair[1, :keys])
            attended[rows, columns] = value.astype(jnp.bfloat16)
    for copy in copies:
        copy.wait()
    tile = 768
    for column in range(0, result.shape[1], tile):
        part = dot_nt(attended[...], weight[column : column + tile, :])
        result[:, column : column + tile] = part.astype(jnp.bfloat16)


def attend(place, queries, pair, behind, near, far, width):
    tokens = queries.shape[0]
    bf16 = jnp.bfloat16
    return pl.pallas_call(
        attend_kernel,
        in_specs=[spec_smem(), spec_vmem(), spec_vmem(), spec_vmem(), spec_any(), spec_any()],
        out_specs=[spec_vmem()] * 2,
        out_shape=[shaped((tokens, GROUP * HEAD_DIM), bf16), shaped((tokens, width), bf16)],
        scratch_shapes=[
            pltpu.VMEM((width, GROUP * HEAD_DIM), bf16),
            pltpu.SemaphoreType.DMA((8,)),
        ],
        compiler_params=kernel_params(),
        cost_estimate=cost(4 * tokens * width * 1024, 8_000_000),
        name="attend",
    )(place, queries, pair, behind, near, far)


def widen_kernel(attn_out, x, gains, ffn, *rest):
    ffn_in, hidden, by_gate, by_up = rest[-4:]
    chunk = 16

    @pl.when(pl.program_id(0) == 0)
    def _():
        @pl.loop(0, x.shape[0] // chunk, unroll=2)
        def _(step):
            rows = pl.ds(pl.multiple_of(step * chunk, chunk), chunk)
            out = attn_out[rows, :].astype(jnp.float32)
            mid = x[rows, :].astype(jnp.float32) + out * row_scale(out) * (1.0 + gains[1:2, :])
            ffn_in[rows, :] = (mid * row_scale(mid) * (1.0 + gains[2:3, :])).astype(jnp.bfloat16)

    value = ffn_in[...]
    gate = dot_nn(value, ffn[0])
    up = dot_nn(value, ffn[1])
    square_of = gate * gate
    bent = jnp.tanh(gate * (gelu_coef + gelu_coef * 0.044715 * square_of))
    half = 0.5 + 0.5 * bent
    curve = gate * half
    slope = half + curve * (1.0 - bent) * (gelu_coef + 3.0 * gelu_coef * 0.044715 * square_of)
    hidden[...] = (curve * up).astype(jnp.bfloat16)
    by_gate[...] = (slope * up).astype(jnp.bfloat16)
    by_up[...] = curve.astype(jnp.bfloat16)


def whole(shape):
    return pl.BlockSpec(shape, lambda *_: (0,) * len(shape))


def widen(attn_out, x, gains, ffn, *earlier):
    tokens, width = x.shape
    units = ffn.shape[2]
    tile = 256
    bf16 = jnp.bfloat16
    columns = pl.BlockSpec((tokens, tile), lambda i: (0, i))
    return pl.pallas_call(
        widen_kernel,
        grid=(units // tile,),
        in_specs=[
            whole((tokens, width)),
            whole((tokens, width)),
            whole((8, width)),
            pl.BlockSpec((2, width, tile), lambda i: (0, 0, i)),
        ]
        + [spec_any()] * len(earlier),
        out_specs=[whole((tokens, width)), columns, columns, columns],
        out_shape=[shaped((tokens, width), bf16)] + [shaped((tokens, units), bf16)] * 3,
        compiler_params=kernel_params(),
        cost_estimate=cost(4 * tokens * width * units, 36_000_000),
        name="widen",
    )(attn_out, x, gains, ffn, *earlier)


def narrow_kernel(hidden, down, result):
    result[...] = dot_nt(hidden[...], down[...]).astype(jnp.bfloat16)


def narrow(hidden, down):
    tokens, units = hidden.shape
    width = down.shape[0]
    tile = 256
    return pl.pallas_call(
        narrow_kernel,
        grid=(width // tile,),
        in_specs=[whole((tokens, units)), pl.BlockSpec((tile, units), lambda i: (i, 0))],
        out_specs=pl.BlockSpec((tokens, tile), lambda i: (0, i)),
        out_shape=shaped((tokens, width), jnp.bfloat16),
        compiler_params=kernel_params(),
        cost_estimate=cost(2 * tokens * width * units, 16_000_000),
        name="narrow",
    )(hidden, down)


def top_back_kernel(ffn_out, top, gains, grad_ffn, gain_out):
    chunk = 16
    gain_out[...] = jnp.zeros_like(gain_out)

    @pl.loop(0, ffn_out.shape[0] // chunk, unroll=2)
    def _(step):
        rows = pl.ds(pl.multiple_of(step * chunk, chunk), chunk)
        out = ffn_out[rows, :].astype(jnp.float32)
        upstream = top[rows, :].astype(jnp.float32)
        pulled, product = norm_pull(out, row_scale(out), gains[3:4, :], upstream)
        grad_ffn[rows, :] = pulled.astype(jnp.bfloat16)
        gain_out[...] += product[:8] + product[8:]


def top_back(ffn_out, top, gains):
    tokens, width = top.shape
    return pl.pallas_call(
        top_back_kernel,
        in_specs=[spec_vmem()] * 3,
        out_specs=[spec_vmem()] * 2,
        out_shape=[shaped((tokens, width), jnp.bfloat16), shaped((8, width), jnp.float32)],
        compiler_params=kernel_params(),
        cost_estimate=cost(20 * tokens * width, 8_000_000),
        name="top_back",
    )(ffn_out, top, gains)


def ffn_back_kernel(grad_ffn, down, gate_up, by_gate, by_up, *rest):
    grad_gate, grad_up, result, total = rest[-4:]

    @pl.when(pl.program_id(0) == 0)
    def _():
        total[...] = jnp.zeros_like(total)

    grad_hidden = dot_nn(grad_ffn[...], down[...])
    one = (grad_hidden * by_gate[...].astype(jnp.float32)).astype(jnp.bfloat16)
    two = (grad_hidden * by_up[...].astype(jnp.float32)).astype(jnp.bfloat16)
    grad_gate[...] = one
    grad_up[...] = two
    total[...] += dot_nt(one, gate_up[0]) + dot_nt(two, gate_up[1])

    @pl.when(pl.program_id(0) == pl.num_programs(0) - 1)
    def _():
        result[...] = total[...].astype(jnp.bfloat16)


def ffn_back(grad_ffn, down, gate_up, by_gate, by_up, *earlier):
    tokens, width = grad_ffn.shape
    units = by_up.shape[1]
    tile = 256
    bf16 = jnp.bfloat16
    columns = pl.BlockSpec((tokens, tile), lambda i: (0, i))
    return pl.pallas_call(
        ffn_back_kernel,
        grid=(units // tile,),
        in_specs=[
            whole((tokens, width)),
            pl.BlockSpec((width, tile), lambda i: (0, i)),
            pl.BlockSpec((2, width, tile), lambda i: (0, 0, i)),
            columns,
            columns,
        ]
        + [spec_any()] * len(earlier),
        out_specs=[columns, columns, whole((tokens, width))],
        out_shape=[
            shaped((tokens, units), bf16),
            shaped((tokens, units), bf16),
            shaped((tokens, width), bf16),
        ],
        scratch_shapes=[pltpu.VMEM((tokens, width), jnp.float32)],
        compiler_params=kernel_params(),
        cost_estimate=cost(6 * tokens * width * units, 52_000_000),
        name="ffn_back",
    )(grad_ffn, down, gate_up, by_gate, by_up, *earlier)


def mid_back_kernel(place, grad_in, x, attn_out, top, gains, near, far, *rest):
    grad_mid, grad_attn, grad_att, gain_out, weight, sems = rest[-6:]
    width = (GROUP + 2) * HEAD_DIM
    copies = fetch_rows(place, near, far, weight, sems, width, GROUP * HEAD_DIM)
    gain_out[...] = jnp.zeros_like(gain_out)
    chunk = 16
    tokens = x.shape[0]

    @pl.loop(0, tokens // chunk, unroll=2)
    def _(step):
        rows = pl.ds(pl.multiple_of(step * chunk, chunk), chunk)
        out = attn_out[rows, :].astype(jnp.float32)
        out_scale = row_scale(out)
        mid = x[rows, :].astype(jnp.float32) + out * out_scale * (1.0 + gains[1:2, :])
        upstream = grad_in[rows, :].astype(jnp.float32)
        pulled, product = norm_pull(mid, row_scale(mid), gains[2:3, :], upstream)
        gain_out[1] += product[:8] + product[8:]
        at_mid = top[rows, :].astype(jnp.float32) + pulled
        grad_mid[rows, :] = at_mid
        pulled, product = norm_pull(out, out_scale, gains[1:2, :], at_mid)
        gain_out[0] += product[:8] + product[8:]
        grad_attn[rows, :] = pulled.astype(jnp.bfloat16)

    for copy in copies:
        copy.wait()
    grad_att[...] = dot_nn(grad_attn[...], weight[...]).astype(jnp.bfloat16)


def mid_back(place, grad_in, x, attn_out, top, gains, near, far, *earlier):
    tokens, width = x.shape
    heads = GROUP * HEAD_DIM
    bf16 = jnp.bfloat16
    return pl.pallas_call(
        mid_back_kernel,
        in_specs=[spec_smem()]
        + [spec_vmem()] * 5
        + [spec_any()] * 2
        + [spec_any()] * len(earlier),
        out_specs=[spec_vmem()] * 4,
        out_shape=[
            shaped((tokens, width), jnp.float32),
            shaped((tokens, width), bf16),
            shaped((tokens, heads), bf16),
            shaped((2, 8, width), jnp.float32),
        ],
        scratch_shapes=[pltpu.VMEM((width, heads), bf16), pltpu.SemaphoreType.DMA((8,))],
        compiler_params=kernel_params(),
        cost_estimate=cost(2 * tokens * width * heads, 24_000_000),
        name="mid_back",
    )(place, grad_in, x, attn_out, top, gains, near, far, *earlier)


def attend_back_kernel(
    place, queries, pair, behind, attended, grad_att, cosine, sine, grad_q, grad_own, grad_old, sums
):
    core = place[1]
    chunk = 128
    tokens = queries.shape[0]
    scale = HEAD_DIM**-0.5
    sums[...] = jnp.zeros_like(sums)
    for start in range(0, tokens, chunk):
        rows = slice(start, start + chunk)
        keys = start + chunk
        cos, sin = cosine[rows, :], sine[rows, :]
        for head in range(GROUP):
            columns = slice(head * HEAD_DIM, (head + 1) * HEAD_DIM)
            query, upstream = queries[rows, columns], grad_att[rows, columns]
            delta = jnp.sum(
                upstream.astype(jnp.float32) * attended[rows, columns].astype(jnp.float32),
                axis=-1,
                keepdims=True,
            )
            bent_old, old = chunk_scores(query, behind[0], True, start, core)
            bent_new, new = chunk_scores(query, pair[0, :keys], False, start, core)
            share = 1.0 / (
                jnp.sum(old, axis=-1, keepdims=True) + jnp.sum(new, axis=-1, keepdims=True)
            )
            total = jnp.zeros((chunk, HEAD_DIM), jnp.float32)
            for bent, powers, block, end, base in (
                (bent_old, old, behind, tokens, 0),
                (bent_new, new, pair, keys, 2),
            ):
                prob = powers * share
                grad_p = dot_nt(upstream, block[1, :end])
                grad_s = (prob * (grad_p - delta) * (1.0 - bent * bent)).astype(jnp.bfloat16)
                total += dot_nn(grad_s, block[0, :end])
                sums[base, :end, :] += dot_tn(grad_s, query)
                sums[base + 1, :end, :] += dot_tn(prob.astype(jnp.bfloat16), upstream)
            grad_q[rows, columns] = rope(total * scale, cos, -sin).astype(jnp.bfloat16)
    grad_old[0] = (sums[0] * scale).astype(jnp.bfloat16)
    grad_old[1] = sums[1].astype(jnp.bfloat16)
    grad_own[0] = sums[2] * scale
    grad_own[1] = sums[3]


def attend_back(place, queries, pair, behind, attended, grad_att, cosine, sine):
    tokens, heads = queries.shape
    bf16 = jnp.bfloat16
    return pl.pallas_call(
        attend_back_kernel,
        in_specs=[spec_smem()] + [spec_vmem()] * 7,
        out_specs=[spec_vmem()] * 3,
        out_shape=[
            shaped((tokens, heads), bf16),
            shaped((2, tokens, HEAD_DIM), jnp.float32),
            shaped((2, tokens, HEAD_DIM), bf16),
        ],
        scratch_shapes=[pltpu.VMEM((4, tokens, HEAD_DIM), jnp.float32)],
        compiler_params=kernel_params(),
        cost_estimate=cost(20 * tokens * 1024 * heads, 5_000_000),
        name="attend_back",
    )(place, queries, pair, behind, attended, grad_att, cosine, sine)


def project_back_kernel(
    place, grad_q, grad_own, grad_ahead, cosine, sine, x, near, far, *rest
):
    proj, result, gain_out, weight, sems = rest[-5:]
    width = (GROUP + 2) * HEAD_DIM
    copies = fetch_rows(place, near, far, weight, sems, 0, width)
    heads = GROUP * HEAD_DIM
    proj[:, :heads] = grad_q[...]
    grad_key = grad_own[0] + grad_ahead[0].astype(jnp.float32)
    proj[:, heads : heads + HEAD_DIM] = rope(grad_key, cosine[...], -sine[...]).astype(jnp.bfloat16)
    proj[:, heads + HEAD_DIM :] = (grad_own[1] + grad_ahead[1].astype(jnp.float32)).astype(
        jnp.bfloat16
    )
    gain_out[...] = jnp.zeros_like(gain_out)
    for copy in copies:
        copy.wait()
    tile = 768
    for column in range(0, result.shape[1], tile):
        part = dot_nt(proj[...], weight[column : column + tile, :])
        result[:, column : column + tile] = part.astype(jnp.bfloat16)
    chunk = 16

    @pl.loop(0, x.shape[0] // chunk, unroll=2)
    def _(step):
        rows = pl.ds(pl.multiple_of(step * chunk, chunk), chunk)
        stream = x[rows, :].astype(jnp.float32)
        product = result[rows, :].astype(jnp.float32) * (stream * row_scale(stream))
        gain_out[...] += product[:8] + product[8:]


def project_back(place, grad_q, grad_own, grad_ahead, cosine, sine, x, near, far, *earlier):
    tokens, width = x.shape
    proj_width = (GROUP + 2) * HEAD_DIM
    bf16 = jnp.bfloat16
    return pl.pallas_call(
        project_back_kernel,
        in_specs=[spec_smem()]
        + [spec_vmem()] * 6
        + [spec_any()] * 2
        + [spec_any()] * len(earlier),
        out_specs=[spec_vmem()] * 3,
        out_shape=[
            shaped((tokens, proj_width), bf16),
            shaped((tokens, width), bf16),
            shaped((8, width), jnp.float32),
        ],
        scratch_shapes=[pltpu.VMEM((width, proj_width), bf16), pltpu.SemaphoreType.DMA((8,))],
        compiler_params=kernel_params(),
        cost_estimate=cost(2 * tokens * width * proj_width, 14_000_000),
        name="project_back",
    )(place, grad_q, grad_own, grad_ahead, cosine, sine, x, near, far, *earlier)


def stream_back_kernel(grad_in, x, gains, grad_mid, *rest):
    result = rest[-1]
    stream = x[...].astype(jnp.float32)
    pulled, _ = norm_pull(
        stream, row_scale(stream), gains[0:1, :], grad_in[...].astype(jnp.float32)
    )
    result[...] = grad_mid[...] + pulled


def stream_back(grad_in, x, gains, grad_mid, *earlier):
    tokens, width = x.shape
    tile = 64
    rows = pl.BlockSpec((tile, width), lambda i: (i, 0))
    return pl.pallas_call(
        stream_back_kernel,
        grid=(tokens // tile,),
        in_specs=[rows, rows, whole((8, width)), rows] + [spec_any()] * len(earlier),
        out_specs=rows,
        out_shape=shaped((tokens, width), jnp.float32),
        compiler_params=kernel_params(),
        cost_estimate=cost(20 * tokens * width, 14_000_000),
        name="stream_back",
    )(grad_in, x, gains, grad_mid, *earlier)


def on_square(
    layer_in,
    cotangent,
    qkv_weight,
    out_weight,
    gate_up_weight,
    down_weight,
    norm_gains,
    qkv_first,
    out_first,
    gate_up_first,
    down_first,
    gains_first,
    qkv_second,
    out_second,
    gate_up_second,
    down_second,
    gains_second,
):
    tok_rows = layer_in.shape[1]
    chip, core = lax.axis_index("batch"), lax.axis_index("seq")
    place = jnp.stack([chip, core]).astype(jnp.int32)
    plane = ("batch", "seq")
    stream, top = layer_in[0], cotangent[0]
    gains_cast = jnp.pad(norm_gains.T, ((0, 0), (0, 128 - norm_gains.shape[0])))
    attn_cast = jnp.concatenate([qkv_weight[:, 0], out_weight.T, gains_cast], axis=1)
    gate_up_cast = gate_up_weight.astype(jnp.bfloat16).transpose(1, 0, 2)
    down_cast = down_weight.T.astype(jnp.bfloat16)
    state, down_cast, gate_up_cast = lax.optimization_barrier(
        (gather_begin(attn_cast.astype(jnp.bfloat16)), down_cast, gate_up_cast)
    )
    near, far = gather_end(state)
    down_state = gather_begin(down_cast)
    near, far, down_state = lax.optimization_barrier((near, far, down_state))
    down = arrange(place, *gather_end(down_state))
    gate_up = lax.all_gather(gate_up_cast, plane, axis=1, tiled=True)
    positions = core * tok_rows + jnp.arange(tok_rows, dtype=jnp.int32)
    cosine, sine = rope_tables(positions, HEAD_DIM)

    queries, pair, attn_in, gains = project(
        place, stream, near, far, cosine, sine, gate_up_cast
    )
    behind = from_behind(pair, "seq", 1)
    attended, attn_part = attend(place, queries, pair, behind, near, far, stream.shape[1])
    attn_out = tensor_sum(attn_part)
    ffn_in, hidden, by_gate, by_up = widen(attn_out, stream, gains, gate_up)
    ffn_out = tensor_sum(narrow(hidden, down))

    grad_ffn, gain_ffn = top_back(ffn_out, top, gains)
    grad_gate, grad_up, grad_ffn_part = ffn_back(grad_ffn, down, gate_up, by_gate, by_up)
    grad_ffn_in = tensor_sum(grad_ffn_part)
    ffn_in_both = both_cores(ffn_in)
    hidden_both = jnp.concatenate([hidden, swap(hidden, "seq", 1)], axis=0)
    grad_gate_both = jnp.concatenate([grad_gate, swap(grad_gate, "seq", 1)], axis=0)
    grad_up_both = jnp.concatenate([grad_up, swap(grad_up, "seq", 1)], axis=0)
    down_grad = scatter_end(scatter_begin(weight_local(both_cores(grad_ffn), hidden_both)))
    gate_state = scatter_begin(weight_local(ffn_in_both, grad_gate_both))
    up_local = weight_local(ffn_in_both, grad_up_both)

    grad_mid, grad_attn, grad_att, gain_mid = mid_back(
        place, grad_ffn_in, stream, attn_out, top, gains, near, far, down_grad, gate_state[0][2],
        gate_state[1][2], up_local
    )
    gate_grad = scatter_end(gate_state)
    up_state = scatter_begin(up_local)
    grad_q, grad_own, grad_old = attend_back(
        place, queries, pair, behind, attended, grad_att, cosine, sine
    )
    grad_ahead = from_behind(grad_old, "seq", -1)
    grad_proj, grad_attn_part, gain_attn = project_back(
        place, grad_q, grad_own, grad_ahead, cosine, sine, stream, near, far, gate_grad,
        up_state[0][2], up_state[1][2]
    )
    grad_attn_in = tensor_sum(grad_attn_part)
    up_grad = scatter_end(up_state)
    gate_up_grad = jnp.stack([gate_grad, up_grad], axis=1)

    att_both = jnp.concatenate([attended, swap(attended, "seq", 1)], axis=0)
    out_grad = scatter_end(scatter_begin(weight_local(both_cores(grad_attn), att_both)))
    proj_both = jnp.concatenate([grad_proj, swap(grad_proj, "seq", 1)], axis=0)
    qkv_grad = scatter_end(scatter_begin(weight_local(both_cores(attn_in), proj_both)))[:, None]
    gains_rest = jnp.concatenate([gain_mid, gain_ffn[None]], axis=0).sum(axis=1)
    gains_rest = jnp.where(lax.axis_index("tensor") == 0, gains_rest, 0.0)
    gains_total = everywhere_sum(jnp.concatenate([gain_attn.sum(axis=0)[None], gains_rest], axis=0))
    own_columns = norm_gains.shape[1]
    gains_grad = lax.dynamic_slice_in_dim(
        gains_total, (chip * 2 + core) * own_columns, own_columns, axis=1
    )
    attn_float = attn_out.astype(jnp.float32)
    mid_stream = stream.astype(jnp.float32) + rms_norm(attn_float, gains[1])
    layer_out = (mid_stream + rms_norm(ffn_out.astype(jnp.float32), gains[3])).astype(jnp.bfloat16)
    qkv_new, qkv_first_new, qkv_second_new = adam_step(
        qkv_weight, qkv_grad, qkv_first, qkv_second, decay_rate
    )
    out_new, out_first_new, out_second_new = adam_step(
        out_weight.T, out_grad, out_first.T, out_second.T, decay_rate
    )
    gate_up_new, gate_up_first_new, gate_up_second_new = adam_step(
        gate_up_weight, gate_up_grad, gate_up_first, gate_up_second, decay_rate
    )
    down_new, down_first_new, down_second_new = adam_step(
        down_weight.T, down_grad, down_first.T, down_second.T, decay_rate
    )
    gains_new, gains_first_new, gains_second_new = adam_step(
        norm_gains, gains_grad, gains_first, gains_second, 0.0
    )
    input_grad = stream_back(
        grad_attn_in, stream, gains, grad_mid, qkv_new, out_new, gate_up_new, down_new, gains_new
    )
    return (
        layer_out[None],
        input_grad[None],
        qkv_grad,
        out_grad.T,
        gate_up_grad,
        down_grad.T,
        gains_grad,
        qkv_new,
        out_new.T,
        gate_up_new,
        down_new.T,
        gains_new,
        qkv_first_new,
        out_first_new.T,
        gate_up_first_new,
        down_first_new.T,
        gains_first_new,
        qkv_second_new,
        out_second_new.T,
        gate_up_second_new,
        down_second_new.T,
        gains_second_new,
    )


def on_device(
    layer_in,
    cotangent,
    qkv_weight,
    out_weight,
    gate_up_weight,
    down_weight,
    norm_gains,
    qkv_first,
    out_first,
    gate_up_first,
    down_first,
    gains_first,
    qkv_second,
    out_second,
    gate_up_second,
    down_second,
    gains_second,
):
    tok_rows = layer_in.shape[1]
    seq_index = lax.axis_index("seq")
    collected = (
        lax.all_gather(qkv_weight.astype(jnp.bfloat16), ("batch", "seq"), axis=0, tiled=True),
        lax.all_gather(out_weight.astype(jnp.bfloat16), ("batch", "seq"), axis=1, tiled=True),
        lax.all_gather(gate_up_weight.astype(jnp.bfloat16), ("batch", "seq"), axis=0, tiled=True),
        lax.all_gather(down_weight.astype(jnp.bfloat16), ("batch", "seq"), axis=1, tiled=True),
        lax.all_gather(norm_gains.astype(jnp.bfloat16), ("batch", "seq"), axis=1, tiled=True),
    )
    qkv_full, out_full, gate_up_full, down_full, gains_full = collected
    model_width = qkv_full.shape[0]
    kv_local = qkv_full.shape[1]
    heads_local = kv_local * GROUP
    ffn_local = gate_up_full.shape[2]
    qkv_flat = qkv_full.reshape(model_width, kv_local * (GROUP + 2) * HEAD_DIM)
    gate_up_flat = gate_up_full.reshape(model_width, 2 * ffn_local)
    gains_float = gains_full.astype(jnp.float32)
    positions = seq_index * tok_rows + jnp.arange(tok_rows, dtype=jnp.int32)
    cosine, sine = rope_tables(positions, HEAD_DIM)
    key_positions = (seq_index - WIN_BLOCKS) * tok_rows + jnp.arange(
        (WIN_BLOCKS + 1) * tok_rows, dtype=jnp.int32
    )
    spread = positions[:, None] - key_positions[None, :]
    allowed = (spread >= 0) & (spread < WIN_BLOCKS * tok_rows) & (key_positions >= 0)[None, :]
    mask = allowed[None, None]
    stream = layer_in[0].astype(jnp.float32)
    attn_in = rms_norm(stream, gains_float[0]).astype(jnp.bfloat16)
    projected = jnp.dot(attn_in, qkv_flat, preferred_element_type=jnp.float32).reshape(
        tok_rows, kv_local, GROUP + 2, HEAD_DIM
    )
    queries = rotate(
        projected[:, :, :GROUP].reshape(tok_rows, heads_local, HEAD_DIM), cosine, sine
    ).astype(jnp.bfloat16)
    keys = rotate(projected[:, :, GROUP], cosine, sine).astype(jnp.bfloat16)
    values = projected[:, :, GROUP + 1].astype(jnp.bfloat16)
    kv_pair = jnp.stack([keys, values], axis=0)
    reach = min(WIN_BLOCKS, lax.axis_size("seq") - 1)
    pieces = []
    for distance in range(WIN_BLOCKS, 0, -1):
        if distance <= reach:
            pieces.append(from_behind(kv_pair, "seq", distance))
        else:
            pieces.append(jnp.zeros_like(kv_pair))
    pieces.append(kv_pair)
    extended = jnp.concatenate(pieces, axis=1)
    ext_keys = extended[0]
    ext_values = extended[1]
    query_groups = queries.reshape(tok_rows, kv_local, GROUP, HEAD_DIM)
    capped = capped_scores(query_groups, ext_keys)
    log_sums = jnp.log(jnp.sum(jnp.where(mask, jnp.exp(capped), 0.0), axis=-1))
    probs = jnp.where(mask, jnp.exp(capped - log_sums[..., None]), 0.0).astype(jnp.bfloat16)
    attended = jnp.einsum(
        "cgij,jcd->icgd", probs, ext_values, preferred_element_type=jnp.float32
    ).astype(jnp.bfloat16)
    att_flat = attended.reshape(tok_rows, heads_local * HEAD_DIM)
    attn_out = lax.psum(jnp.dot(att_flat, out_full, preferred_element_type=jnp.float32), "tensor")
    mid_stream = stream + rms_norm(attn_out, gains_float[1])
    ffn_in = rms_norm(mid_stream, gains_float[2]).astype(jnp.bfloat16)
    gate_up = jnp.dot(ffn_in, gate_up_flat, preferred_element_type=jnp.float32).reshape(
        tok_rows, 2, ffn_local
    )
    hidden = geglu(gate_up[:, 0], gate_up[:, 1]).astype(jnp.bfloat16)
    ffn_out = lax.psum(jnp.dot(hidden, down_full, preferred_element_type=jnp.float32), "tensor")
    layer_out = (mid_stream + rms_norm(ffn_out, gains_float[3])).astype(jnp.bfloat16)
    grad_top = cotangent[0].astype(jnp.float32)
    grad_ffn_out, gain_three = norm_back(ffn_out, gains_float[3], grad_top)
    grad_ffn = grad_ffn_out.astype(jnp.bfloat16)
    grad_hidden = cols_product(grad_ffn, down_full)
    _, geglu_pull = jax.vjp(geglu, gate_up[:, 0], gate_up[:, 1])
    grad_gate, grad_up = geglu_pull(grad_hidden)
    grad_gate_up = (
        jnp.stack([grad_gate, grad_up], axis=1)
        .reshape(tok_rows, 2 * ffn_local)
        .astype(jnp.bfloat16)
    )
    grad_ffn_in = lax.psum(cols_product(grad_gate_up, gate_up_flat), "tensor")
    grad_mid_norm, gain_two = norm_back(mid_stream, gains_float[2], grad_ffn_in)
    grad_mid = grad_top + grad_mid_norm
    grad_attn_out, gain_one = norm_back(attn_out, gains_float[1], grad_mid)
    grad_attn = grad_attn_out.astype(jnp.bfloat16)
    grad_att = (
        cols_product(grad_attn, out_full)
        .astype(jnp.bfloat16)
        .reshape(tok_rows, kv_local, GROUP, HEAD_DIM)
    )
    capped_again = capped_scores(query_groups, ext_keys)
    probs_float = jnp.where(mask, jnp.exp(capped_again - log_sums[..., None]), 0.0)
    probs_again = probs_float.astype(jnp.bfloat16)
    delta = jnp.einsum("icgd,icgd->cgi", grad_att, attended, preferred_element_type=jnp.float32)
    grad_probs = jnp.einsum(
        "icgd,jcd->cgij", grad_att, ext_values, preferred_element_type=jnp.float32
    )
    grad_scores = (
        probs_float * (grad_probs - delta[..., None]) * (1.0 - (capped_again / soft_cap) ** 2)
    ).astype(jnp.bfloat16)
    score_scale = HEAD_DIM ** (-0.5)
    grad_values_ext = jnp.einsum(
        "cgij,icgd->jcd", probs_again, grad_att, preferred_element_type=jnp.float32
    )
    grad_keys_ext = (
        jnp.einsum("cgij,icgd->jcd", grad_scores, query_groups, preferred_element_type=jnp.float32)
        * score_scale
    )
    grad_queries = (
        jnp.einsum("cgij,jcd->icgd", grad_scores, ext_keys, preferred_element_type=jnp.float32)
        * score_scale
    )
    grad_pair_ext = jnp.stack([grad_keys_ext, grad_values_ext], axis=0)
    grad_pair = grad_pair_ext[:, WIN_BLOCKS * tok_rows :]
    for distance in range(1, reach + 1):
        start = (WIN_BLOCKS - distance) * tok_rows
        piece = grad_pair_ext[:, start : start + tok_rows]
        grad_pair = grad_pair + from_behind(piece.astype(jnp.bfloat16), "seq", -distance).astype(
            piece.dtype
        )
    grad_queries = rotate(
        grad_queries.reshape(tok_rows, heads_local, HEAD_DIM), cosine, -sine
    ).reshape(tok_rows, kv_local, GROUP, HEAD_DIM)
    grad_keys = rotate(grad_pair[0], cosine, -sine)
    grad_values = grad_pair[1]
    grad_proj = (
        jnp.concatenate([grad_queries, grad_keys[:, :, None], grad_values[:, :, None]], axis=2)
        .reshape(tok_rows, kv_local * (GROUP + 2) * HEAD_DIM)
        .astype(jnp.bfloat16)
    )
    grad_attn_in = lax.psum(
        cols_product(grad_proj, qkv_flat).astype(jnp.bfloat16), "tensor"
    ).astype(jnp.float32)
    grad_stream_norm, gain_zero = norm_back(stream, gains_float[0], grad_attn_in)
    input_grad = grad_mid + grad_stream_norm
    qkv_local = rows_product(attn_in, grad_proj).reshape(
        model_width, kv_local, (GROUP + 2) * HEAD_DIM
    )
    out_local = rows_product(att_flat, grad_attn)
    gate_up_local = rows_product(ffn_in, grad_gate_up).reshape(model_width, 2, ffn_local)
    down_local = rows_product(hidden, grad_ffn)
    gains_local = jnp.stack([gain_zero, gain_one, gain_two, gain_three])
    summed = (
        lax.psum_scatter(
            qkv_local.astype(jnp.bfloat16), ("batch", "seq"), scatter_dimension=0, tiled=True
        ).astype(jnp.float32),
        lax.psum_scatter(
            out_local.astype(jnp.bfloat16), ("batch", "seq"), scatter_dimension=1, tiled=True
        ).astype(jnp.float32),
        lax.psum_scatter(
            gate_up_local.astype(jnp.bfloat16), ("batch", "seq"), scatter_dimension=0, tiled=True
        ).astype(jnp.float32),
        lax.psum_scatter(
            down_local.astype(jnp.bfloat16), ("batch", "seq"), scatter_dimension=1, tiled=True
        ).astype(jnp.float32),
        lax.psum_scatter(
            gains_local.astype(jnp.bfloat16), ("batch", "seq"), scatter_dimension=1, tiled=True
        ).astype(jnp.float32),
    )
    qkv_grad, out_grad, gate_up_grad, down_grad, gains_grad = summed
    qkv_new, qkv_first_new, qkv_second_new = adam_step(
        qkv_weight, qkv_grad, qkv_first, qkv_second, decay_rate
    )
    out_new, out_first_new, out_second_new = adam_step(
        out_weight, out_grad, out_first, out_second, decay_rate
    )
    gate_up_new, gate_up_first_new, gate_up_second_new = adam_step(
        gate_up_weight, gate_up_grad, gate_up_first, gate_up_second, decay_rate
    )
    down_new, down_first_new, down_second_new = adam_step(
        down_weight, down_grad, down_first, down_second, decay_rate
    )
    gains_new, gains_first_new, gains_second_new = adam_step(
        norm_gains, gains_grad, gains_first, gains_second, 0.0
    )
    return (
        layer_out[None],
        input_grad[None],
        qkv_grad,
        out_grad,
        gate_up_grad,
        down_grad,
        gains_grad,
        qkv_new,
        out_new,
        gate_up_new,
        down_new,
        gains_new,
        qkv_first_new,
        out_first_new,
        gate_up_first_new,
        down_first_new,
        gains_first_new,
        qkv_second_new,
        out_second_new,
        gate_up_second_new,
        down_second_new,
        gains_second_new,
    )


def solution(mesh):
    in_specs = (
        P("batch", "seq", None),
        P("batch", "seq", None),
        P(("batch", "seq"), "tensor", None),
        P("tensor", ("batch", "seq")),
        P(("batch", "seq"), None, "tensor"),
        P("tensor", ("batch", "seq")),
        P(None, ("batch", "seq")),
        P(("batch", "seq"), "tensor", None),
        P("tensor", ("batch", "seq")),
        P(("batch", "seq"), None, "tensor"),
        P("tensor", ("batch", "seq")),
        P(None, ("batch", "seq")),
        P(("batch", "seq"), "tensor", None),
        P("tensor", ("batch", "seq")),
        P(("batch", "seq"), None, "tensor"),
        P("tensor", ("batch", "seq")),
        P(None, ("batch", "seq")),
    )
    out_specs = (
        P("batch", "seq", None),
        P("batch", "seq", None),
        P(("batch", "seq"), "tensor", None),
        P("tensor", ("batch", "seq")),
        P(("batch", "seq"), None, "tensor"),
        P("tensor", ("batch", "seq")),
        P(None, ("batch", "seq")),
        P(("batch", "seq"), "tensor", None),
        P("tensor", ("batch", "seq")),
        P(("batch", "seq"), None, "tensor"),
        P("tensor", ("batch", "seq")),
        P(None, ("batch", "seq")),
        P(("batch", "seq"), "tensor", None),
        P("tensor", ("batch", "seq")),
        P(("batch", "seq"), None, "tensor"),
        P("tensor", ("batch", "seq")),
        P(None, ("batch", "seq")),
        P(("batch", "seq"), "tensor", None),
        P("tensor", ("batch", "seq")),
        P(("batch", "seq"), None, "tensor"),
        P("tensor", ("batch", "seq")),
        P(None, ("batch", "seq")),
    )
    sizes = tuple(mesh.shape[axis] for axis in ("batch", "seq", "tensor"))
    body = on_square if sizes == (4, 2, 4) else on_device
    return jax.shard_map(
        body, mesh=mesh, in_specs=in_specs, out_specs=out_specs, check_vma=False
    )
```

```python
import functools
import jax
import jax.numpy as jnp
from jax import lax
from jax.experimental.layout import Layout, with_layout_constraint
from jax.experimental import pallas as pl
from jax.experimental.pallas import tpu as pltpu
from jax.sharding import PartitionSpec as P

HEAD_DIM = 256
WIN_BLOCKS = 4
STEP = 10
GROUP = 2


norm_eps = 1e-06
soft_cap = 50.0
learn_rate = 0.02
decay_rate = 0.1
beta_first = 0.9
beta_second = 0.95
adam_eps = 1e-08
gelu_coef = 0.7978845608028654


def from_behind(value, axis, steps):
    count = lax.axis_size(axis)
    initial, last = (max(0, -steps), min(count, count - steps))
    return lax.ppermute(value, axis, [(source, source + steps) for source in range(initial, last)])


def rms_norm(values, gain):
    scale = lax.rsqrt(jnp.mean(values * values, axis=-1, keepdims=True) + norm_eps)
    return values * scale * (1.0 + gain)


def norm_back(values, gain, upstream):
    _, pullback = jax.vjp(rms_norm, values, gain)
    return pullback(upstream)


def gelu_tanh(values):
    inner = gelu_coef * (values + 0.044715 * values * values * values)
    return 0.5 * values * (1.0 + jnp.tanh(inner))


def geglu(gate, up_part):
    return gelu_tanh(gate) * up_part


def rope_tables(positions, head_size):
    half = head_size // 2
    exponent = jnp.arange(half, dtype=jnp.float32) * (2.0 / head_size)
    freqs = 10000.0 ** (-exponent)
    angles = positions.astype(jnp.float32)[:, None] * freqs[None, :]
    return (jnp.cos(angles), jnp.sin(angles))


def rotate(values, cosine, sine):
    half = values.shape[-1] // 2
    first = values[..., :half]
    second = values[..., half:]
    cosine = cosine[:, None, :]
    sine = sine[:, None, :]
    return jnp.concatenate(
        [first * cosine - second * sine, second * cosine + first * sine], axis=-1
    )


def adam_step(weight, grad, first, second, decay):
    first_new = beta_first * first + (1.0 - beta_first) * grad
    second_new = beta_second * second + (1.0 - beta_second) * grad * grad
    first_hat = first_new / (1.0 - beta_first**STEP)
    second_hat = second_new / (1.0 - beta_second**STEP)
    weight_new = weight - learn_rate * (
        first_hat / (jnp.sqrt(second_hat) + adam_eps) + decay * weight
    )
    return (weight_new, first_new, second_new)


def rows_product(left, right):
    return lax.dot_general(
        left, right, (((0,), (0,)), ((), ())), preferred_element_type=jnp.float32
    )


def cols_product(left, right):
    return lax.dot_general(
        left, right, (((1,), (1,)), ((), ())), preferred_element_type=jnp.float32
    )


def capped_scores(query_groups, ext_keys):
    raw = jnp.einsum(
        "icgd,jcd->cgij", query_groups, ext_keys, preferred_element_type=jnp.float32
    ) * query_groups.shape[-1] ** (-0.5)
    return soft_cap * jnp.tanh(raw / soft_cap)


def tensor_sum(part):
    return lax.psum(part, "tensor")


def swap(value, axis, bit):
    count = lax.axis_size(axis)
    return lax.ppermute(value, axis, [(source, source ^ bit) for source in range(count)])


def after(value, *earlier):
    return lax.optimization_barrier((value, earlier))[0]


def trade(value, turn):
    pairs = []
    for chip in range(4):
        for core in range(2):
            pairs.append((chip * 2 + core, (chip ^ (1 + (core ^ turn))) * 2 + core))
    return lax.ppermute(value, ("batch", "seq"), pairs)


def offsets(owner):
    return (0, 1 + owner, 2 - owner, 3)


def gather_end(shard, first, second):
    return jnp.concatenate([shard[None], first[None], second], axis=0)


def own_blocks(wide):
    tokens, width = wide.shape
    chip, core = lax.axis_index("batch"), lax.axis_index("seq")
    split = wide.reshape(tokens, 8, width // 8)
    halves = []
    for owner in (core, 1 - core):
        parts = [
            lax.dynamic_index_in_dim(split, (chip ^ offset) * 2 + owner, 1, keepdims=False)
            for offset in offsets(owner)
        ]
        halves.append(jnp.concatenate(parts, axis=1))
    return halves


def both_cores(wide):
    mine, theirs = own_blocks(wide)
    return jnp.concatenate([mine, swap(theirs, "seq", 1)], axis=0)


def weight_local(wide, narrow):
    local = rows_product(wide, narrow).astype(jnp.bfloat16)
    return local.reshape(4, -1, local.shape[1])


def scatter_begin(local):
    got = trade(jnp.stack([local[1], local[3]]), 0)
    far = local[2].astype(jnp.float32) + got[1].astype(jnp.float32)
    return local[0], got[0], far.astype(jnp.bfloat16)


def scatter_end(state):
    own, got, far = state
    return own, got, trade(far, 1)


def everywhere_sum(value):
    for axis, bit in (("seq", 1), ("batch", 1), ("batch", 2), ("tensor", 1), ("tensor", 2)):
        value = value + swap(value, axis, bit)
    return value


FFN_TILE = 768
ROW_CHUNK = 16
ROW_UNROLL = 4
MID_ROWS = 128


def spec_any():
    return pl.BlockSpec(memory_space=pl.ANY)


def spec_vmem():
    return pl.BlockSpec(memory_space=pltpu.VMEM)


def spec_smem():
    return pl.BlockSpec(memory_space=pltpu.SMEM)


def kernel_params():
    return pltpu.CompilerParams(vmem_limit_bytes=56 * 1024 * 1024)


def cost(flops, moved):
    return pl.CostEstimate(flops=flops, bytes_accessed=moved, transcendentals=0)


def shaped(shape, kind):
    return jax.ShapeDtypeStruct(shape, kind)


def dot_nn(left, right):
    return lax.dot_general(
        left, right, (((1,), (0,)), ((), ())), preferred_element_type=jnp.float32
    )


def dot_nt(left, right):
    return lax.dot_general(
        left, right, (((1,), (1,)), ((), ())), preferred_element_type=jnp.float32
    )


def dot_tn(left, right):
    return lax.dot_general(
        left, right, (((0,), (0,)), ((), ())), preferred_element_type=jnp.float32
    )


def row_scale(values):
    return lax.rsqrt(jnp.mean(values * values, axis=-1, keepdims=True) + norm_eps)


def norm_pull(values, scale, gain, upstream):
    normed = values * scale
    inner = upstream * (1.0 + gain)
    pulled = scale * (inner - normed * jnp.mean(normed * inner, axis=-1, keepdims=True))
    return pulled, upstream * normed


def fold_rows(values):
    total = values[:8]
    for start in range(8, values.shape[0], 8):
        total += values[start : start + 8]
    return total


def fetch_rows(place, near, far, target, sems, column, columns):
    chip, core = place[0], place[1]
    rows = near.shape[1]
    copies = []
    for k in range(4):
        for which, source in enumerate((near, far)):
            owner = which ^ core
            offset = (0, 1 + owner, 2 - owner, 3)[k]
            row = ((offset ^ chip) * 2 + owner) * rows
            copies.append(
                pltpu.make_async_copy(
                    source.at[k, :, pl.ds(column, columns)],
                    target.at[pl.ds(pl.multiple_of(row, 16), rows), :],
                    sems.at[k * 2 + which],
                )
            )
    return copies


def rope(values, cosine, sine):
    half = HEAD_DIM // 2
    first, second = values[:, :half], values[:, half:]
    return jnp.concatenate(
        [first * cosine - second * sine, second * cosine + first * sine], axis=1
    )


def arrange_kernel(place, near, far, result, sems):
    copies = fetch_rows(place, near, far, result, sems, 0, result.shape[1])
    for copy in copies:
        copy.start()
    for copy in copies:
        copy.wait()


def arrange(place, near, far):
    return pl.pallas_call(
        arrange_kernel,
        in_specs=[spec_smem(), spec_any(), spec_any()],
        out_specs=spec_vmem(),
        out_shape=shaped((8 * near.shape[1], near.shape[2]), jnp.bfloat16),
        scratch_shapes=[pltpu.SemaphoreType.DMA((8,))],
        compiler_params=kernel_params(),
        cost_estimate=cost(0, 4 * near.size * 4),
        name="arrange",
    )(place, near, far)


def project_kernel(place, x, near, far, cosine, sine, *rest):
    queries, pair, attn_in, gains, weight, sems = rest[-6:]
    copies = fetch_rows(place, near, far, weight, sems, 0, weight.shape[1])
    for copy in copies:
        copy.start()
    for copy in copies:
        copy.wait()
    width = (GROUP + 2) * HEAD_DIM
    tail = weight[:, width + GROUP * HEAD_DIM :].astype(jnp.float32)
    gains[...] = jnp.transpose(tail)[:8]
    gain = 1.0 + gains[0:1, :]
    chunk = ROW_CHUNK

    @pl.loop(0, x.shape[0] // chunk, unroll=ROW_UNROLL)
    def _(step):
        rows = pl.ds(pl.multiple_of(step * chunk, chunk), chunk)
        stream = x[rows, :].astype(jnp.float32)
        attn_in[rows, :] = (stream * row_scale(stream) * gain).astype(jnp.bfloat16)

    for member in range(GROUP + 2):
        columns = slice(member * HEAD_DIM, (member + 1) * HEAD_DIM)
        part = dot_nn(attn_in[...], weight[:, columns])
        if member < GROUP:
            queries[:, columns] = rope(part, cosine[...], sine[...]).astype(jnp.bfloat16)
        elif member == GROUP:
            pair[0] = rope(part, cosine[...], sine[...]).astype(jnp.bfloat16)
        else:
            pair[1] = part.astype(jnp.bfloat16)


def project(place, x, near, far, cosine, sine, *earlier):
    tokens, width = x.shape
    bf16 = jnp.bfloat16
    return pl.pallas_call(
        project_kernel,
        in_specs=[spec_smem(), spec_vmem(), spec_any(), spec_any(), spec_vmem(), spec_vmem()]
        + [spec_any()] * len(earlier),
        out_specs=[spec_vmem()] * 4,
        out_shape=[
            shaped((tokens, GROUP * HEAD_DIM), bf16),
            shaped((2, tokens, HEAD_DIM), bf16),
            shaped((tokens, width), bf16),
            shaped((8, width), jnp.float32),
        ],
        scratch_shapes=[pltpu.VMEM((width, near.shape[2]), bf16), pltpu.SemaphoreType.DMA((8,))],
        compiler_params=kernel_params(),
        cost_estimate=cost(2 * tokens * width * 1024, 12_000_000),
        name="project",
    )(place, x, near, far, cosine, sine, *earlier)


def chunk_scores(query, key, behind, row, core):
    raw = dot_nt(query, key) * (HEAD_DIM**-0.5 / soft_cap)
    bent = jnp.tanh(raw)
    powers = jnp.exp(soft_cap * bent)
    if behind:
        powers = jnp.where(core > 0, powers, 0.0)
    else:
        at = row + lax.broadcasted_iota(jnp.int32, powers.shape, 0)
        powers = jnp.where(at >= lax.broadcasted_iota(jnp.int32, powers.shape, 1), powers, 0.0)
    return bent, powers


def attend_kernel(place, queries, pair, behind, near, far, *rest):
    attended, result, weight, sems = rest[-4:]
    width = (GROUP + 2) * HEAD_DIM
    copies = fetch_rows(place, near, far, weight, sems, width, GROUP * HEAD_DIM)
    for copy in copies:
        copy.start()
    core = place[1]
    chunk = 128
    tokens = queries.shape[0]
    for start in range(0, tokens, chunk):
        rows = slice(start, start + chunk)
        keys = start + chunk
        for head in range(GROUP):
            columns = slice(head * HEAD_DIM, (head + 1) * HEAD_DIM)
            query = queries[rows, columns]
            _, old = chunk_scores(query, behind[0], True, start, core)
            _, new = chunk_scores(query, pair[0, :keys], False, start, core)
            total = jnp.sum(old, axis=-1, keepdims=True) + jnp.sum(new, axis=-1, keepdims=True)
            share = 1.0 / total
            value = dot_nn((old * share).astype(jnp.bfloat16), behind[1])
            value += dot_nn((new * share).astype(jnp.bfloat16), pair[1, :keys])
            attended[rows, columns] = value.astype(jnp.bfloat16)
    for copy in copies:
        copy.wait()
    tile = 768
    for column in range(0, result.shape[1], tile):
        part = dot_nt(attended[...], weight[column : column + tile, :])
        result[:, column : column + tile] = part.astype(jnp.bfloat16)


def attend(place, queries, pair, behind, near, far, width, *earlier):
    tokens = queries.shape[0]
    bf16 = jnp.bfloat16
    return pl.pallas_call(
        attend_kernel,
        in_specs=[spec_smem()] + [spec_vmem()] * 3 + [spec_any()] * (2 + len(earlier)),
        out_specs=[spec_vmem()] * 2,
        out_shape=[shaped((tokens, GROUP * HEAD_DIM), bf16), shaped((tokens, width), bf16)],
        scratch_shapes=[
            pltpu.VMEM((width, GROUP * HEAD_DIM), bf16),
            pltpu.SemaphoreType.DMA((8,)),
        ],
        compiler_params=kernel_params(),
        cost_estimate=cost(4 * tokens * width * 1024, 8_000_000),
        name="attend",
    )(place, queries, pair, behind, near, far, *earlier)


def whole(shape):
    return pl.BlockSpec(shape, lambda *_: (0,) * len(shape))


def ffn_params():
    return pltpu.CompilerParams(vmem_limit_bytes=58 * 1024 * 1024)


def move(source, target, sem):
    copy = pltpu.make_async_copy(source, target, sem)
    copy.start()
    return copy


def ffn_kernel(attn_out, x, gains, gate_up, down, *rest):
    outs, (sides, gate_up_here, down_here, in_sems, down_sems, out_sems) = rest[-11:-6], rest[-6:]
    ffn_in, hidden, by_gate, by_up, result = (sides.at[k] for k in range(5))
    tokens, width = x.shape
    units = gate_up.shape[2]
    tile = FFN_TILE
    steps, turns = units // tile, width // tile

    def load(step):
        columns = pl.ds(pl.multiple_of(step * tile, tile), tile)
        return pltpu.make_async_copy(
            gate_up.at[:, :, columns], gate_up_here.at[:, :, columns], in_sems.at[step]
        )

    def load_down(turn):
        rows = pl.ds(pl.multiple_of(turn * tile, tile), tile)
        return pltpu.make_async_copy(down.at[rows, :], down_here.at[rows, :], down_sems.at[turn])

    for step in range(steps):
        load(step).start()
    for turn in range(turns):
        load_down(turn).start()
    chunk = ROW_CHUNK

    @pl.loop(0, tokens // chunk, unroll=ROW_UNROLL)
    def _(step):
        rows = pl.ds(pl.multiple_of(step * chunk, chunk), chunk)
        out = attn_out[rows, :].astype(jnp.float32)
        mid = x[rows, :].astype(jnp.float32) + out * row_scale(out) * (1.0 + gains[1:2, :])
        ffn_in[rows, :] = (mid * row_scale(mid) * (1.0 + gains[2:3, :])).astype(jnp.bfloat16)

    stores = [move(ffn_in, outs[0], out_sems.at[0])]

    @pl.loop(0, steps)
    def _(step):
        load(step).wait()
        columns = pl.ds(pl.multiple_of(step * tile, tile), tile)
        for rows in (slice(None),):
            value = ffn_in[...]
            gate = dot_nn(value, gate_up_here[0, :, columns])
            up = dot_nn(value, gate_up_here[1, :, columns])
            square_of = gate * gate
            bent = jnp.tanh(gate * (gelu_coef + gelu_coef * 0.044715 * square_of))
            half = 0.5 + 0.5 * bent
            curve = gate * half
            slope = half + curve * (1.0 - bent) * (
                gelu_coef + 3.0 * gelu_coef * 0.044715 * square_of
            )
            hidden[rows, columns] = (curve * up).astype(jnp.bfloat16)
            by_gate[rows, columns] = (slope * up).astype(jnp.bfloat16)
            by_up[rows, columns] = curve.astype(jnp.bfloat16)

    for k, side in ((1, hidden), (2, by_gate), (3, by_up)):
        stores.append(move(side, outs[k], out_sems.at[k]))

    def store(turn):
        columns = pl.ds(pl.multiple_of(turn * tile, tile), tile)
        return pltpu.make_async_copy(
            result.at[:, columns], outs[4].at[:, columns], out_sems.at[4 + turn]
        )

    @pl.loop(0, turns)
    def _(turn):
        load_down(turn).wait()
        rows = pl.ds(pl.multiple_of(turn * tile, tile), tile)
        result[:, rows] = dot_nt(hidden[...], down_here[rows, :]).astype(jnp.bfloat16)
        store(turn).start()

    for copy in stores:
        copy.wait()
    for turn in range(turns):
        store(turn).wait()


def ffn_forward(attn_out, x, gains, gate_up, down, *earlier):
    tokens, width = x.shape
    units = gate_up.shape[2]
    bf16 = jnp.bfloat16
    return pl.pallas_call(
        ffn_kernel,
        in_specs=[spec_vmem()] * 3 + [spec_any()] * (2 + len(earlier)),
        out_specs=[spec_any()] * 5,
        out_shape=[shaped((tokens, width), bf16)]
        + [shaped((tokens, units), bf16)] * 3
        + [shaped((tokens, width), bf16)],
        scratch_shapes=[
            pltpu.VMEM((5, tokens, width), bf16),
            pltpu.VMEM((2, width, units), bf16),
            pltpu.VMEM((width, units), bf16),
            pltpu.SemaphoreType.DMA((units // FFN_TILE,)),
            pltpu.SemaphoreType.DMA((width // FFN_TILE,)),
            pltpu.SemaphoreType.DMA((4 + width // FFN_TILE,)),
        ],
        compiler_params=ffn_params(),
        cost_estimate=cost(6 * tokens * width * units, 50_000_000),
        name="ffn_forward",
    )(attn_out, x, gains, gate_up, down, *earlier)


def ffn_back_kernel(ffn_out, top, gains, gate_up, down, by_gate, by_up, *rest):
    grad_out, gate_out, up_out, gain_out, result_out = rest[-13:-8]
    sides, grads, gate_up_here, down_here, in_sems, down_sems, gate_sems, out_sems = rest[-8:]
    grad_ffn, result = sides.at[0], sides.at[1]
    tokens, width = top.shape
    units = gate_up.shape[2]
    grad_gate, grad_up = grads.at[:, pl.ds(0, units)], grads.at[:, pl.ds(units, units)]
    tile = FFN_TILE
    steps, turns = units // tile, width // tile

    def load_down(step):
        columns = pl.ds(pl.multiple_of(step * tile, tile), tile)
        return pltpu.make_async_copy(
            down.at[:, columns], down_here.at[:, columns], down_sems.at[step]
        )

    def load(turn, which):
        rows = pl.ds(pl.multiple_of(turn * tile, tile), tile)
        return pltpu.make_async_copy(
            gate_up.at[which, rows, :],
            gate_up_here.at[rows, pl.ds(which * units, units)],
            gate_sems.at[turn, which],
        )

    load_down(0).start()
    factors = [
        move(by_gate, grad_gate, in_sems.at[0]),
        move(by_up, grad_up, in_sems.at[1]),
    ]
    load_down(1).start()
    gain_out[...] = jnp.zeros_like(gain_out)
    chunk = ROW_CHUNK

    @pl.loop(0, tokens // chunk, unroll=ROW_UNROLL)
    def _(step):
        rows = pl.ds(pl.multiple_of(step * chunk, chunk), chunk)
        out = ffn_out[rows, :].astype(jnp.float32)
        upstream = top[rows, :].astype(jnp.float32)
        pulled, product = norm_pull(out, row_scale(out), gains[3:4, :], upstream)
        grad_ffn[rows, :] = pulled.astype(jnp.bfloat16)
        gain_out[...] += fold_rows(product)

    stores = [move(grad_ffn, grad_out, out_sems.at[0])]
    for copy in factors:
        copy.wait()

    @pl.loop(0, steps)
    def _(step):
        load_down(step).wait()

        @pl.when(step + 2 < steps)
        def _():
            load_down(step + 2).start()

        @pl.when(step + 2 >= steps)
        def _():
            load(step + 2 - steps, 0).start()
            load(step + 2 - steps, 1).start()

        columns = pl.ds(pl.multiple_of(step * tile, tile), tile)
        for start in range(0, tokens, tokens // 2):
            rows = pl.ds(start, tokens // 2)
            grad_hidden = dot_nn(grad_ffn[rows, :], down_here[:, columns])
            one = grad_hidden * grad_gate[rows, columns].astype(jnp.float32)
            two = grad_hidden * grad_up[rows, columns].astype(jnp.float32)
            grad_gate[rows, columns] = one.astype(jnp.bfloat16)
            grad_up[rows, columns] = two.astype(jnp.bfloat16)

    stores.append(move(grad_gate, gate_out, out_sems.at[1]))
    stores.append(move(grad_up, up_out, out_sems.at[2]))

    def store(turn):
        columns = pl.ds(pl.multiple_of(turn * tile, tile), tile)
        return pltpu.make_async_copy(
            result.at[:, columns], result_out.at[:, columns], out_sems.at[3 + turn]
        )

    @pl.loop(0, turns)
    def _(turn):
        load(turn, 0).wait()
        load(turn, 1).wait()

        @pl.when(turn + 2 < turns)
        def _():
            load(turn + 2, 0).start()
            load(turn + 2, 1).start()

        rows = pl.ds(pl.multiple_of(turn * tile, tile), tile)
        part = dot_nt(grads[...], gate_up_here[rows, :])
        result[:, rows] = part.astype(jnp.bfloat16)
        store(turn).start()

    for copy in stores:
        copy.wait()
    for turn in range(turns):
        store(turn).wait()


def ffn_back(ffn_out, top, gains, gate_up, down, by_gate, by_up, *earlier):
    tokens, width = top.shape
    units = by_up.shape[1]
    bf16 = jnp.bfloat16
    return pl.pallas_call(
        ffn_back_kernel,
        in_specs=[spec_vmem()] * 3 + [spec_any()] * (4 + len(earlier)),
        out_specs=[spec_any()] * 3 + [spec_vmem(), spec_any()],
        out_shape=[
            shaped((tokens, width), bf16),
            shaped((tokens, units), bf16),
            shaped((tokens, units), bf16),
            shaped((8, width), jnp.float32),
            shaped((tokens, width), bf16),
        ],
        scratch_shapes=[
            pltpu.VMEM((2, tokens, width), bf16),
            pltpu.VMEM((tokens, 2 * units), bf16),
            pltpu.VMEM((width, 2 * units), bf16),
            pltpu.VMEM((width, units), bf16),
            pltpu.SemaphoreType.DMA((2,)),
            pltpu.SemaphoreType.DMA((units // FFN_TILE,)),
            pltpu.SemaphoreType.DMA((width // FFN_TILE, 2)),
            pltpu.SemaphoreType.DMA((3 + width // FFN_TILE,)),
        ],
        compiler_params=ffn_params(),
        cost_estimate=cost(6 * tokens * width * units, 55_000_000),
        name="ffn_back",
    )(ffn_out, top, gains, gate_up, down, by_gate, by_up, *earlier)


def mid_back_kernel(place, grad_in, x, attn_out, top, gains, near, far, *rest):
    grad_mid, grad_attn, grad_att, gain_out, weight, sems = rest[-6:]
    width = (GROUP + 2) * HEAD_DIM
    first = pl.program_id(0) == 0

    def fetch():
        return fetch_rows(place, near, far, weight, sems, width, GROUP * HEAD_DIM)

    @pl.when(first)
    def _():
        gain_out[...] = jnp.zeros_like(gain_out)
        for copy in fetch():
            copy.start()

    chunk = ROW_CHUNK

    @pl.loop(0, x.shape[0] // chunk, unroll=ROW_UNROLL)
    def _(step):
        rows = pl.ds(pl.multiple_of(step * chunk, chunk), chunk)
        out = attn_out[rows, :].astype(jnp.float32)
        out_scale = row_scale(out)
        mid = x[rows, :].astype(jnp.float32) + out * out_scale * (1.0 + gains[1:2, :])
        upstream = grad_in[rows, :].astype(jnp.float32)
        pulled, product = norm_pull(mid, row_scale(mid), gains[2:3, :], upstream)
        gain_out[1] += fold_rows(product)
        at_mid = top[rows, :].astype(jnp.float32) + pulled
        grad_mid[rows, :] = at_mid
        pulled, product = norm_pull(out, out_scale, gains[1:2, :], at_mid)
        gain_out[0] += fold_rows(product)
        grad_attn[rows, :] = pulled.astype(jnp.bfloat16)

    @pl.when(first)
    def _():
        for copy in fetch():
            copy.wait()

    grad_att[...] = dot_nn(grad_attn[...], weight[...]).astype(jnp.bfloat16)


def mid_back(place, grad_in, x, attn_out, top, gains, near, far, *earlier):
    tokens, width = x.shape
    heads = GROUP * HEAD_DIM
    bf16 = jnp.bfloat16
    rows = pl.BlockSpec((MID_ROWS, width), lambda i: (i, 0))
    return pl.pallas_call(
        mid_back_kernel,
        grid=(tokens // MID_ROWS,),
        in_specs=[spec_smem()]
        + [rows] * 4
        + [whole((8, width))]
        + [spec_any()] * (2 + len(earlier)),
        out_specs=[
            rows,
            rows,
            pl.BlockSpec((MID_ROWS, heads), lambda i: (i, 0)),
            whole((2, 8, width)),
        ],
        out_shape=[
            shaped((tokens, width), jnp.float32),
            shaped((tokens, width), bf16),
            shaped((tokens, heads), bf16),
            shaped((2, 8, width), jnp.float32),
        ],
        scratch_shapes=[pltpu.VMEM((width, heads), bf16), pltpu.SemaphoreType.DMA((8,))],
        compiler_params=kernel_params(),
        cost_estimate=cost(2 * tokens * width * heads, 24_000_000),
        name="mid_back",
    )(place, grad_in, x, attn_out, top, gains, near, far, *earlier)


def attend_back_kernel(
    place, queries, pair, behind, attended, grad_att, cosine, sine, *rest
):
    grad_q, grad_own, grad_old, sums = rest[-4:]
    core = place[1]
    chunk = 128
    tokens = queries.shape[0]
    scale = HEAD_DIM**-0.5
    sums[...] = jnp.zeros_like(sums)
    for start in range(0, tokens, chunk):
        rows = slice(start, start + chunk)
        keys = start + chunk
        cos, sin = cosine[rows, :], sine[rows, :]
        for head in range(GROUP):
            columns = slice(head * HEAD_DIM, (head + 1) * HEAD_DIM)
            query, upstream = queries[rows, columns], grad_att[rows, columns]
            delta = jnp.sum(
                upstream.astype(jnp.float32) * attended[rows, columns].astype(jnp.float32),
                axis=-1,
                keepdims=True,
            )
            bent_old, old = chunk_scores(query, behind[0], True, start, core)
            bent_new, new = chunk_scores(query, pair[0, :keys], False, start, core)
            share = 1.0 / (
                jnp.sum(old, axis=-1, keepdims=True) + jnp.sum(new, axis=-1, keepdims=True)
            )
            total = jnp.zeros((chunk, HEAD_DIM), jnp.float32)
            for bent, powers, block, end, base in (
                (bent_old, old, behind, tokens, 0),
                (bent_new, new, pair, keys, 2),
            ):
                prob = powers * share
                grad_p = dot_nt(upstream, block[1, :end])
                grad_s = (prob * (grad_p - delta) * (1.0 - bent * bent)).astype(jnp.bfloat16)
                total += dot_nn(grad_s, block[0, :end])
                sums[base, :end, :] += dot_tn(grad_s, query)
                sums[base + 1, :end, :] += dot_tn(prob.astype(jnp.bfloat16), upstream)
            grad_q[rows, columns] = rope(total * scale, cos, -sin).astype(jnp.bfloat16)
    grad_old[0] = (sums[0] * scale).astype(jnp.bfloat16)
    grad_old[1] = sums[1].astype(jnp.bfloat16)
    grad_own[0] = sums[2] * scale
    grad_own[1] = sums[3]


def attend_back(place, queries, pair, behind, attended, grad_att, cosine, sine, *earlier):
    tokens, heads = queries.shape
    bf16 = jnp.bfloat16
    return pl.pallas_call(
        attend_back_kernel,
        in_specs=[spec_smem()] + [spec_vmem()] * 7 + [spec_any()] * len(earlier),
        out_specs=[spec_vmem()] * 3,
        out_shape=[
            shaped((tokens, heads), bf16),
            shaped((2, tokens, HEAD_DIM), jnp.float32),
            shaped((2, tokens, HEAD_DIM), bf16),
        ],
        scratch_shapes=[pltpu.VMEM((4, tokens, HEAD_DIM), jnp.float32)],
        compiler_params=kernel_params(),
        cost_estimate=cost(20 * tokens * 1024 * heads, 5_000_000),
        name="attend_back",
    )(place, queries, pair, behind, attended, grad_att, cosine, sine, *earlier)


def project_back_kernel(
    place, grad_q, grad_own, grad_ahead, cosine, sine, x, near, far, *rest
):
    proj, result, gain_out, weight, sems = rest[-5:]
    width = (GROUP + 2) * HEAD_DIM
    copies = fetch_rows(place, near, far, weight, sems, 0, width)
    for copy in copies:
        copy.start()
    heads = GROUP * HEAD_DIM
    proj[:, :heads] = grad_q[...]
    grad_key = grad_own[0] + grad_ahead[0].astype(jnp.float32)
    proj[:, heads : heads + HEAD_DIM] = rope(grad_key, cosine[...], -sine[...]).astype(jnp.bfloat16)
    proj[:, heads + HEAD_DIM :] = (grad_own[1] + grad_ahead[1].astype(jnp.float32)).astype(
        jnp.bfloat16
    )
    gain_out[...] = jnp.zeros_like(gain_out)
    for copy in copies:
        copy.wait()
    tile = 768
    for column in range(0, result.shape[1], tile):
        part = dot_nt(proj[...], weight[column : column + tile, :])
        result[:, column : column + tile] = part.astype(jnp.bfloat16)
    chunk = ROW_CHUNK

    @pl.loop(0, x.shape[0] // chunk, unroll=ROW_UNROLL)
    def _(step):
        rows = pl.ds(pl.multiple_of(step * chunk, chunk), chunk)
        stream = x[rows, :].astype(jnp.float32)
        product = result[rows, :].astype(jnp.float32) * (stream * row_scale(stream))
        gain_out[...] += fold_rows(product)


def project_back(place, grad_q, grad_own, grad_ahead, cosine, sine, x, near, far, *earlier):
    tokens, width = x.shape
    proj_width = (GROUP + 2) * HEAD_DIM
    bf16 = jnp.bfloat16
    return pl.pallas_call(
        project_back_kernel,
        in_specs=[spec_smem()]
        + [spec_vmem()] * 6
        + [spec_any()] * 2
        + [spec_any()] * len(earlier),
        out_specs=[spec_vmem()] * 3,
        out_shape=[
            shaped((tokens, proj_width), bf16),
            shaped((tokens, width), bf16),
            shaped((8, width), jnp.float32),
        ],
        scratch_shapes=[pltpu.VMEM((width, proj_width), bf16), pltpu.SemaphoreType.DMA((8,))],
        compiler_params=kernel_params(),
        cost_estimate=cost(2 * tokens * width * proj_width, 14_000_000),
        name="project_back",
    )(place, grad_q, grad_own, grad_ahead, cosine, sine, x, near, far, *earlier)


def stream_back_kernel(grad_in, x, gains, grad_mid, *rest):
    result = rest[-1]
    chunk = ROW_CHUNK

    @pl.loop(0, x.shape[0] // chunk, unroll=ROW_UNROLL)
    def _(step):
        rows = pl.ds(pl.multiple_of(step * chunk, chunk), chunk)
        stream = x[rows, :].astype(jnp.float32)
        upstream = grad_in[rows, :].astype(jnp.float32)
        pulled, _ = norm_pull(stream, row_scale(stream), gains[0:1, :], upstream)
        result[rows, :] = grad_mid[rows, :] + pulled


def stream_back(grad_in, x, gains, grad_mid, *earlier):
    tokens, width = x.shape
    tile = MID_ROWS
    rows = pl.BlockSpec((tile, width), lambda i: (i, 0))
    return pl.pallas_call(
        stream_back_kernel,
        grid=(tokens // tile,),
        in_specs=[rows, rows, whole((8, width)), rows] + [spec_any()] * len(earlier),
        out_specs=rows,
        out_shape=shaped((tokens, width), jnp.float32),
        compiler_params=kernel_params(),
        cost_estimate=cost(20 * tokens * width, 14_000_000),
        name="stream_back",
    )(grad_in, x, gains, grad_mid, *earlier)


def flat(values):
    rows, pair, width = values.shape
    lanes = width // 128
    if pair == 1:
        return values.reshape(rows * lanes, 128)
    tiles = with_layout_constraint(
        values.reshape(rows, pair, lanes, 128), Layout(major_to_minor=(0, 2, 1, 3))
    )
    return tiles.transpose(0, 2, 1, 3).reshape(rows * pair * lanes, 128)


def unflat(values, shape):
    rows, pair, width = shape
    lanes = width // 128
    if pair == 1:
        return values.reshape(shape)
    tiles = values.reshape(rows, lanes, pair, 128).transpose(0, 2, 1, 3)
    return with_layout_constraint(tiles, Layout(major_to_minor=(0, 2, 1, 3))).reshape(shape)


def join_kernel(*refs):
    result = refs[-1]
    for which in range(2):
        own, got, far = (refs[which * 3 + k][...].astype(jnp.float32) for k in range(3))
        result[:, which, :] = own + got + far


def join(gate, up):
    rows, width = gate[0].shape
    tile = 32
    block = pl.BlockSpec((tile, width), lambda i: (i, 0))
    return pl.pallas_call(
        join_kernel,
        grid=(rows // tile,),
        in_specs=[block] * 6,
        out_specs=pl.BlockSpec((tile, 2, width), lambda i: (i, 0, 0)),
        out_shape=shaped((rows, 2, width), jnp.float32),
        compiler_params=kernel_params(),
        cost_estimate=cost(0, 200_000_000),
        name="join",
    )(*gate, *up)


def adam_kernel(parts, decay, *refs):
    weight, first, second = (ref[...] for ref in refs[parts : parts + 3])
    outs = refs[parts + 3 :]
    grad = refs[0][...].astype(jnp.float32)
    for ref in refs[1:parts]:
        grad += ref[...].astype(jnp.float32)
    if parts > 1:
        outs[-1][...] = grad
    outs[0][...], outs[1][...], outs[2][...] = adam_step(weight, grad, first, second, decay)


def adam(grads, weight, first, second, decay):
    rows, width = weight.shape
    tile = rows // 9
    block = pl.BlockSpec((tile, width), lambda i: (i, 0))
    count = 3 if len(grads) == 1 else 4
    return pl.pallas_call(
        functools.partial(adam_kernel, len(grads), decay),
        grid=(9,),
        in_specs=[block] * (len(grads) + 3),
        out_specs=[block] * count,
        out_shape=[shaped((rows, width), jnp.float32)] * count,
        compiler_params=kernel_params(),
        cost_estimate=cost(0, 200_000_000),
        name="adam",
    )(*grads, weight, first, second)


def on_square(
    layer_in,
    cotangent,
    qkv_weight,
    out_weight,
    gate_up_weight,
    down_weight,
    norm_gains,
    qkv_first,
    out_first,
    gate_up_first,
    down_first,
    gains_first,
    qkv_second,
    out_second,
    gate_up_second,
    down_second,
    gains_second,
):
    tok_rows = layer_in.shape[1]
    chip, core = lax.axis_index("batch"), lax.axis_index("seq")
    place = jnp.stack([chip, core]).astype(jnp.int32)
    plane = ("batch", "seq")
    stream, top = layer_in[0], cotangent[0]
    gains_cast = jnp.pad(norm_gains.T, ((0, 0), (0, 128 - norm_gains.shape[0])))
    attn_cast = jnp.concatenate([qkv_weight[:, 0], out_weight.T, gains_cast], axis=1)
    gate_up_cast = gate_up_weight.astype(jnp.bfloat16).transpose(1, 0, 2)
    down_cast = down_weight.T.astype(jnp.bfloat16)
    attn_cast = attn_cast.astype(jnp.bfloat16)
    first, down_cast, gate_up_cast = lax.optimization_barrier(
        (trade(attn_cast, 0), down_cast, gate_up_cast)
    )
    second = trade(jnp.stack([attn_cast, first]), 1)
    down_one = trade(down_cast, 0)
    near = gather_end(attn_cast, first, second)
    far = swap(near, "seq", 1)
    down_one, far = lax.optimization_barrier((down_one, far))
    down_two = trade(jnp.stack([down_cast, down_one]), 1)
    down_near = gather_end(down_cast, down_one, down_two)
    down = arrange(place, down_near, swap(down_near, "seq", 1))
    gate_up = lax.all_gather(gate_up_cast, plane, axis=1, tiled=True)
    positions = core * tok_rows + jnp.arange(tok_rows, dtype=jnp.int32)
    cosine, sine = rope_tables(positions, HEAD_DIM)

    queries, pair, attn_in, gains = project(
        place, stream, near, far, cosine, sine, gate_up_cast
    )
    behind = from_behind(pair, "seq", 1)
    attended, attn_part = attend(
        place, queries, pair, behind, near, far, stream.shape[1], down_two
    )
    attn_out = tensor_sum(attn_part)
    ffn_in, hidden, by_gate, by_up, ffn_part = ffn_forward(attn_out, stream, gains, gate_up, down)
    ffn_out = tensor_sum(ffn_part)

    att_both = jnp.concatenate([attended, swap(attended, "seq", 1)], axis=0)
    attn_in_both = both_cores(attn_in)
    ffn_in_both = both_cores(ffn_in)
    hidden_both = jnp.concatenate([hidden, swap(hidden, "seq", 1)], axis=0)
    grad_ffn, grad_gate, grad_up, gain_ffn, grad_ffn_part = ffn_back(
        ffn_out, top, gains, gate_up, down, by_gate, by_up, att_both, attn_in_both, ffn_in_both,
        hidden_both
    )
    grad_ffn_in = tensor_sum(grad_ffn_part)
    grad_gate_both = jnp.concatenate([grad_gate, swap(grad_gate, "seq", 1)], axis=0)
    grad_up_both = jnp.concatenate([grad_up, swap(grad_up, "seq", 1)], axis=0)
    down_local = weight_local(both_cores(grad_ffn), hidden_both)
    gate_local = weight_local(ffn_in_both, grad_gate_both)
    up_local = weight_local(ffn_in_both, grad_up_both)
    down_state = scatter_begin(down_local)
    gate_state = scatter_begin(gate_local)
    up_state = scatter_begin(up_local)
    down_grad = scatter_end(down_state)

    grad_mid, grad_attn, grad_att, gain_mid = mid_back(
        place, grad_ffn_in, stream, attn_out, top, gains, near, far, down_state[2], gate_state[1]
    )
    gate_grad = scatter_end(gate_state)
    grad_q, grad_own, grad_old = attend_back(
        place, queries, pair, behind, attended, grad_att, cosine, sine
    )
    grad_ahead = from_behind(grad_old, "seq", -1)
    grad_proj, grad_attn_part, gain_attn = project_back(
        place, grad_q, grad_own, grad_ahead, cosine, sine, stream, near, far, down_grad[2], up_state[1]
    )
    grad_attn_in = tensor_sum(grad_attn_part)
    up_grad = scatter_end(up_state)
    gate_up_grad = join(gate_grad, up_grad)

    out_local = weight_local(both_cores(grad_attn), att_both)
    out_grad = scatter_end(scatter_begin(out_local))
    proj_both = jnp.concatenate([grad_proj, swap(grad_proj, "seq", 1)], axis=0)
    qkv_local = weight_local(attn_in_both, proj_both)
    qkv_grad = sum(part.astype(jnp.float32) for part in scatter_end(scatter_begin(qkv_local)))[:, None]
    gains_rest = jnp.concatenate([gain_mid, gain_ffn[None]], axis=0).sum(axis=1)
    gains_rest = jnp.where(lax.axis_index("tensor") == 0, gains_rest, 0.0)
    gains_total = everywhere_sum(jnp.concatenate([gain_attn.sum(axis=0)[None], gains_rest], axis=0))
    own_columns = norm_gains.shape[1]
    gains_grad = lax.dynamic_slice_in_dim(
        gains_total, (chip * 2 + core) * own_columns, own_columns, axis=1
    )
    attn_float = attn_out.astype(jnp.float32)
    mid_stream = stream.astype(jnp.float32) + rms_norm(attn_float, gains[1])
    layer_out = (mid_stream + rms_norm(ffn_out.astype(jnp.float32), gains[3])).astype(jnp.bfloat16)
    qkv_shape, gate_up_shape = qkv_weight.shape, gate_up_weight.shape
    qkv_new, qkv_first_new, qkv_second_new = (
        unflat(value, qkv_shape)
        for value in adam(
            [flat(qkv_grad)], flat(qkv_weight), flat(qkv_first), flat(qkv_second), decay_rate
        )
    )
    out_new, out_first_new, out_second_new, out_grad = adam(
        out_grad, out_weight.T, out_first.T, out_second.T, decay_rate
    )
    gate_up_new, gate_up_first_new, gate_up_second_new = (
        unflat(value, gate_up_shape)
        for value in adam(
            [flat(gate_up_grad)],
            flat(gate_up_weight),
            flat(gate_up_first),
            flat(gate_up_second),
            decay_rate,
        )
    )
    down_new, down_first_new, down_second_new, down_grad = adam(
        down_grad, down_weight.T, down_first.T, down_second.T, decay_rate
    )
    gains_new, gains_first_new, gains_second_new = adam_step(
        norm_gains, gains_grad, gains_first, gains_second, 0.0
    )
    input_grad = stream_back(
        grad_attn_in, stream, gains, grad_mid, qkv_new, out_new, gate_up_new, down_new, gains_new
    )
    return (
        layer_out[None],
        input_grad[None],
        qkv_grad,
        out_grad.T,
        gate_up_grad,
        down_grad.T,
        gains_grad,
        qkv_new,
        out_new.T,
        gate_up_new,
        down_new.T,
        gains_new,
        qkv_first_new,
        out_first_new.T,
        gate_up_first_new,
        down_first_new.T,
        gains_first_new,
        qkv_second_new,
        out_second_new.T,
        gate_up_second_new,
        down_second_new.T,
        gains_second_new,
    )


def on_device(
    layer_in,
    cotangent,
    qkv_weight,
    out_weight,
    gate_up_weight,
    down_weight,
    norm_gains,
    qkv_first,
    out_first,
    gate_up_first,
    down_first,
    gains_first,
    qkv_second,
    out_second,
    gate_up_second,
    down_second,
    gains_second,
):
    tok_rows = layer_in.shape[1]
    seq_index = lax.axis_index("seq")
    collected = (
        lax.all_gather(qkv_weight.astype(jnp.bfloat16), ("batch", "seq"), axis=0, tiled=True),
        lax.all_gather(out_weight.astype(jnp.bfloat16), ("batch", "seq"), axis=1, tiled=True),
        lax.all_gather(gate_up_weight.astype(jnp.bfloat16), ("batch", "seq"), axis=0, tiled=True),
        lax.all_gather(down_weight.astype(jnp.bfloat16), ("batch", "seq"), axis=1, tiled=True),
        lax.all_gather(norm_gains.astype(jnp.bfloat16), ("batch", "seq"), axis=1, tiled=True),
    )
    qkv_full, out_full, gate_up_full, down_full, gains_full = collected
    model_width = qkv_full.shape[0]
    kv_local = qkv_full.shape[1]
    heads_local = kv_local * GROUP
    ffn_local = gate_up_full.shape[2]
    qkv_flat = qkv_full.reshape(model_width, kv_local * (GROUP + 2) * HEAD_DIM)
    gate_up_flat = gate_up_full.reshape(model_width, 2 * ffn_local)
    gains_float = gains_full.astype(jnp.float32)
    positions = seq_index * tok_rows + jnp.arange(tok_rows, dtype=jnp.int32)
    cosine, sine = rope_tables(positions, HEAD_DIM)
    key_positions = (seq_index - WIN_BLOCKS) * tok_rows + jnp.arange(
        (WIN_BLOCKS + 1) * tok_rows, dtype=jnp.int32
    )
    spread = positions[:, None] - key_positions[None, :]
    allowed = (spread >= 0) & (spread < WIN_BLOCKS * tok_rows) & (key_positions >= 0)[None, :]
    mask = allowed[None, None]
    stream = layer_in[0].astype(jnp.float32)
    attn_in = rms_norm(stream, gains_float[0]).astype(jnp.bfloat16)
    projected = jnp.dot(attn_in, qkv_flat, preferred_element_type=jnp.float32).reshape(
        tok_rows, kv_local, GROUP + 2, HEAD_DIM
    )
    queries = rotate(
        projected[:, :, :GROUP].reshape(tok_rows, heads_local, HEAD_DIM), cosine, sine
    ).astype(jnp.bfloat16)
    keys = rotate(projected[:, :, GROUP], cosine, sine).astype(jnp.bfloat16)
    values = projected[:, :, GROUP + 1].astype(jnp.bfloat16)
    kv_pair = jnp.stack([keys, values], axis=0)
    reach = min(WIN_BLOCKS, lax.axis_size("seq") - 1)
    pieces = []
    for distance in range(WIN_BLOCKS, 0, -1):
        if distance <= reach:
            pieces.append(from_behind(kv_pair, "seq", distance))
        else:
            pieces.append(jnp.zeros_like(kv_pair))
    pieces.append(kv_pair)
    extended = jnp.concatenate(pieces, axis=1)
    ext_keys = extended[0]
    ext_values = extended[1]
    query_groups = queries.reshape(tok_rows, kv_local, GROUP, HEAD_DIM)
    capped = capped_scores(query_groups, ext_keys)
    log_sums = jnp.log(jnp.sum(jnp.where(mask, jnp.exp(capped), 0.0), axis=-1))
    probs = jnp.where(mask, jnp.exp(capped - log_sums[..., None]), 0.0).astype(jnp.bfloat16)
    attended = jnp.einsum(
        "cgij,jcd->icgd", probs, ext_values, preferred_element_type=jnp.float32
    ).astype(jnp.bfloat16)
    att_flat = attended.reshape(tok_rows, heads_local * HEAD_DIM)
    attn_out = lax.psum(jnp.dot(att_flat, out_full, preferred_element_type=jnp.float32), "tensor")
    mid_stream = stream + rms_norm(attn_out, gains_float[1])
    ffn_in = rms_norm(mid_stream, gains_float[2]).astype(jnp.bfloat16)
    gate_up = jnp.dot(ffn_in, gate_up_flat, preferred_element_type=jnp.float32).reshape(
        tok_rows, 2, ffn_local
    )
    hidden = geglu(gate_up[:, 0], gate_up[:, 1]).astype(jnp.bfloat16)
    ffn_out = lax.psum(jnp.dot(hidden, down_full, preferred_element_type=jnp.float32), "tensor")
    layer_out = (mid_stream + rms_norm(ffn_out, gains_float[3])).astype(jnp.bfloat16)
    grad_top = cotangent[0].astype(jnp.float32)
    grad_ffn_out, gain_three = norm_back(ffn_out, gains_float[3], grad_top)
    grad_ffn = grad_ffn_out.astype(jnp.bfloat16)
    grad_hidden = cols_product(grad_ffn, down_full)
    _, geglu_pull = jax.vjp(geglu, gate_up[:, 0], gate_up[:, 1])
    grad_gate, grad_up = geglu_pull(grad_hidden)
    grad_gate_up = (
        jnp.stack([grad_gate, grad_up], axis=1)
        .reshape(tok_rows, 2 * ffn_local)
        .astype(jnp.bfloat16)
    )
    grad_ffn_in = lax.psum(cols_product(grad_gate_up, gate_up_flat), "tensor")
    grad_mid_norm, gain_two = norm_back(mid_stream, gains_float[2], grad_ffn_in)
    grad_mid = grad_top + grad_mid_norm
    grad_attn_out, gain_one = norm_back(attn_out, gains_float[1], grad_mid)
    grad_attn = grad_attn_out.astype(jnp.bfloat16)
    grad_att = (
        cols_product(grad_attn, out_full)
        .astype(jnp.bfloat16)
        .reshape(tok_rows, kv_local, GROUP, HEAD_DIM)
    )
    capped_again = capped_scores(query_groups, ext_keys)
    probs_float = jnp.where(mask, jnp.exp(capped_again - log_sums[..., None]), 0.0)
    probs_again = probs_float.astype(jnp.bfloat16)
    delta = jnp.einsum("icgd,icgd->cgi", grad_att, attended, preferred_element_type=jnp.float32)
    grad_probs = jnp.einsum(
        "icgd,jcd->cgij", grad_att, ext_values, preferred_element_type=jnp.float32
    )
    grad_scores = (
        probs_float * (grad_probs - delta[..., None]) * (1.0 - (capped_again / soft_cap) ** 2)
    ).astype(jnp.bfloat16)
    score_scale = HEAD_DIM ** (-0.5)
    grad_values_ext = jnp.einsum(
        "cgij,icgd->jcd", probs_again, grad_att, preferred_element_type=jnp.float32
    )
    grad_keys_ext = (
        jnp.einsum("cgij,icgd->jcd", grad_scores, query_groups, preferred_element_type=jnp.float32)
        * score_scale
    )
    grad_queries = (
        jnp.einsum("cgij,jcd->icgd", grad_scores, ext_keys, preferred_element_type=jnp.float32)
        * score_scale
    )
    grad_pair_ext = jnp.stack([grad_keys_ext, grad_values_ext], axis=0)
    grad_pair = grad_pair_ext[:, WIN_BLOCKS * tok_rows :]
    for distance in range(1, reach + 1):
        start = (WIN_BLOCKS - distance) * tok_rows
        piece = grad_pair_ext[:, start : start + tok_rows]
        grad_pair = grad_pair + from_behind(piece.astype(jnp.bfloat16), "seq", -distance).astype(
            piece.dtype
        )
    grad_queries = rotate(
        grad_queries.reshape(tok_rows, heads_local, HEAD_DIM), cosine, -sine
    ).reshape(tok_rows, kv_local, GROUP, HEAD_DIM)
    grad_keys = rotate(grad_pair[0], cosine, -sine)
    grad_values = grad_pair[1]
    grad_proj = (
        jnp.concatenate([grad_queries, grad_keys[:, :, None], grad_values[:, :, None]], axis=2)
        .reshape(tok_rows, kv_local * (GROUP + 2) * HEAD_DIM)
        .astype(jnp.bfloat16)
    )
    grad_attn_in = lax.psum(
        cols_product(grad_proj, qkv_flat).astype(jnp.bfloat16), "tensor"
    ).astype(jnp.float32)
    grad_stream_norm, gain_zero = norm_back(stream, gains_float[0], grad_attn_in)
    input_grad = grad_mid + grad_stream_norm
    qkv_local = rows_product(attn_in, grad_proj).reshape(
        model_width, kv_local, (GROUP + 2) * HEAD_DIM
    )
    out_local = rows_product(att_flat, grad_attn)
    gate_up_local = rows_product(ffn_in, grad_gate_up).reshape(model_width, 2, ffn_local)
    down_local = rows_product(hidden, grad_ffn)
    gains_local = jnp.stack([gain_zero, gain_one, gain_two, gain_three])
    summed = (
        lax.psum_scatter(
            qkv_local.astype(jnp.bfloat16), ("batch", "seq"), scatter_dimension=0, tiled=True
        ).astype(jnp.float32),
        lax.psum_scatter(
            out_local.astype(jnp.bfloat16), ("batch", "seq"), scatter_dimension=1, tiled=True
        ).astype(jnp.float32),
        lax.psum_scatter(
            gate_up_local.astype(jnp.bfloat16), ("batch", "seq"), scatter_dimension=0, tiled=True
        ).astype(jnp.float32),
        lax.psum_scatter(
            down_local.astype(jnp.bfloat16), ("batch", "seq"), scatter_dimension=1, tiled=True
        ).astype(jnp.float32),
        lax.psum_scatter(
            gains_local.astype(jnp.bfloat16), ("batch", "seq"), scatter_dimension=1, tiled=True
        ).astype(jnp.float32),
    )
    qkv_grad, out_grad, gate_up_grad, down_grad, gains_grad = summed
    qkv_new, qkv_first_new, qkv_second_new = adam_step(
        qkv_weight, qkv_grad, qkv_first, qkv_second, decay_rate
    )
    out_new, out_first_new, out_second_new = adam_step(
        out_weight, out_grad, out_first, out_second, decay_rate
    )
    gate_up_new, gate_up_first_new, gate_up_second_new = adam_step(
        gate_up_weight, gate_up_grad, gate_up_first, gate_up_second, decay_rate
    )
    down_new, down_first_new, down_second_new = adam_step(
        down_weight, down_grad, down_first, down_second, decay_rate
    )
    gains_new, gains_first_new, gains_second_new = adam_step(
        norm_gains, gains_grad, gains_first, gains_second, 0.0
    )
    return (
        layer_out[None],
        input_grad[None],
        qkv_grad,
        out_grad,
        gate_up_grad,
        down_grad,
        gains_grad,
        qkv_new,
        out_new,
        gate_up_new,
        down_new,
        gains_new,
        qkv_first_new,
        out_first_new,
        gate_up_first_new,
        down_first_new,
        gains_first_new,
        qkv_second_new,
        out_second_new,
        gate_up_second_new,
        down_second_new,
        gains_second_new,
    )


def solution(mesh):
    in_specs = (
        P("batch", "seq", None),
        P("batch", "seq", None),
        P(("batch", "seq"), "tensor", None),
        P("tensor", ("batch", "seq")),
        P(("batch", "seq"), None, "tensor"),
        P("tensor", ("batch", "seq")),
        P(None, ("batch", "seq")),
        P(("batch", "seq"), "tensor", None),
        P("tensor", ("batch", "seq")),
        P(("batch", "seq"), None, "tensor"),
        P("tensor", ("batch", "seq")),
        P(None, ("batch", "seq")),
        P(("batch", "seq"), "tensor", None),
        P("tensor", ("batch", "seq")),
        P(("batch", "seq"), None, "tensor"),
        P("tensor", ("batch", "seq")),
        P(None, ("batch", "seq")),
    )
    out_specs = (
        P("batch", "seq", None),
        P("batch", "seq", None),
        P(("batch", "seq"), "tensor", None),
        P("tensor", ("batch", "seq")),
        P(("batch", "seq"), None, "tensor"),
        P("tensor", ("batch", "seq")),
        P(None, ("batch", "seq")),
        P(("batch", "seq"), "tensor", None),
        P("tensor", ("batch", "seq")),
        P(("batch", "seq"), None, "tensor"),
        P("tensor", ("batch", "seq")),
        P(None, ("batch", "seq")),
        P(("batch", "seq"), "tensor", None),
        P("tensor", ("batch", "seq")),
        P(("batch", "seq"), None, "tensor"),
        P("tensor", ("batch", "seq")),
        P(None, ("batch", "seq")),
        P(("batch", "seq"), "tensor", None),
        P("tensor", ("batch", "seq")),
        P(("batch", "seq"), None, "tensor"),
        P("tensor", ("batch", "seq")),
        P(None, ("batch", "seq")),
    )
    sizes = tuple(mesh.shape[axis] for axis in ("batch", "seq", "tensor"))
    body = on_square if sizes == (4, 2, 4) else on_device
    return jax.shard_map(
        body, mesh=mesh, in_specs=in_specs, out_specs=out_specs, check_vma=False
    )
```

```python
import functools
import jax
import jax.numpy as jnp
from jax import lax
from jax.experimental.layout import Layout, with_layout_constraint
from jax.experimental import pallas as pl
from jax.experimental.pallas import tpu as pltpu
from jax.sharding import PartitionSpec as P

HEAD_DIM = 256
WIN_BLOCKS = 4
STEP = 10
GROUP = 2


norm_eps = 1e-06
soft_cap = 50.0
learn_rate = 0.02
decay_rate = 0.1
beta_first = 0.9
beta_second = 0.95
adam_eps = 1e-08
gelu_coef = 0.7978845608028654


def from_behind(value, axis, steps):
    count = lax.axis_size(axis)
    initial, last = (max(0, -steps), min(count, count - steps))
    return lax.ppermute(value, axis, [(source, source + steps) for source in range(initial, last)])


def rms_norm(values, gain):
    scale = lax.rsqrt(jnp.mean(values * values, axis=-1, keepdims=True) + norm_eps)
    return values * scale * (1.0 + gain)


def norm_back(values, gain, upstream):
    _, pullback = jax.vjp(rms_norm, values, gain)
    return pullback(upstream)


def gelu_tanh(values):
    inner = gelu_coef * (values + 0.044715 * values * values * values)
    return 0.5 * values * (1.0 + jnp.tanh(inner))


def geglu(gate, up_part):
    return gelu_tanh(gate) * up_part


def rope_tables(positions, head_size):
    half = head_size // 2
    exponent = jnp.arange(half, dtype=jnp.float32) * (2.0 / head_size)
    freqs = 10000.0 ** (-exponent)
    angles = positions.astype(jnp.float32)[:, None] * freqs[None, :]
    return (jnp.cos(angles), jnp.sin(angles))


def rotate(values, cosine, sine):
    half = values.shape[-1] // 2
    first = values[..., :half]
    second = values[..., half:]
    cosine = cosine[:, None, :]
    sine = sine[:, None, :]
    return jnp.concatenate(
        [first * cosine - second * sine, second * cosine + first * sine], axis=-1
    )


def adam_step(weight, grad, first, second, decay):
    first_new = beta_first * first + (1.0 - beta_first) * grad
    second_new = beta_second * second + (1.0 - beta_second) * grad * grad
    first_hat = first_new / (1.0 - beta_first**STEP)
    second_hat = second_new / (1.0 - beta_second**STEP)
    weight_new = weight - learn_rate * (
        first_hat / (jnp.sqrt(second_hat) + adam_eps) + decay * weight
    )
    return (weight_new, first_new, second_new)


def rows_product(left, right):
    return lax.dot_general(
        left, right, (((0,), (0,)), ((), ())), preferred_element_type=jnp.float32
    )


def cols_product(left, right):
    return lax.dot_general(
        left, right, (((1,), (1,)), ((), ())), preferred_element_type=jnp.float32
    )


def capped_scores(query_groups, ext_keys):
    raw = jnp.einsum(
        "icgd,jcd->cgij", query_groups, ext_keys, preferred_element_type=jnp.float32
    ) * query_groups.shape[-1] ** (-0.5)
    return soft_cap * jnp.tanh(raw / soft_cap)


def tensor_sum(part):
    return lax.psum(part, "tensor")


def swap(value, axis, bit):
    count = lax.axis_size(axis)
    return lax.ppermute(value, axis, [(source, source ^ bit) for source in range(count)])


def after(value, *earlier):
    return lax.optimization_barrier((value, earlier))[0]


def trade(value, turn):
    pairs = []
    for chip in range(4):
        for core in range(2):
            pairs.append((chip * 2 + core, (chip ^ (1 + (core ^ turn))) * 2 + core))
    return lax.ppermute(value, ("batch", "seq"), pairs)


def offsets(owner):
    return (0, 1 + owner, 2 - owner, 3)


def own_blocks(wide):
    tokens, width = wide.shape
    chip, core = lax.axis_index("batch"), lax.axis_index("seq")
    split = wide.reshape(tokens, 8, width // 8)
    halves = []
    for owner in (core, 1 - core):
        parts = [
            lax.dynamic_index_in_dim(split, (chip ^ offset) * 2 + owner, 1, keepdims=False)
            for offset in offsets(owner)
        ]
        halves.append(jnp.concatenate(parts, axis=1))
    return halves


def both_cores(wide):
    mine, theirs = own_blocks(wide)
    return jnp.concatenate([mine, swap(theirs, "seq", 1)], axis=0)


def weight_local(wide, narrow):
    local = rows_product(wide, narrow).astype(jnp.bfloat16)
    return local.reshape(4, -1, local.shape[1])


def scatter_begin(local):
    got = trade(jnp.stack([local[1], local[3]]), 0)
    far = local[2].astype(jnp.float32) + got[1].astype(jnp.float32)
    return local[0], got[0], far.astype(jnp.bfloat16)


def scatter_end(state):
    own, got, far = state
    return own, got, trade(far, 1)


def everywhere_sum(value):
    for axis, bit in (("seq", 1), ("batch", 1), ("batch", 2), ("tensor", 1), ("tensor", 2)):
        value = value + swap(value, axis, bit)
    return value


FFN_TILE = 768
ROW_CHUNK = 16
ROW_UNROLL = 4
MID_ROWS = 128


def spec_any():
    return pl.BlockSpec(memory_space=pl.ANY)


def spec_vmem():
    return pl.BlockSpec(memory_space=pltpu.VMEM)


def spec_smem():
    return pl.BlockSpec(memory_space=pltpu.SMEM)


def kernel_params():
    return pltpu.CompilerParams(vmem_limit_bytes=56 * 1024 * 1024)


def cost(flops, moved):
    return pl.CostEstimate(flops=flops, bytes_accessed=moved, transcendentals=0)


def shaped(shape, kind):
    return jax.ShapeDtypeStruct(shape, kind)


def dot_nn(left, right):
    return lax.dot_general(
        left, right, (((1,), (0,)), ((), ())), preferred_element_type=jnp.float32
    )


def dot_nt(left, right):
    return lax.dot_general(
        left, right, (((1,), (1,)), ((), ())), preferred_element_type=jnp.float32
    )


def dot_tn(left, right):
    return lax.dot_general(
        left, right, (((0,), (0,)), ((), ())), preferred_element_type=jnp.float32
    )


def row_scale(values):
    return lax.rsqrt(jnp.mean(values * values, axis=-1, keepdims=True) + norm_eps)


def norm_pull(values, scale, gain, upstream):
    normed = values * scale
    inner = upstream * (1.0 + gain)
    pulled = scale * (inner - normed * jnp.mean(normed * inner, axis=-1, keepdims=True))
    return pulled, upstream * normed


def fold_rows(values):
    total = values[:8]
    for start in range(8, values.shape[0], 8):
        total += values[start : start + 8]
    return total


def fetch_rows(place, near, far, target, sems, column, columns):
    chip, core = place[0], place[1]
    rows = near[0].shape[1]
    copies = []
    for which, (one, two) in enumerate((near, far)):
        owner = which ^ core
        blocks = ((one.at[0], 0), (one.at[1], 1 + owner), (two.at[0], 2 - owner), (two.at[1], 3))
        for block, offset in blocks:
            row = ((offset ^ chip) * 2 + owner) * rows
            copies.append(
                pltpu.make_async_copy(
                    block.at[:, pl.ds(column, columns)],
                    target.at[pl.ds(pl.multiple_of(row, 16), rows), :],
                    sems.at[len(copies)],
                )
            )
    return copies


def rope(values, cosine, sine):
    half = HEAD_DIM // 2
    first, second = values[:, :half], values[:, half:]
    return jnp.concatenate(
        [first * cosine - second * sine, second * cosine + first * sine], axis=1
    )


def arrange_kernel(place, one, two, one_far, two_far, result, sems):
    copies = fetch_rows(place, (one, two), (one_far, two_far), result, sems, 0, result.shape[1])
    for copy in copies:
        copy.start()
    for copy in copies:
        copy.wait()


def arrange(place, near, far):
    return pl.pallas_call(
        arrange_kernel,
        in_specs=[spec_smem()] + [spec_any()] * 4,
        out_specs=spec_vmem(),
        out_shape=shaped((8 * near[0].shape[1], near[0].shape[2]), jnp.bfloat16),
        scratch_shapes=[pltpu.SemaphoreType.DMA((8,))],
        compiler_params=kernel_params(),
        cost_estimate=cost(0, 16 * near[0].size),
        name="arrange",
    )(place, *near, *far)


def project_kernel(place, x, one, two, one_far, two_far, cosine, sine, *rest):
    queries, pair, attn_in, gains, weight, sems = rest[-6:]
    copies = fetch_rows(place, (one, two), (one_far, two_far), weight, sems, 0, weight.shape[1])
    for copy in copies:
        copy.start()
    for copy in copies:
        copy.wait()
    width = (GROUP + 2) * HEAD_DIM
    tail = weight[:, width + GROUP * HEAD_DIM :].astype(jnp.float32)
    gains[...] = jnp.transpose(tail)[:8]
    gain = 1.0 + gains[0:1, :]
    chunk = ROW_CHUNK

    @pl.loop(0, x.shape[0] // chunk, unroll=ROW_UNROLL)
    def _(step):
        rows = pl.ds(pl.multiple_of(step * chunk, chunk), chunk)
        stream = x[rows, :].astype(jnp.float32)
        attn_in[rows, :] = (stream * row_scale(stream) * gain).astype(jnp.bfloat16)

    for member in range(GROUP + 2):
        columns = slice(member * HEAD_DIM, (member + 1) * HEAD_DIM)
        part = dot_nn(attn_in[...], weight[:, columns])
        if member < GROUP:
            queries[:, columns] = rope(part, cosine[...], sine[...]).astype(jnp.bfloat16)
        elif member == GROUP:
            pair[0] = rope(part, cosine[...], sine[...]).astype(jnp.bfloat16)
        else:
            pair[1] = part.astype(jnp.bfloat16)


def project(place, x, near, far, cosine, sine, *earlier):
    tokens, width = x.shape
    bf16 = jnp.bfloat16
    return pl.pallas_call(
        project_kernel,
        in_specs=[spec_smem(), spec_vmem()]
        + [spec_any()] * 4
        + [spec_vmem()] * 2
        + [spec_any()] * len(earlier),
        out_specs=[spec_vmem()] * 4,
        out_shape=[
            shaped((tokens, GROUP * HEAD_DIM), bf16),
            shaped((2, tokens, HEAD_DIM), bf16),
            shaped((tokens, width), bf16),
            shaped((8, width), jnp.float32),
        ],
        scratch_shapes=[pltpu.VMEM((width, near[0].shape[2]), bf16), pltpu.SemaphoreType.DMA((8,))],
        compiler_params=kernel_params(),
        cost_estimate=cost(2 * tokens * width * 1024, 12_000_000),
        name="project",
    )(place, x, *near, *far, cosine, sine, *earlier)


def chunk_scores(query, key, behind, row, core):
    raw = dot_nt(query, key) * (HEAD_DIM**-0.5 / soft_cap)
    bent = jnp.tanh(raw)
    powers = jnp.exp(soft_cap * bent)
    if behind:
        powers = jnp.where(core > 0, powers, 0.0)
    else:
        at = row + lax.broadcasted_iota(jnp.int32, powers.shape, 0)
        powers = jnp.where(at >= lax.broadcasted_iota(jnp.int32, powers.shape, 1), powers, 0.0)
    return bent, powers


def attend_kernel(place, queries, pair, behind, one, two, one_far, two_far, *rest):
    attended, result, weight, sems = rest[-4:]
    width = (GROUP + 2) * HEAD_DIM
    copies = fetch_rows(place, (one, two), (one_far, two_far), weight, sems, width, GROUP * HEAD_DIM)
    for copy in copies:
        copy.start()
    core = place[1]
    chunk = 128
    tokens = queries.shape[0]
    for start in range(0, tokens, chunk):
        rows = slice(start, start + chunk)
        keys = start + chunk
        for head in range(GROUP):
            columns = slice(head * HEAD_DIM, (head + 1) * HEAD_DIM)
            query = queries[rows, columns]
            _, old = chunk_scores(query, behind[0], True, start, core)
            _, new = chunk_scores(query, pair[0, :keys], False, start, core)
            total = jnp.sum(old, axis=-1, keepdims=True) + jnp.sum(new, axis=-1, keepdims=True)
            share = 1.0 / total
            value = dot_nn((old * share).astype(jnp.bfloat16), behind[1])
            value += dot_nn((new * share).astype(jnp.bfloat16), pair[1, :keys])
            attended[rows, columns] = value.astype(jnp.bfloat16)
    for copy in copies:
        copy.wait()
    tile = 768
    for column in range(0, result.shape[1], tile):
        part = dot_nt(attended[...], weight[column : column + tile, :])
        result[:, column : column + tile] = part.astype(jnp.bfloat16)


def attend(place, queries, pair, behind, near, far, width, *earlier):
    tokens = queries.shape[0]
    bf16 = jnp.bfloat16
    return pl.pallas_call(
        attend_kernel,
        in_specs=[spec_smem()] + [spec_vmem()] * 3 + [spec_any()] * (4 + len(earlier)),
        out_specs=[spec_vmem()] * 2,
        out_shape=[shaped((tokens, GROUP * HEAD_DIM), bf16), shaped((tokens, width), bf16)],
        scratch_shapes=[
            pltpu.VMEM((width, GROUP * HEAD_DIM), bf16),
            pltpu.SemaphoreType.DMA((8,)),
        ],
        compiler_params=kernel_params(),
        cost_estimate=cost(4 * tokens * width * 1024, 8_000_000),
        name="attend",
    )(place, queries, pair, behind, *near, *far, *earlier)


def whole(shape):
    return pl.BlockSpec(shape, lambda *_: (0,) * len(shape))


def ffn_params():
    return pltpu.CompilerParams(vmem_limit_bytes=58 * 1024 * 1024)


def move(source, target, sem):
    copy = pltpu.make_async_copy(source, target, sem)
    copy.start()
    return copy


def ffn_kernel(place, attn_out, x, gains, up_full, *rest):
    gate_near, gate_far, down_near, down_far = (rest[k : k + 2] for k in (0, 2, 4, 6))
    outs, (sides, gate_up_here, down_here, in_sems, down_sems, out_sems) = rest[-11:-6], rest[-6:]
    ffn_in, hidden, by_gate, by_up, result = (sides.at[k] for k in range(5))
    tokens, width = x.shape
    units = up_full.shape[1]
    tile = FFN_TILE
    steps, turns = units // tile, width // tile

    def load(step):
        columns = pl.ds(pl.multiple_of(step * tile, tile), tile)
        up_copy = pltpu.make_async_copy(
            up_full.at[:, columns], gate_up_here.at[1, :, columns], in_sems.at[step, 8]
        )
        target = gate_up_here.at[0, :, columns]
        return [up_copy] + fetch_rows(
            place, gate_near, gate_far, target, in_sems.at[step], columns.start, tile
        )

    down_copies = fetch_rows(place, down_near, down_far, down_here, down_sems, 0, units)
    for step in range(steps):
        for copy in load(step):
            copy.start()
    for copy in down_copies:
        copy.start()
    chunk = ROW_CHUNK

    @pl.loop(0, tokens // chunk, unroll=ROW_UNROLL)
    def _(step):
        rows = pl.ds(pl.multiple_of(step * chunk, chunk), chunk)
        out = attn_out[rows, :].astype(jnp.float32)
        mid = x[rows, :].astype(jnp.float32) + out * row_scale(out) * (1.0 + gains[1:2, :])
        ffn_in[rows, :] = (mid * row_scale(mid) * (1.0 + gains[2:3, :])).astype(jnp.bfloat16)

    stores = [move(ffn_in, outs[0], out_sems.at[0])]

    @pl.loop(0, steps)
    def _(step):
        for copy in load(step):
            copy.wait()
        columns = pl.ds(pl.multiple_of(step * tile, tile), tile)
        for rows in (slice(None),):
            value = ffn_in[...]
            gate = dot_nn(value, gate_up_here[0, :, columns])
            up = dot_nn(value, gate_up_here[1, :, columns])
            square_of = gate * gate
            bent = jnp.tanh(gate * (gelu_coef + gelu_coef * 0.044715 * square_of))
            half = 0.5 + 0.5 * bent
            curve = gate * half
            slope = half + curve * (1.0 - bent) * (
                gelu_coef + 3.0 * gelu_coef * 0.044715 * square_of
            )
            hidden[rows, columns] = (curve * up).astype(jnp.bfloat16)
            by_gate[rows, columns] = (slope * up).astype(jnp.bfloat16)
            by_up[rows, columns] = curve.astype(jnp.bfloat16)

    for k, side in ((1, hidden), (2, by_gate), (3, by_up)):
        stores.append(move(side, outs[k], out_sems.at[k]))

    def store(turn):
        columns = pl.ds(pl.multiple_of(turn * tile, tile), tile)
        return pltpu.make_async_copy(
            result.at[:, columns], outs[4].at[:, columns], out_sems.at[4 + turn]
        )

    for copy in down_copies:
        copy.wait()

    @pl.loop(0, turns)
    def _(turn):
        rows = pl.ds(pl.multiple_of(turn * tile, tile), tile)
        result[:, rows] = dot_nt(hidden[...], down_here[rows, :]).astype(jnp.bfloat16)
        store(turn).start()

    for copy in stores:
        copy.wait()
    for turn in range(turns):
        store(turn).wait()


def ffn_forward(place, attn_out, x, gains, up, gate, down):
    tokens, width = x.shape
    units = up.shape[1]
    bf16 = jnp.bfloat16
    return pl.pallas_call(
        ffn_kernel,
        in_specs=[spec_smem()] + [spec_vmem()] * 3 + [spec_any()] * 9,
        out_specs=[spec_any()] * 5,
        out_shape=[shaped((tokens, width), bf16)]
        + [shaped((tokens, units), bf16)] * 3
        + [shaped((tokens, width), bf16)],
        scratch_shapes=[
            pltpu.VMEM((5, tokens, width), bf16),
            pltpu.VMEM((2, width, units), bf16),
            pltpu.VMEM((width, units), bf16),
            pltpu.SemaphoreType.DMA((units // FFN_TILE, 9)),
            pltpu.SemaphoreType.DMA((8,)),
            pltpu.SemaphoreType.DMA((4 + width // FFN_TILE,)),
        ],
        compiler_params=ffn_params(),
        cost_estimate=cost(6 * tokens * width * units, 50_000_000),
        name="ffn_forward",
    )(place, attn_out, x, gains, up, *gate[0], *gate[1], *down[0], *down[1])


def ffn_back_kernel(ffn_out, top, gains, gate, up_full, down, by_gate, by_up, *rest):
    grad_out, gate_out, up_out, gain_out, result_out = rest[-13:-8]
    sides, grads, gate_up_here, down_here, in_sems, down_sems, gate_sems, out_sems = rest[-8:]
    grad_ffn, result = sides.at[0], sides.at[1]
    tokens, width = top.shape
    units = gate.shape[1]
    grad_gate, grad_up = grads.at[:, pl.ds(0, units)], grads.at[:, pl.ds(units, units)]
    tile = FFN_TILE
    steps, turns = units // tile, width // tile

    def load_down(step):
        columns = pl.ds(pl.multiple_of(step * tile, tile), tile)
        return pltpu.make_async_copy(
            down.at[:, columns], down_here.at[:, columns], down_sems.at[step]
        )

    def load(turn, which):
        rows = pl.ds(pl.multiple_of(turn * tile, tile), tile)
        return pltpu.make_async_copy(
            (gate, up_full)[which].at[rows, :],
            gate_up_here.at[rows, pl.ds(which * units, units)],
            gate_sems.at[turn, which],
        )

    load_down(0).start()
    factors = [
        move(by_gate, grad_gate, in_sems.at[0]),
        move(by_up, grad_up, in_sems.at[1]),
    ]
    load_down(1).start()
    gain_out[...] = jnp.zeros_like(gain_out)
    chunk = ROW_CHUNK

    @pl.loop(0, tokens // chunk, unroll=ROW_UNROLL)
    def _(step):
        rows = pl.ds(pl.multiple_of(step * chunk, chunk), chunk)
        out = ffn_out[rows, :].astype(jnp.float32)
        upstream = top[rows, :].astype(jnp.float32)
        pulled, product = norm_pull(out, row_scale(out), gains[3:4, :], upstream)
        grad_ffn[rows, :] = pulled.astype(jnp.bfloat16)
        gain_out[...] += fold_rows(product)

    stores = [move(grad_ffn, grad_out, out_sems.at[0])]
    for copy in factors:
        copy.wait()

    @pl.loop(0, steps)
    def _(step):
        load_down(step).wait()

        @pl.when(step + 2 < steps)
        def _():
            load_down(step + 2).start()

        @pl.when(step + 2 >= steps)
        def _():
            load(step + 2 - steps, 0).start()
            load(step + 2 - steps, 1).start()

        columns = pl.ds(pl.multiple_of(step * tile, tile), tile)
        for start in range(0, tokens, tokens // 2):
            rows = pl.ds(start, tokens // 2)
            grad_hidden = dot_nn(grad_ffn[rows, :], down_here[:, columns])
            one = grad_hidden * grad_gate[rows, columns].astype(jnp.float32)
            two = grad_hidden * grad_up[rows, columns].astype(jnp.float32)
            grad_gate[rows, columns] = one.astype(jnp.bfloat16)
            grad_up[rows, columns] = two.astype(jnp.bfloat16)

    stores.append(move(grad_gate, gate_out, out_sems.at[1]))
    stores.append(move(grad_up, up_out, out_sems.at[2]))

    def store(turn):
        columns = pl.ds(pl.multiple_of(turn * tile, tile), tile)
        return pltpu.make_async_copy(
            result.at[:, columns], result_out.at[:, columns], out_sems.at[3 + turn]
        )

    @pl.loop(0, turns)
    def _(turn):
        load(turn, 0).wait()
        load(turn, 1).wait()

        @pl.when(turn + 2 < turns)
        def _():
            load(turn + 2, 0).start()
            load(turn + 2, 1).start()

        rows = pl.ds(pl.multiple_of(turn * tile, tile), tile)
        part = dot_nt(grads[...], gate_up_here[rows, :])
        result[:, rows] = part.astype(jnp.bfloat16)
        store(turn).start()

    for copy in stores:
        copy.wait()
    for turn in range(turns):
        store(turn).wait()


def ffn_back(ffn_out, top, gains, gate, up, down, by_gate, by_up, *earlier):
    tokens, width = top.shape
    units = by_up.shape[1]
    bf16 = jnp.bfloat16
    return pl.pallas_call(
        ffn_back_kernel,
        in_specs=[spec_vmem()] * 3 + [spec_any()] * (5 + len(earlier)),
        out_specs=[spec_any()] * 3 + [spec_vmem(), spec_any()],
        out_shape=[
            shaped((tokens, width), bf16),
            shaped((tokens, units), bf16),
            shaped((tokens, units), bf16),
            shaped((8, width), jnp.float32),
            shaped((tokens, width), bf16),
        ],
        scratch_shapes=[
            pltpu.VMEM((2, tokens, width), bf16),
            pltpu.VMEM((tokens, 2 * units), bf16),
            pltpu.VMEM((width, 2 * units), bf16),
            pltpu.VMEM((width, units), bf16),
            pltpu.SemaphoreType.DMA((2,)),
            pltpu.SemaphoreType.DMA((units // FFN_TILE,)),
            pltpu.SemaphoreType.DMA((width // FFN_TILE, 2)),
            pltpu.SemaphoreType.DMA((3 + width // FFN_TILE,)),
        ],
        compiler_params=ffn_params(),
        cost_estimate=cost(6 * tokens * width * units, 55_000_000),
        name="ffn_back",
    )(ffn_out, top, gains, gate, up, down, by_gate, by_up, *earlier)


def mid_back_kernel(place, grad_in, x, attn_out, top, gains, one, two, one_far, two_far, *rest):
    grad_mid, grad_attn, grad_att, gain_out, weight, sems = rest[-6:]
    width = (GROUP + 2) * HEAD_DIM
    first = pl.program_id(0) == 0

    def fetch():
        return fetch_rows(place, (one, two), (one_far, two_far), weight, sems, width, GROUP * HEAD_DIM)

    @pl.when(first)
    def _():
        gain_out[...] = jnp.zeros_like(gain_out)
        for copy in fetch():
            copy.start()

    chunk = ROW_CHUNK

    @pl.loop(0, x.shape[0] // chunk, unroll=ROW_UNROLL)
    def _(step):
        rows = pl.ds(pl.multiple_of(step * chunk, chunk), chunk)
        out = attn_out[rows, :].astype(jnp.float32)
        out_scale = row_scale(out)
        mid = x[rows, :].astype(jnp.float32) + out * out_scale * (1.0 + gains[1:2, :])
        upstream = grad_in[rows, :].astype(jnp.float32)
        pulled, product = norm_pull(mid, row_scale(mid), gains[2:3, :], upstream)
        gain_out[1] += fold_rows(product)
        at_mid = top[rows, :].astype(jnp.float32) + pulled
        grad_mid[rows, :] = at_mid
        pulled, product = norm_pull(out, out_scale, gains[1:2, :], at_mid)
        gain_out[0] += fold_rows(product)
        grad_attn[rows, :] = pulled.astype(jnp.bfloat16)

    @pl.when(first)
    def _():
        for copy in fetch():
            copy.wait()

    grad_att[...] = dot_nn(grad_attn[...], weight[...]).astype(jnp.bfloat16)


def mid_back(place, grad_in, x, attn_out, top, gains, near, far, *earlier):
    tokens, width = x.shape
    heads = GROUP * HEAD_DIM
    bf16 = jnp.bfloat16
    rows = pl.BlockSpec((MID_ROWS, width), lambda i: (i, 0))
    return pl.pallas_call(
        mid_back_kernel,
        grid=(tokens // MID_ROWS,),
        in_specs=[spec_smem()]
        + [rows] * 4
        + [whole((8, width))]
        + [spec_any()] * (4 + len(earlier)),
        out_specs=[
            rows,
            rows,
            pl.BlockSpec((MID_ROWS, heads), lambda i: (i, 0)),
            whole((2, 8, width)),
        ],
        out_shape=[
            shaped((tokens, width), jnp.float32),
            shaped((tokens, width), bf16),
            shaped((tokens, heads), bf16),
            shaped((2, 8, width), jnp.float32),
        ],
        scratch_shapes=[pltpu.VMEM((width, heads), bf16), pltpu.SemaphoreType.DMA((8,))],
        compiler_params=kernel_params(),
        cost_estimate=cost(2 * tokens * width * heads, 24_000_000),
        name="mid_back",
    )(place, grad_in, x, attn_out, top, gains, *near, *far, *earlier)


def attend_back_kernel(
    place, queries, pair, behind, attended, grad_att, cosine, sine, *rest
):
    grad_q, grad_own, grad_old, sums = rest[-4:]
    core = place[1]
    chunk = 128
    tokens = queries.shape[0]
    scale = HEAD_DIM**-0.5
    sums[...] = jnp.zeros_like(sums)
    for start in range(0, tokens, chunk):
        rows = slice(start, start + chunk)
        keys = start + chunk
        cos, sin = cosine[rows, :], sine[rows, :]
        for head in range(GROUP):
            columns = slice(head * HEAD_DIM, (head + 1) * HEAD_DIM)
            query, upstream = queries[rows, columns], grad_att[rows, columns]
            delta = jnp.sum(
                upstream.astype(jnp.float32) * attended[rows, columns].astype(jnp.float32),
                axis=-1,
                keepdims=True,
            )
            bent_old, old = chunk_scores(query, behind[0], True, start, core)
            bent_new, new = chunk_scores(query, pair[0, :keys], False, start, core)
            share = 1.0 / (
                jnp.sum(old, axis=-1, keepdims=True) + jnp.sum(new, axis=-1, keepdims=True)
            )
            total = jnp.zeros((chunk, HEAD_DIM), jnp.float32)
            for bent, powers, block, end, base in (
                (bent_old, old, behind, tokens, 0),
                (bent_new, new, pair, keys, 2),
            ):
                prob = powers * share
                grad_p = dot_nt(upstream, block[1, :end])
                grad_s = (prob * (grad_p - delta) * (1.0 - bent * bent)).astype(jnp.bfloat16)
                total += dot_nn(grad_s, block[0, :end])
                sums[base, :end, :] += dot_tn(grad_s, query)
                sums[base + 1, :end, :] += dot_tn(prob.astype(jnp.bfloat16), upstream)
            grad_q[rows, columns] = rope(total * scale, cos, -sin).astype(jnp.bfloat16)
    grad_old[0] = (sums[0] * scale).astype(jnp.bfloat16)
    grad_old[1] = sums[1].astype(jnp.bfloat16)
    grad_own[0] = sums[2] * scale
    grad_own[1] = sums[3]


def attend_back(place, queries, pair, behind, attended, grad_att, cosine, sine, *earlier):
    tokens, heads = queries.shape
    bf16 = jnp.bfloat16
    return pl.pallas_call(
        attend_back_kernel,
        in_specs=[spec_smem()] + [spec_vmem()] * 7 + [spec_any()] * len(earlier),
        out_specs=[spec_vmem()] * 3,
        out_shape=[
            shaped((tokens, heads), bf16),
            shaped((2, tokens, HEAD_DIM), jnp.float32),
            shaped((2, tokens, HEAD_DIM), bf16),
        ],
        scratch_shapes=[pltpu.VMEM((4, tokens, HEAD_DIM), jnp.float32)],
        compiler_params=kernel_params(),
        cost_estimate=cost(20 * tokens * 1024 * heads, 5_000_000),
        name="attend_back",
    )(place, queries, pair, behind, attended, grad_att, cosine, sine, *earlier)


def project_back_kernel(
    place, grad_q, grad_own, grad_ahead, cosine, sine, x, one, two, one_far, two_far, *rest
):
    proj, result, gain_out, weight, sems = rest[-5:]
    width = (GROUP + 2) * HEAD_DIM
    copies = fetch_rows(place, (one, two), (one_far, two_far), weight, sems, 0, width)
    for copy in copies:
        copy.start()
    heads = GROUP * HEAD_DIM
    proj[:, :heads] = grad_q[...]
    grad_key = grad_own[0] + grad_ahead[0].astype(jnp.float32)
    proj[:, heads : heads + HEAD_DIM] = rope(grad_key, cosine[...], -sine[...]).astype(jnp.bfloat16)
    proj[:, heads + HEAD_DIM :] = (grad_own[1] + grad_ahead[1].astype(jnp.float32)).astype(
        jnp.bfloat16
    )
    gain_out[...] = jnp.zeros_like(gain_out)
    for copy in copies:
        copy.wait()
    tile = 768
    for column in range(0, result.shape[1], tile):
        part = dot_nt(proj[...], weight[column : column + tile, :])
        result[:, column : column + tile] = part.astype(jnp.bfloat16)
    chunk = ROW_CHUNK

    @pl.loop(0, x.shape[0] // chunk, unroll=ROW_UNROLL)
    def _(step):
        rows = pl.ds(pl.multiple_of(step * chunk, chunk), chunk)
        stream = x[rows, :].astype(jnp.float32)
        product = result[rows, :].astype(jnp.float32) * (stream * row_scale(stream))
        gain_out[...] += fold_rows(product)


def project_back(place, grad_q, grad_own, grad_ahead, cosine, sine, x, near, far, *earlier):
    tokens, width = x.shape
    proj_width = (GROUP + 2) * HEAD_DIM
    bf16 = jnp.bfloat16
    return pl.pallas_call(
        project_back_kernel,
        in_specs=[spec_smem()]
        + [spec_vmem()] * 6
        + [spec_any()] * 4
        + [spec_any()] * len(earlier),
        out_specs=[spec_vmem()] * 3,
        out_shape=[
            shaped((tokens, proj_width), bf16),
            shaped((tokens, width), bf16),
            shaped((8, width), jnp.float32),
        ],
        scratch_shapes=[pltpu.VMEM((width, proj_width), bf16), pltpu.SemaphoreType.DMA((8,))],
        compiler_params=kernel_params(),
        cost_estimate=cost(2 * tokens * width * proj_width, 14_000_000),
        name="project_back",
    )(place, grad_q, grad_own, grad_ahead, cosine, sine, x, *near, *far, *earlier)


def stream_back_kernel(grad_in, x, gains, grad_mid, *rest):
    result = rest[-1]
    chunk = ROW_CHUNK

    @pl.loop(0, x.shape[0] // chunk, unroll=ROW_UNROLL)
    def _(step):
        rows = pl.ds(pl.multiple_of(step * chunk, chunk), chunk)
        stream = x[rows, :].astype(jnp.float32)
        upstream = grad_in[rows, :].astype(jnp.float32)
        pulled, _ = norm_pull(stream, row_scale(stream), gains[0:1, :], upstream)
        result[rows, :] = grad_mid[rows, :] + pulled


def stream_back(grad_in, x, gains, grad_mid, *earlier):
    tokens, width = x.shape
    tile = MID_ROWS
    rows = pl.BlockSpec((tile, width), lambda i: (i, 0))
    return pl.pallas_call(
        stream_back_kernel,
        grid=(tokens // tile,),
        in_specs=[rows, rows, whole((8, width)), rows] + [spec_any()] * len(earlier),
        out_specs=rows,
        out_shape=shaped((tokens, width), jnp.float32),
        compiler_params=kernel_params(),
        cost_estimate=cost(20 * tokens * width, 14_000_000),
        name="stream_back",
    )(grad_in, x, gains, grad_mid, *earlier)


def flat(values):
    rows, pair, width = values.shape
    lanes = width // 128
    if pair == 1:
        return values.reshape(rows * lanes, 128)
    tiles = with_layout_constraint(
        values.reshape(rows, pair, lanes, 128), Layout(major_to_minor=(0, 2, 1, 3))
    )
    return tiles.transpose(0, 2, 1, 3).reshape(rows * pair * lanes, 128)


def unflat(values, shape):
    rows, pair, width = shape
    lanes = width // 128
    if pair == 1:
        return values.reshape(shape)
    tiles = values.reshape(rows, lanes, pair, 128).transpose(0, 2, 1, 3)
    return with_layout_constraint(tiles, Layout(major_to_minor=(0, 2, 1, 3))).reshape(shape)


def join_kernel(*refs):
    result = refs[-1]
    for which in range(2):
        own, got, far = (refs[which * 3 + k][...].astype(jnp.float32) for k in range(3))
        result[:, which, :] = own + got + far


def join(gate, up):
    rows, width = gate[0].shape
    tile = 32
    block = pl.BlockSpec((tile, width), lambda i: (i, 0))
    return pl.pallas_call(
        join_kernel,
        grid=(rows // tile,),
        in_specs=[block] * 6,
        out_specs=pl.BlockSpec((tile, 2, width), lambda i: (i, 0, 0)),
        out_shape=shaped((rows, 2, width), jnp.float32),
        compiler_params=kernel_params(),
        cost_estimate=cost(0, 200_000_000),
        name="join",
    )(*gate, *up)


def adam_kernel(parts, decay, *refs):
    weight, first, second = (ref[...] for ref in refs[parts : parts + 3])
    outs = refs[parts + 3 :]
    grad = refs[0][...].astype(jnp.float32)
    for ref in refs[1:parts]:
        grad += ref[...].astype(jnp.float32)
    if parts > 1:
        outs[-1][...] = grad
    outs[0][...], outs[1][...], outs[2][...] = adam_step(weight, grad, first, second, decay)


def adam(grads, weight, first, second, decay):
    rows, width = weight.shape
    tile = rows // 9
    block = pl.BlockSpec((tile, width), lambda i: (i, 0))
    count = 3 if len(grads) == 1 else 4
    return pl.pallas_call(
        functools.partial(adam_kernel, len(grads), decay),
        grid=(9,),
        in_specs=[block] * (len(grads) + 3),
        out_specs=[block] * count,
        out_shape=[shaped((rows, width), jnp.float32)] * count,
        compiler_params=kernel_params(),
        cost_estimate=cost(0, 200_000_000),
        name="adam",
    )(*grads, weight, first, second)


def on_square(
    layer_in,
    cotangent,
    qkv_weight,
    out_weight,
    gate_up_weight,
    down_weight,
    norm_gains,
    qkv_first,
    out_first,
    gate_up_first,
    down_first,
    gains_first,
    qkv_second,
    out_second,
    gate_up_second,
    down_second,
    gains_second,
):
    tok_rows = layer_in.shape[1]
    chip, core = lax.axis_index("batch"), lax.axis_index("seq")
    place = jnp.stack([chip, core]).astype(jnp.int32)
    plane = ("batch", "seq")
    stream, top = layer_in[0], cotangent[0]
    gains_cast = jnp.pad(norm_gains.T, ((0, 0), (0, 128 - norm_gains.shape[0])))
    attn_cast = jnp.concatenate([qkv_weight[:, 0], out_weight.T, gains_cast], axis=1)
    gate_cast = gate_up_weight[:, 0].astype(jnp.bfloat16)
    up_cast = gate_up_weight[:, 1].astype(jnp.bfloat16)
    down_cast = down_weight.T.astype(jnp.bfloat16)
    attn_cast = attn_cast.astype(jnp.bfloat16)
    first, gate_cast, up_cast, down_cast = lax.optimization_barrier(
        (trade(attn_cast, 0), gate_cast, up_cast, down_cast)
    )
    attn_pair = jnp.stack([attn_cast, first])
    near = (attn_pair, trade(attn_pair, 1))
    far = tuple(swap(part, "seq", 1) for part in near)
    down_one = trade(down_cast, 0)
    gate_one = trade(gate_cast, 0)
    down_pair, gate_pair = jnp.stack([down_cast, down_one]), jnp.stack([gate_cast, gate_one])
    down_pair_far, gate_pair_far = swap(down_pair, "seq", 1), swap(gate_pair, "seq", 1)
    down_two = trade(down_pair, 1)
    gate_two = trade(after(gate_pair, down_pair_far, gate_pair_far), 1)
    down_parts = (down_pair, down_two), (down_pair_far, swap(down_two, "seq", 1))
    gate_parts = (gate_pair, gate_two), (gate_pair_far, swap(gate_two, "seq", 1))
    up = lax.all_gather(up_cast, plane, axis=0, tiled=True)
    positions = core * tok_rows + jnp.arange(tok_rows, dtype=jnp.int32)
    cosine, sine = rope_tables(positions, HEAD_DIM)

    queries, pair, attn_in, gains = project(
        place, stream, near, far, cosine, sine, up_cast
    )
    behind = from_behind(pair, "seq", 1)
    attended, attn_part = attend(
        place, queries, pair, behind, near, far, stream.shape[1], down_one, gate_one
    )
    attn_out = tensor_sum(attn_part)
    ffn_in, hidden, by_gate, by_up, ffn_part = ffn_forward(
        place, attn_out, stream, gains, up, gate_parts, down_parts
    )
    ffn_out = tensor_sum(ffn_part)

    gate = arrange(place, *gate_parts)
    down = arrange(place, *down_parts)
    att_both = jnp.concatenate([attended, swap(attended, "seq", 1)], axis=0)
    attn_in_both = both_cores(attn_in)
    ffn_in_both = both_cores(ffn_in)
    hidden_both = jnp.concatenate([hidden, swap(hidden, "seq", 1)], axis=0)
    grad_ffn, grad_gate, grad_up, gain_ffn, grad_ffn_part = ffn_back(
        ffn_out, top, gains, gate, up, down, by_gate, by_up, att_both, attn_in_both, ffn_in_both,
        hidden_both
    )
    grad_ffn_in = tensor_sum(grad_ffn_part)
    grad_gate_both = jnp.concatenate([grad_gate, swap(grad_gate, "seq", 1)], axis=0)
    grad_up_both = jnp.concatenate([grad_up, swap(grad_up, "seq", 1)], axis=0)
    down_local = weight_local(both_cores(grad_ffn), hidden_both)
    gate_local = weight_local(ffn_in_both, grad_gate_both)
    up_local = weight_local(ffn_in_both, grad_up_both)
    down_state = scatter_begin(down_local)
    gate_state = scatter_begin(gate_local)
    up_state = scatter_begin(up_local)
    down_grad = scatter_end(down_state)

    grad_mid, grad_attn, grad_att, gain_mid = mid_back(
        place, grad_ffn_in, stream, attn_out, top, gains, near, far, down_state[2], gate_state[1]
    )
    gate_grad = scatter_end(gate_state)
    grad_q, grad_own, grad_old = attend_back(
        place, queries, pair, behind, attended, grad_att, cosine, sine
    )
    grad_ahead = from_behind(grad_old, "seq", -1)
    grad_proj, grad_attn_part, gain_attn = project_back(
        place, grad_q, grad_own, grad_ahead, cosine, sine, stream, near, far, down_grad[2], up_state[1]
    )
    grad_attn_in = tensor_sum(grad_attn_part)
    up_grad = scatter_end(up_state)
    gate_up_grad = join(gate_grad, up_grad)

    out_local = weight_local(both_cores(grad_attn), att_both)
    out_grad = scatter_end(scatter_begin(out_local))
    proj_both = jnp.concatenate([grad_proj, swap(grad_proj, "seq", 1)], axis=0)
    qkv_local = weight_local(attn_in_both, proj_both)
    qkv_grad = sum(part.astype(jnp.float32) for part in scatter_end(scatter_begin(qkv_local)))[:, None]
    gains_rest = jnp.concatenate([gain_mid, gain_ffn[None]], axis=0).sum(axis=1)
    gains_rest = jnp.where(lax.axis_index("tensor") == 0, gains_rest, 0.0)
    gains_total = everywhere_sum(jnp.concatenate([gain_attn.sum(axis=0)[None], gains_rest], axis=0))
    own_columns = norm_gains.shape[1]
    gains_grad = lax.dynamic_slice_in_dim(
        gains_total, (chip * 2 + core) * own_columns, own_columns, axis=1
    )
    attn_float = attn_out.astype(jnp.float32)
    mid_stream = stream.astype(jnp.float32) + rms_norm(attn_float, gains[1])
    layer_out = (mid_stream + rms_norm(ffn_out.astype(jnp.float32), gains[3])).astype(jnp.bfloat16)
    qkv_shape, gate_up_shape = qkv_weight.shape, gate_up_weight.shape
    qkv_new, qkv_first_new, qkv_second_new = (
        unflat(value, qkv_shape)
        for value in adam(
            [flat(qkv_grad)], flat(qkv_weight), flat(qkv_first), flat(qkv_second), decay_rate
        )
    )
    out_new, out_first_new, out_second_new, out_grad = adam(
        out_grad, out_weight.T, out_first.T, out_second.T, decay_rate
    )
    gate_up_new, gate_up_first_new, gate_up_second_new = (
        unflat(value, gate_up_shape)
        for value in adam(
            [flat(gate_up_grad)],
            flat(gate_up_weight),
            flat(gate_up_first),
            flat(gate_up_second),
            decay_rate,
        )
    )
    down_new, down_first_new, down_second_new, down_grad = adam(
        down_grad, down_weight.T, down_first.T, down_second.T, decay_rate
    )
    gains_new, gains_first_new, gains_second_new = adam_step(
        norm_gains, gains_grad, gains_first, gains_second, 0.0
    )
    input_grad = stream_back(
        grad_attn_in, stream, gains, grad_mid, qkv_new, out_new, gate_up_new, down_new, gains_new
    )
    return (
        layer_out[None],
        input_grad[None],
        qkv_grad,
        out_grad.T,
        gate_up_grad,
        down_grad.T,
        gains_grad,
        qkv_new,
        out_new.T,
        gate_up_new,
        down_new.T,
        gains_new,
        qkv_first_new,
        out_first_new.T,
        gate_up_first_new,
        down_first_new.T,
        gains_first_new,
        qkv_second_new,
        out_second_new.T,
        gate_up_second_new,
        down_second_new.T,
        gains_second_new,
    )


def on_device(
    layer_in,
    cotangent,
    qkv_weight,
    out_weight,
    gate_up_weight,
    down_weight,
    norm_gains,
    qkv_first,
    out_first,
    gate_up_first,
    down_first,
    gains_first,
    qkv_second,
    out_second,
    gate_up_second,
    down_second,
    gains_second,
):
    tok_rows = layer_in.shape[1]
    seq_index = lax.axis_index("seq")
    collected = (
        lax.all_gather(qkv_weight.astype(jnp.bfloat16), ("batch", "seq"), axis=0, tiled=True),
        lax.all_gather(out_weight.astype(jnp.bfloat16), ("batch", "seq"), axis=1, tiled=True),
        lax.all_gather(gate_up_weight.astype(jnp.bfloat16), ("batch", "seq"), axis=0, tiled=True),
        lax.all_gather(down_weight.astype(jnp.bfloat16), ("batch", "seq"), axis=1, tiled=True),
        lax.all_gather(norm_gains.astype(jnp.bfloat16), ("batch", "seq"), axis=1, tiled=True),
    )
    qkv_full, out_full, gate_up_full, down_full, gains_full = collected
    model_width = qkv_full.shape[0]
    kv_local = qkv_full.shape[1]
    heads_local = kv_local * GROUP
    ffn_local = gate_up_full.shape[2]
    qkv_flat = qkv_full.reshape(model_width, kv_local * (GROUP + 2) * HEAD_DIM)
    gate_up_flat = gate_up_full.reshape(model_width, 2 * ffn_local)
    gains_float = gains_full.astype(jnp.float32)
    positions = seq_index * tok_rows + jnp.arange(tok_rows, dtype=jnp.int32)
    cosine, sine = rope_tables(positions, HEAD_DIM)
    key_positions = (seq_index - WIN_BLOCKS) * tok_rows + jnp.arange(
        (WIN_BLOCKS + 1) * tok_rows, dtype=jnp.int32
    )
    spread = positions[:, None] - key_positions[None, :]
    allowed = (spread >= 0) & (spread < WIN_BLOCKS * tok_rows) & (key_positions >= 0)[None, :]
    mask = allowed[None, None]
    stream = layer_in[0].astype(jnp.float32)
    attn_in = rms_norm(stream, gains_float[0]).astype(jnp.bfloat16)
    projected = jnp.dot(attn_in, qkv_flat, preferred_element_type=jnp.float32).reshape(
        tok_rows, kv_local, GROUP + 2, HEAD_DIM
    )
    queries = rotate(
        projected[:, :, :GROUP].reshape(tok_rows, heads_local, HEAD_DIM), cosine, sine
    ).astype(jnp.bfloat16)
    keys = rotate(projected[:, :, GROUP], cosine, sine).astype(jnp.bfloat16)
    values = projected[:, :, GROUP + 1].astype(jnp.bfloat16)
    kv_pair = jnp.stack([keys, values], axis=0)
    reach = min(WIN_BLOCKS, lax.axis_size("seq") - 1)
    pieces = []
    for distance in range(WIN_BLOCKS, 0, -1):
        if distance <= reach:
            pieces.append(from_behind(kv_pair, "seq", distance))
        else:
            pieces.append(jnp.zeros_like(kv_pair))
    pieces.append(kv_pair)
    extended = jnp.concatenate(pieces, axis=1)
    ext_keys = extended[0]
    ext_values = extended[1]
    query_groups = queries.reshape(tok_rows, kv_local, GROUP, HEAD_DIM)
    capped = capped_scores(query_groups, ext_keys)
    log_sums = jnp.log(jnp.sum(jnp.where(mask, jnp.exp(capped), 0.0), axis=-1))
    probs = jnp.where(mask, jnp.exp(capped - log_sums[..., None]), 0.0).astype(jnp.bfloat16)
    attended = jnp.einsum(
        "cgij,jcd->icgd", probs, ext_values, preferred_element_type=jnp.float32
    ).astype(jnp.bfloat16)
    att_flat = attended.reshape(tok_rows, heads_local * HEAD_DIM)
    attn_out = lax.psum(jnp.dot(att_flat, out_full, preferred_element_type=jnp.float32), "tensor")
    mid_stream = stream + rms_norm(attn_out, gains_float[1])
    ffn_in = rms_norm(mid_stream, gains_float[2]).astype(jnp.bfloat16)
    gate_up = jnp.dot(ffn_in, gate_up_flat, preferred_element_type=jnp.float32).reshape(
        tok_rows, 2, ffn_local
    )
    hidden = geglu(gate_up[:, 0], gate_up[:, 1]).astype(jnp.bfloat16)
    ffn_out = lax.psum(jnp.dot(hidden, down_full, preferred_element_type=jnp.float32), "tensor")
    layer_out = (mid_stream + rms_norm(ffn_out, gains_float[3])).astype(jnp.bfloat16)
    grad_top = cotangent[0].astype(jnp.float32)
    grad_ffn_out, gain_three = norm_back(ffn_out, gains_float[3], grad_top)
    grad_ffn = grad_ffn_out.astype(jnp.bfloat16)
    grad_hidden = cols_product(grad_ffn, down_full)
    _, geglu_pull = jax.vjp(geglu, gate_up[:, 0], gate_up[:, 1])
    grad_gate, grad_up = geglu_pull(grad_hidden)
    grad_gate_up = (
        jnp.stack([grad_gate, grad_up], axis=1)
        .reshape(tok_rows, 2 * ffn_local)
        .astype(jnp.bfloat16)
    )
    grad_ffn_in = lax.psum(cols_product(grad_gate_up, gate_up_flat), "tensor")
    grad_mid_norm, gain_two = norm_back(mid_stream, gains_float[2], grad_ffn_in)
    grad_mid = grad_top + grad_mid_norm
    grad_attn_out, gain_one = norm_back(attn_out, gains_float[1], grad_mid)
    grad_attn = grad_attn_out.astype(jnp.bfloat16)
    grad_att = (
        cols_product(grad_attn, out_full)
        .astype(jnp.bfloat16)
        .reshape(tok_rows, kv_local, GROUP, HEAD_DIM)
    )
    capped_again = capped_scores(query_groups, ext_keys)
    probs_float = jnp.where(mask, jnp.exp(capped_again - log_sums[..., None]), 0.0)
    probs_again = probs_float.astype(jnp.bfloat16)
    delta = jnp.einsum("icgd,icgd->cgi", grad_att, attended, preferred_element_type=jnp.float32)
    grad_probs = jnp.einsum(
        "icgd,jcd->cgij", grad_att, ext_values, preferred_element_type=jnp.float32
    )
    grad_scores = (
        probs_float * (grad_probs - delta[..., None]) * (1.0 - (capped_again / soft_cap) ** 2)
    ).astype(jnp.bfloat16)
    score_scale = HEAD_DIM ** (-0.5)
    grad_values_ext = jnp.einsum(
        "cgij,icgd->jcd", probs_again, grad_att, preferred_element_type=jnp.float32
    )
    grad_keys_ext = (
        jnp.einsum("cgij,icgd->jcd", grad_scores, query_groups, preferred_element_type=jnp.float32)
        * score_scale
    )
    grad_queries = (
        jnp.einsum("cgij,jcd->icgd", grad_scores, ext_keys, preferred_element_type=jnp.float32)
        * score_scale
    )
    grad_pair_ext = jnp.stack([grad_keys_ext, grad_values_ext], axis=0)
    grad_pair = grad_pair_ext[:, WIN_BLOCKS * tok_rows :]
    for distance in range(1, reach + 1):
        start = (WIN_BLOCKS - distance) * tok_rows
        piece = grad_pair_ext[:, start : start + tok_rows]
        grad_pair = grad_pair + from_behind(piece.astype(jnp.bfloat16), "seq", -distance).astype(
            piece.dtype
        )
    grad_queries = rotate(
        grad_queries.reshape(tok_rows, heads_local, HEAD_DIM), cosine, -sine
    ).reshape(tok_rows, kv_local, GROUP, HEAD_DIM)
    grad_keys = rotate(grad_pair[0], cosine, -sine)
    grad_values = grad_pair[1]
    grad_proj = (
        jnp.concatenate([grad_queries, grad_keys[:, :, None], grad_values[:, :, None]], axis=2)
        .reshape(tok_rows, kv_local * (GROUP + 2) * HEAD_DIM)
        .astype(jnp.bfloat16)
    )
    grad_attn_in = lax.psum(
        cols_product(grad_proj, qkv_flat).astype(jnp.bfloat16), "tensor"
    ).astype(jnp.float32)
    grad_stream_norm, gain_zero = norm_back(stream, gains_float[0], grad_attn_in)
    input_grad = grad_mid + grad_stream_norm
    qkv_local = rows_product(attn_in, grad_proj).reshape(
        model_width, kv_local, (GROUP + 2) * HEAD_DIM
    )
    out_local = rows_product(att_flat, grad_attn)
    gate_up_local = rows_product(ffn_in, grad_gate_up).reshape(model_width, 2, ffn_local)
    down_local = rows_product(hidden, grad_ffn)
    gains_local = jnp.stack([gain_zero, gain_one, gain_two, gain_three])
    summed = (
        lax.psum_scatter(
            qkv_local.astype(jnp.bfloat16), ("batch", "seq"), scatter_dimension=0, tiled=True
        ).astype(jnp.float32),
        lax.psum_scatter(
            out_local.astype(jnp.bfloat16), ("batch", "seq"), scatter_dimension=1, tiled=True
        ).astype(jnp.float32),
        lax.psum_scatter(
            gate_up_local.astype(jnp.bfloat16), ("batch", "seq"), scatter_dimension=0, tiled=True
        ).astype(jnp.float32),
        lax.psum_scatter(
            down_local.astype(jnp.bfloat16), ("batch", "seq"), scatter_dimension=1, tiled=True
        ).astype(jnp.float32),
        lax.psum_scatter(
            gains_local.astype(jnp.bfloat16), ("batch", "seq"), scatter_dimension=1, tiled=True
        ).astype(jnp.float32),
    )
    qkv_grad, out_grad, gate_up_grad, down_grad, gains_grad = summed
    qkv_new, qkv_first_new, qkv_second_new = adam_step(
        qkv_weight, qkv_grad, qkv_first, qkv_second, decay_rate
    )
    out_new, out_first_new, out_second_new = adam_step(
        out_weight, out_grad, out_first, out_second, decay_rate
    )
    gate_up_new, gate_up_first_new, gate_up_second_new = adam_step(
        gate_up_weight, gate_up_grad, gate_up_first, gate_up_second, decay_rate
    )
    down_new, down_first_new, down_second_new = adam_step(
        down_weight, down_grad, down_first, down_second, decay_rate
    )
    gains_new, gains_first_new, gains_second_new = adam_step(
        norm_gains, gains_grad, gains_first, gains_second, 0.0
    )
    return (
        layer_out[None],
        input_grad[None],
        qkv_grad,
        out_grad,
        gate_up_grad,
        down_grad,
        gains_grad,
        qkv_new,
        out_new,
        gate_up_new,
        down_new,
        gains_new,
        qkv_first_new,
        out_first_new,
        gate_up_first_new,
        down_first_new,
        gains_first_new,
        qkv_second_new,
        out_second_new,
        gate_up_second_new,
        down_second_new,
        gains_second_new,
    )


def solution(mesh):
    in_specs = (
        P("batch", "seq", None),
        P("batch", "seq", None),
        P(("batch", "seq"), "tensor", None),
        P("tensor", ("batch", "seq")),
        P(("batch", "seq"), None, "tensor"),
        P("tensor", ("batch", "seq")),
        P(None, ("batch", "seq")),
        P(("batch", "seq"), "tensor", None),
        P("tensor", ("batch", "seq")),
        P(("batch", "seq"), None, "tensor"),
        P("tensor", ("batch", "seq")),
        P(None, ("batch", "seq")),
        P(("batch", "seq"), "tensor", None),
        P("tensor", ("batch", "seq")),
        P(("batch", "seq"), None, "tensor"),
        P("tensor", ("batch", "seq")),
        P(None, ("batch", "seq")),
    )
    out_specs = (
        P("batch", "seq", None),
        P("batch", "seq", None),
        P(("batch", "seq"), "tensor", None),
        P("tensor", ("batch", "seq")),
        P(("batch", "seq"), None, "tensor"),
        P("tensor", ("batch", "seq")),
        P(None, ("batch", "seq")),
        P(("batch", "seq"), "tensor", None),
        P("tensor", ("batch", "seq")),
        P(("batch", "seq"), None, "tensor"),
        P("tensor", ("batch", "seq")),
        P(None, ("batch", "seq")),
        P(("batch", "seq"), "tensor", None),
        P("tensor", ("batch", "seq")),
        P(("batch", "seq"), None, "tensor"),
        P("tensor", ("batch", "seq")),
        P(None, ("batch", "seq")),
        P(("batch", "seq"), "tensor", None),
        P("tensor", ("batch", "seq")),
        P(("batch", "seq"), None, "tensor"),
        P("tensor", ("batch", "seq")),
        P(None, ("batch", "seq")),
    )
    sizes = tuple(mesh.shape[axis] for axis in ("batch", "seq", "tensor"))
    body = on_square if sizes == (4, 2, 4) else on_device
    return jax.shard_map(
        body, mesh=mesh, in_specs=in_specs, out_specs=out_specs, check_vma=False
    )
```

```python
import functools
import jax
import jax.numpy as jnp
from jax import lax
from jax.experimental.layout import Layout, with_layout_constraint
from jax.experimental import pallas as pl
from jax.experimental.pallas import tpu as pltpu
from jax.sharding import PartitionSpec as P

HEAD_DIM = 256
WIN_BLOCKS = 4
STEP = 10
GROUP = 2


norm_eps = 1e-06
soft_cap = 50.0
learn_rate = 0.02
decay_rate = 0.1
beta_first = 0.9
beta_second = 0.95
adam_eps = 1e-08
gelu_coef = 0.7978845608028654


def from_behind(value, axis, steps):
    count = lax.axis_size(axis)
    initial, last = (max(0, -steps), min(count, count - steps))
    return lax.ppermute(value, axis, [(source, source + steps) for source in range(initial, last)])


def rms_norm(values, gain):
    scale = lax.rsqrt(jnp.mean(values * values, axis=-1, keepdims=True) + norm_eps)
    return values * scale * (1.0 + gain)


def norm_back(values, gain, upstream):
    _, pullback = jax.vjp(rms_norm, values, gain)
    return pullback(upstream)


def gelu_tanh(values):
    inner = gelu_coef * (values + 0.044715 * values * values * values)
    return 0.5 * values * (1.0 + jnp.tanh(inner))


def geglu(gate, up_part):
    return gelu_tanh(gate) * up_part


def rope_tables(positions, head_size):
    half = head_size // 2
    exponent = jnp.arange(half, dtype=jnp.float32) * (2.0 / head_size)
    freqs = 10000.0 ** (-exponent)
    angles = positions.astype(jnp.float32)[:, None] * freqs[None, :]
    return (jnp.cos(angles), jnp.sin(angles))


def rotate(values, cosine, sine):
    half = values.shape[-1] // 2
    first = values[..., :half]
    second = values[..., half:]
    cosine = cosine[:, None, :]
    sine = sine[:, None, :]
    return jnp.concatenate(
        [first * cosine - second * sine, second * cosine + first * sine], axis=-1
    )


def adam_step(weight, grad, first, second, decay):
    first_new = beta_first * first + (1.0 - beta_first) * grad
    second_new = beta_second * second + (1.0 - beta_second) * grad * grad
    first_hat = first_new / (1.0 - beta_first**STEP)
    second_hat = second_new / (1.0 - beta_second**STEP)
    weight_new = weight - learn_rate * (
        first_hat / (jnp.sqrt(second_hat) + adam_eps) + decay * weight
    )
    return (weight_new, first_new, second_new)


def rows_product(left, right):
    return lax.dot_general(
        left, right, (((0,), (0,)), ((), ())), preferred_element_type=jnp.float32
    )


def cols_product(left, right):
    return lax.dot_general(
        left, right, (((1,), (1,)), ((), ())), preferred_element_type=jnp.float32
    )


def capped_scores(query_groups, ext_keys):
    raw = jnp.einsum(
        "icgd,jcd->cgij", query_groups, ext_keys, preferred_element_type=jnp.float32
    ) * query_groups.shape[-1] ** (-0.5)
    return soft_cap * jnp.tanh(raw / soft_cap)


def tensor_sum(part):
    return lax.psum(part, "tensor")


def swap(value, axis, bit):
    count = lax.axis_size(axis)
    return lax.ppermute(value, axis, [(source, source ^ bit) for source in range(count)])


def after(value, *earlier):
    return lax.optimization_barrier((value, earlier))[0]


def trade(value, turn):
    pairs = []
    for chip in range(4):
        for core in range(2):
            pairs.append((chip * 2 + core, (chip ^ (1 + (core ^ turn))) * 2 + core))
    return lax.ppermute(value, ("batch", "seq"), pairs)


def offsets(owner):
    return (0, 1 + owner, 2 - owner, 3)


def own_blocks(wide):
    tokens, width = wide.shape
    chip, core = lax.axis_index("batch"), lax.axis_index("seq")
    split = wide.reshape(tokens, 8, width // 8)
    halves = []
    for owner in (core, 1 - core):
        parts = [
            lax.dynamic_index_in_dim(split, (chip ^ offset) * 2 + owner, 1, keepdims=False)
            for offset in offsets(owner)
        ]
        halves.append(jnp.concatenate(parts, axis=1))
    return halves


def both_cores(wide):
    mine, theirs = own_blocks(wide)
    return jnp.concatenate([mine, swap(theirs, "seq", 1)], axis=0)


def weight_local(wide, narrow):
    local = rows_product(wide, narrow).astype(jnp.bfloat16)
    return local.reshape(4, -1, local.shape[1])


def scatter_begin(local, got=None):
    if got is None:
        got = trade(jnp.stack([local[1], local[3]]), 0)
    far = local[2].astype(jnp.float32) + got[1].astype(jnp.float32)
    return local, got, far.astype(jnp.bfloat16)


def scatter_end(state):
    local, got, far = state
    return local[0], got[0], trade(far, 1)


def everywhere_sum(value):
    for axis, bit in (("seq", 1), ("batch", 1), ("batch", 2), ("tensor", 1), ("tensor", 2)):
        value = value + swap(value, axis, bit)
    return value


FFN_TILE = 768
ROW_CHUNK = 16
ROW_UNROLL = 4
MID_ROWS = 128


def spec_any():
    return pl.BlockSpec(memory_space=pl.ANY)


def spec_vmem():
    return pl.BlockSpec(memory_space=pltpu.VMEM)


def spec_smem():
    return pl.BlockSpec(memory_space=pltpu.SMEM)


def kernel_params():
    return pltpu.CompilerParams(vmem_limit_bytes=56 * 1024 * 1024)


def cost(flops, moved):
    return pl.CostEstimate(flops=flops, bytes_accessed=moved, transcendentals=0)


def shaped(shape, kind):
    return jax.ShapeDtypeStruct(shape, kind)


def dot_nn(left, right):
    return lax.dot_general(
        left, right, (((1,), (0,)), ((), ())), preferred_element_type=jnp.float32
    )


def dot_nt(left, right):
    return lax.dot_general(
        left, right, (((1,), (1,)), ((), ())), preferred_element_type=jnp.float32
    )


def dot_tn(left, right):
    return lax.dot_general(
        left, right, (((0,), (0,)), ((), ())), preferred_element_type=jnp.float32
    )


def row_scale(values):
    return lax.rsqrt(jnp.mean(values * values, axis=-1, keepdims=True) + norm_eps)


def norm_pull(values, scale, gain, upstream):
    normed = values * scale
    inner = upstream * (1.0 + gain)
    pulled = scale * (inner - normed * jnp.mean(normed * inner, axis=-1, keepdims=True))
    return pulled, upstream * normed


def fold_rows(values):
    total = values[:8]
    for start in range(8, values.shape[0], 8):
        total += values[start : start + 8]
    return total


def fetch_rows(place, near, far, target, sems, column, columns):
    chip, core = place[0], place[1]
    rows = near[0].shape[1]
    copies = []
    for which, (one, two) in enumerate((near, far)):
        owner = which ^ core
        blocks = ((one.at[0], 0), (one.at[1], 1 + owner), (two.at[0], 2 - owner), (two.at[1], 3))
        for block, offset in blocks:
            row = ((offset ^ chip) * 2 + owner) * rows
            copies.append(
                pltpu.make_async_copy(
                    block.at[:, pl.ds(column, columns)],
                    target.at[pl.ds(pl.multiple_of(row, 16), rows), :],
                    sems.at[len(copies)],
                )
            )
    return copies


def rope(values, cosine, sine):
    half = HEAD_DIM // 2
    first, second = values[:, :half], values[:, half:]
    return jnp.concatenate(
        [first * cosine - second * sine, second * cosine + first * sine], axis=1
    )


def arrange_kernel(place, one, two, one_far, two_far, result, sems):
    copies = fetch_rows(place, (one, two), (one_far, two_far), result, sems, 0, result.shape[1])
    for copy in copies:
        copy.start()
    for copy in copies:
        copy.wait()


def arrange(place, near, far):
    return pl.pallas_call(
        arrange_kernel,
        in_specs=[spec_smem()] + [spec_any()] * 4,
        out_specs=spec_vmem(),
        out_shape=shaped((8 * near[0].shape[1], near[0].shape[2]), jnp.bfloat16),
        scratch_shapes=[pltpu.SemaphoreType.DMA((8,))],
        compiler_params=kernel_params(),
        cost_estimate=cost(0, 16 * near[0].size),
        name="arrange",
    )(place, *near, *far)


def project_kernel(place, x, one, two, one_far, two_far, cosine, sine, *rest):
    queries, pair, attn_in, gains, weight, sems = rest[-6:]
    copies = fetch_rows(place, (one, two), (one_far, two_far), weight, sems, 0, weight.shape[1])
    for copy in copies:
        copy.start()
    for copy in copies:
        copy.wait()
    width = (GROUP + 2) * HEAD_DIM
    tail = weight[:, width + GROUP * HEAD_DIM :].astype(jnp.float32)
    gains[...] = jnp.transpose(tail)[:8]
    gain = 1.0 + gains[0:1, :]
    chunk = ROW_CHUNK

    @pl.loop(0, x.shape[0] // chunk, unroll=ROW_UNROLL)
    def _(step):
        rows = pl.ds(pl.multiple_of(step * chunk, chunk), chunk)
        stream = x[rows, :].astype(jnp.float32)
        attn_in[rows, :] = (stream * row_scale(stream) * gain).astype(jnp.bfloat16)

    for member in range(GROUP + 2):
        columns = slice(member * HEAD_DIM, (member + 1) * HEAD_DIM)
        part = dot_nn(attn_in[...], weight[:, columns])
        if member < GROUP:
            queries[:, columns] = rope(part, cosine[...], sine[...]).astype(jnp.bfloat16)
        elif member == GROUP:
            pair[0] = rope(part, cosine[...], sine[...]).astype(jnp.bfloat16)
        else:
            pair[1] = part.astype(jnp.bfloat16)


def project(place, x, near, far, cosine, sine, *earlier):
    tokens, width = x.shape
    bf16 = jnp.bfloat16
    return pl.pallas_call(
        project_kernel,
        in_specs=[spec_smem(), spec_vmem()]
        + [spec_any()] * 4
        + [spec_vmem()] * 2
        + [spec_any()] * len(earlier),
        out_specs=[spec_vmem()] * 4,
        out_shape=[
            shaped((tokens, GROUP * HEAD_DIM), bf16),
            shaped((2, tokens, HEAD_DIM), bf16),
            shaped((tokens, width), bf16),
            shaped((8, width), jnp.float32),
        ],
        scratch_shapes=[pltpu.VMEM((width, near[0].shape[2]), bf16), pltpu.SemaphoreType.DMA((8,))],
        compiler_params=kernel_params(),
        cost_estimate=cost(2 * tokens * width * 1024, 12_000_000),
        name="project",
    )(place, x, *near, *far, cosine, sine, *earlier)


def chunk_scores(query, key, behind, row, core):
    raw = dot_nt(query, key) * (HEAD_DIM**-0.5 / soft_cap)
    bent = jnp.tanh(raw)
    powers = jnp.exp(soft_cap * bent)
    if behind:
        powers = jnp.where(core > 0, powers, 0.0)
    else:
        at = row + lax.broadcasted_iota(jnp.int32, powers.shape, 0)
        powers = jnp.where(at >= lax.broadcasted_iota(jnp.int32, powers.shape, 1), powers, 0.0)
    return bent, powers


def attend_kernel(place, queries, pair, behind, one, two, one_far, two_far, *rest):
    attended, result, weight, sems = rest[-4:]
    width = (GROUP + 2) * HEAD_DIM
    copies = fetch_rows(place, (one, two), (one_far, two_far), weight, sems, width, GROUP * HEAD_DIM)
    for copy in copies:
        copy.start()
    core = place[1]
    chunk = 128
    tokens = queries.shape[0]
    for start in range(0, tokens, chunk):
        rows = slice(start, start + chunk)
        keys = start + chunk
        for head in range(GROUP):
            columns = slice(head * HEAD_DIM, (head + 1) * HEAD_DIM)
            query = queries[rows, columns]
            _, old = chunk_scores(query, behind[0], True, start, core)
            _, new = chunk_scores(query, pair[0, :keys], False, start, core)
            total = jnp.sum(old, axis=-1, keepdims=True) + jnp.sum(new, axis=-1, keepdims=True)
            share = 1.0 / total
            value = dot_nn((old * share).astype(jnp.bfloat16), behind[1])
            value += dot_nn((new * share).astype(jnp.bfloat16), pair[1, :keys])
            attended[rows, columns] = value.astype(jnp.bfloat16)
    for copy in copies:
        copy.wait()
    tile = 768
    for column in range(0, result.shape[1], tile):
        part = dot_nt(attended[...], weight[column : column + tile, :])
        result[:, column : column + tile] = part.astype(jnp.bfloat16)


def attend(place, queries, pair, behind, near, far, width, *earlier):
    tokens = queries.shape[0]
    bf16 = jnp.bfloat16
    return pl.pallas_call(
        attend_kernel,
        in_specs=[spec_smem()] + [spec_vmem()] * 3 + [spec_any()] * (4 + len(earlier)),
        out_specs=[spec_vmem()] * 2,
        out_shape=[shaped((tokens, GROUP * HEAD_DIM), bf16), shaped((tokens, width), bf16)],
        scratch_shapes=[
            pltpu.VMEM((width, GROUP * HEAD_DIM), bf16),
            pltpu.SemaphoreType.DMA((8,)),
        ],
        compiler_params=kernel_params(),
        cost_estimate=cost(4 * tokens * width * 1024, 8_000_000),
        name="attend",
    )(place, queries, pair, behind, *near, *far, *earlier)


def whole(shape):
    return pl.BlockSpec(shape, lambda *_: (0,) * len(shape))


def ffn_params():
    return pltpu.CompilerParams(vmem_limit_bytes=58 * 1024 * 1024)


def move(source, target, sem):
    copy = pltpu.make_async_copy(source, target, sem)
    copy.start()
    return copy


def ffn_kernel(place, attn_out, x, gains, up_full, *rest):
    gate_near, gate_far, down_near, down_far = (rest[k : k + 2] for k in (0, 2, 4, 6))
    outs, (sides, gate_up_here, down_here, in_sems, down_sems, out_sems) = rest[-11:-6], rest[-6:]
    ffn_in, hidden, by_gate, by_up, result = (sides.at[k] for k in range(5))
    tokens, width = x.shape
    units = up_full.shape[1]
    tile = FFN_TILE
    steps, turns = units // tile, width // tile

    def load(step):
        columns = pl.ds(pl.multiple_of(step * tile, tile), tile)
        up_copy = pltpu.make_async_copy(
            up_full.at[:, columns], gate_up_here.at[1, :, columns], in_sems.at[step, 8]
        )
        target = gate_up_here.at[0, :, columns]
        return [up_copy] + fetch_rows(
            place, gate_near, gate_far, target, in_sems.at[step], columns.start, tile
        )

    down_copies = fetch_rows(place, down_near, down_far, down_here, down_sems, 0, units)
    for step in range(steps):
        for copy in load(step):
            copy.start()
    for copy in down_copies:
        copy.start()
    chunk = ROW_CHUNK

    @pl.loop(0, tokens // chunk, unroll=ROW_UNROLL)
    def _(step):
        rows = pl.ds(pl.multiple_of(step * chunk, chunk), chunk)
        out = attn_out[rows, :].astype(jnp.float32)
        mid = x[rows, :].astype(jnp.float32) + out * row_scale(out) * (1.0 + gains[1:2, :])
        ffn_in[rows, :] = (mid * row_scale(mid) * (1.0 + gains[2:3, :])).astype(jnp.bfloat16)

    stores = [move(ffn_in, outs[0], out_sems.at[0])]

    @pl.loop(0, steps)
    def _(step):
        for copy in load(step):
            copy.wait()
        columns = pl.ds(pl.multiple_of(step * tile, tile), tile)
        for rows in (slice(None),):
            value = ffn_in[...]
            gate = dot_nn(value, gate_up_here[0, :, columns])
            up = dot_nn(value, gate_up_here[1, :, columns])
            square_of = gate * gate
            bent = jnp.tanh(gate * (gelu_coef + gelu_coef * 0.044715 * square_of))
            half = 0.5 + 0.5 * bent
            curve = gate * half
            slope = half + curve * (1.0 - bent) * (
                gelu_coef + 3.0 * gelu_coef * 0.044715 * square_of
            )
            hidden[rows, columns] = (curve * up).astype(jnp.bfloat16)
            by_gate[rows, columns] = (slope * up).astype(jnp.bfloat16)
            by_up[rows, columns] = curve.astype(jnp.bfloat16)

    for k, side in ((1, hidden), (2, by_gate), (3, by_up)):
        stores.append(move(side, outs[k], out_sems.at[k]))

    def store(turn):
        columns = pl.ds(pl.multiple_of(turn * tile, tile), tile)
        return pltpu.make_async_copy(
            result.at[:, columns], outs[4].at[:, columns], out_sems.at[4 + turn]
        )

    for copy in down_copies:
        copy.wait()

    @pl.loop(0, turns)
    def _(turn):
        rows = pl.ds(pl.multiple_of(turn * tile, tile), tile)
        result[:, rows] = dot_nt(hidden[...], down_here[rows, :]).astype(jnp.bfloat16)
        store(turn).start()

    for copy in stores:
        copy.wait()
    for turn in range(turns):
        store(turn).wait()


def ffn_forward(place, attn_out, x, gains, up, gate, down):
    tokens, width = x.shape
    units = up.shape[1]
    bf16 = jnp.bfloat16
    return pl.pallas_call(
        ffn_kernel,
        in_specs=[spec_smem()] + [spec_vmem()] * 3 + [spec_any()] * 9,
        out_specs=[spec_any()] * 5,
        out_shape=[shaped((tokens, width), bf16)]
        + [shaped((tokens, units), bf16)] * 3
        + [shaped((tokens, width), bf16)],
        scratch_shapes=[
            pltpu.VMEM((5, tokens, width), bf16),
            pltpu.VMEM((2, width, units), bf16),
            pltpu.VMEM((width, units), bf16),
            pltpu.SemaphoreType.DMA((units // FFN_TILE, 9)),
            pltpu.SemaphoreType.DMA((8,)),
            pltpu.SemaphoreType.DMA((4 + width // FFN_TILE,)),
        ],
        compiler_params=ffn_params(),
        cost_estimate=cost(6 * tokens * width * units, 50_000_000),
        name="ffn_forward",
    )(place, attn_out, x, gains, up, *gate[0], *gate[1], *down[0], *down[1])


def ffn_back_kernel(ffn_out, top, gains, gate, up_full, down, by_gate, by_up, *rest):
    grad_out, gate_out, up_out, gain_out, result_out = rest[-13:-8]
    sides, grads, gate_up_here, down_here, in_sems, down_sems, gate_sems, out_sems = rest[-8:]
    grad_ffn, result = sides.at[0], sides.at[1]
    tokens, width = top.shape
    units = gate.shape[1]
    grad_gate, grad_up = grads.at[:, pl.ds(0, units)], grads.at[:, pl.ds(units, units)]
    tile = FFN_TILE
    steps, turns = units // tile, width // tile

    def load_down(step):
        columns = pl.ds(pl.multiple_of(step * tile, tile), tile)
        return pltpu.make_async_copy(
            down.at[:, columns], down_here.at[:, columns], down_sems.at[step]
        )

    def load(turn, which):
        rows = pl.ds(pl.multiple_of(turn * tile, tile), tile)
        return pltpu.make_async_copy(
            (gate, up_full)[which].at[rows, :],
            gate_up_here.at[rows, pl.ds(which * units, units)],
            gate_sems.at[turn, which],
        )

    load_down(0).start()
    factors = [
        move(by_gate, grad_gate, in_sems.at[0]),
        move(by_up, grad_up, in_sems.at[1]),
    ]
    load_down(1).start()
    gain_out[...] = jnp.zeros_like(gain_out)
    chunk = ROW_CHUNK

    @pl.loop(0, tokens // chunk, unroll=ROW_UNROLL)
    def _(step):
        rows = pl.ds(pl.multiple_of(step * chunk, chunk), chunk)
        out = ffn_out[rows, :].astype(jnp.float32)
        upstream = top[rows, :].astype(jnp.float32)
        pulled, product = norm_pull(out, row_scale(out), gains[3:4, :], upstream)
        grad_ffn[rows, :] = pulled.astype(jnp.bfloat16)
        gain_out[...] += fold_rows(product)

    stores = [move(grad_ffn, grad_out, out_sems.at[0])]
    for copy in factors:
        copy.wait()

    @pl.loop(0, steps)
    def _(step):
        load_down(step).wait()

        @pl.when(step + 2 < steps)
        def _():
            load_down(step + 2).start()

        @pl.when(step + 2 >= steps)
        def _():
            load(step + 2 - steps, 0).start()
            load(step + 2 - steps, 1).start()

        columns = pl.ds(pl.multiple_of(step * tile, tile), tile)
        for start in range(0, tokens, tokens // 2):
            rows = pl.ds(start, tokens // 2)
            grad_hidden = dot_nn(grad_ffn[rows, :], down_here[:, columns])
            one = grad_hidden * grad_gate[rows, columns].astype(jnp.float32)
            two = grad_hidden * grad_up[rows, columns].astype(jnp.float32)
            grad_gate[rows, columns] = one.astype(jnp.bfloat16)
            grad_up[rows, columns] = two.astype(jnp.bfloat16)

    stores.append(move(grad_gate, gate_out, out_sems.at[1]))
    stores.append(move(grad_up, up_out, out_sems.at[2]))

    def store(turn):
        columns = pl.ds(pl.multiple_of(turn * tile, tile), tile)
        return pltpu.make_async_copy(
            result.at[:, columns], result_out.at[:, columns], out_sems.at[3 + turn]
        )

    @pl.loop(0, turns)
    def _(turn):
        load(turn, 0).wait()
        load(turn, 1).wait()

        @pl.when(turn + 2 < turns)
        def _():
            load(turn + 2, 0).start()
            load(turn + 2, 1).start()

        rows = pl.ds(pl.multiple_of(turn * tile, tile), tile)
        part = dot_nt(grads[...], gate_up_here[rows, :])
        result[:, rows] = part.astype(jnp.bfloat16)
        store(turn).start()

    for copy in stores:
        copy.wait()
    for turn in range(turns):
        store(turn).wait()


def ffn_back(ffn_out, top, gains, gate, up, down, by_gate, by_up, *earlier):
    tokens, width = top.shape
    units = by_up.shape[1]
    bf16 = jnp.bfloat16
    return pl.pallas_call(
        ffn_back_kernel,
        in_specs=[spec_vmem()] * 3 + [spec_any()] * (5 + len(earlier)),
        out_specs=[spec_any()] * 3 + [spec_vmem(), spec_any()],
        out_shape=[
            shaped((tokens, width), bf16),
            shaped((tokens, units), bf16),
            shaped((tokens, units), bf16),
            shaped((8, width), jnp.float32),
            shaped((tokens, width), bf16),
        ],
        scratch_shapes=[
            pltpu.VMEM((2, tokens, width), bf16),
            pltpu.VMEM((tokens, 2 * units), bf16),
            pltpu.VMEM((width, 2 * units), bf16),
            pltpu.VMEM((width, units), bf16),
            pltpu.SemaphoreType.DMA((2,)),
            pltpu.SemaphoreType.DMA((units // FFN_TILE,)),
            pltpu.SemaphoreType.DMA((width // FFN_TILE, 2)),
            pltpu.SemaphoreType.DMA((3 + width // FFN_TILE,)),
        ],
        compiler_params=ffn_params(),
        cost_estimate=cost(6 * tokens * width * units, 55_000_000),
        name="ffn_back",
    )(ffn_out, top, gains, gate, up, down, by_gate, by_up, *earlier)


def mid_back_kernel(place, grad_in, x, attn_out, top, gains, one, two, one_far, two_far, *rest):
    grad_mid, grad_attn, grad_att, gain_out, weight, sems = rest[-6:]
    width = (GROUP + 2) * HEAD_DIM
    first = pl.program_id(0) == 0

    def fetch():
        return fetch_rows(place, (one, two), (one_far, two_far), weight, sems, width, GROUP * HEAD_DIM)

    @pl.when(first)
    def _():
        gain_out[...] = jnp.zeros_like(gain_out)
        for copy in fetch():
            copy.start()

    chunk = ROW_CHUNK

    @pl.loop(0, x.shape[0] // chunk, unroll=ROW_UNROLL)
    def _(step):
        rows = pl.ds(pl.multiple_of(step * chunk, chunk), chunk)
        out = attn_out[rows, :].astype(jnp.float32)
        out_scale = row_scale(out)
        mid = x[rows, :].astype(jnp.float32) + out * out_scale * (1.0 + gains[1:2, :])
        upstream = grad_in[rows, :].astype(jnp.float32)
        pulled, product = norm_pull(mid, row_scale(mid), gains[2:3, :], upstream)
        gain_out[1] += fold_rows(product)
        at_mid = top[rows, :].astype(jnp.float32) + pulled
        grad_mid[rows, :] = at_mid
        pulled, product = norm_pull(out, out_scale, gains[1:2, :], at_mid)
        gain_out[0] += fold_rows(product)
        grad_attn[rows, :] = pulled.astype(jnp.bfloat16)

    @pl.when(first)
    def _():
        for copy in fetch():
            copy.wait()

    grad_att[...] = dot_nn(grad_attn[...], weight[...]).astype(jnp.bfloat16)


def mid_back(place, grad_in, x, attn_out, top, gains, near, far, *earlier):
    tokens, width = x.shape
    heads = GROUP * HEAD_DIM
    bf16 = jnp.bfloat16
    rows = pl.BlockSpec((MID_ROWS, width), lambda i: (i, 0))
    return pl.pallas_call(
        mid_back_kernel,
        grid=(tokens // MID_ROWS,),
        in_specs=[spec_smem()]
        + [rows] * 4
        + [whole((8, width))]
        + [spec_any()] * (4 + len(earlier)),
        out_specs=[
            rows,
            rows,
            pl.BlockSpec((MID_ROWS, heads), lambda i: (i, 0)),
            whole((2, 8, width)),
        ],
        out_shape=[
            shaped((tokens, width), jnp.float32),
            shaped((tokens, width), bf16),
            shaped((tokens, heads), bf16),
            shaped((2, 8, width), jnp.float32),
        ],
        scratch_shapes=[pltpu.VMEM((width, heads), bf16), pltpu.SemaphoreType.DMA((8,))],
        compiler_params=kernel_params(),
        cost_estimate=cost(2 * tokens * width * heads, 24_000_000),
        name="mid_back",
    )(place, grad_in, x, attn_out, top, gains, *near, *far, *earlier)


def attend_back_kernel(
    place, queries, pair, behind, attended, grad_att, cosine, sine, *rest
):
    grad_q, grad_own, grad_old, sums = rest[-4:]
    core = place[1]
    chunk = 128
    tokens = queries.shape[0]
    scale = HEAD_DIM**-0.5
    sums[...] = jnp.zeros_like(sums)
    for start in range(0, tokens, chunk):
        rows = slice(start, start + chunk)
        keys = start + chunk
        cos, sin = cosine[rows, :], sine[rows, :]
        for head in range(GROUP):
            columns = slice(head * HEAD_DIM, (head + 1) * HEAD_DIM)
            query, upstream = queries[rows, columns], grad_att[rows, columns]
            delta = jnp.sum(
                upstream.astype(jnp.float32) * attended[rows, columns].astype(jnp.float32),
                axis=-1,
                keepdims=True,
            )
            bent_old, old = chunk_scores(query, behind[0], True, start, core)
            bent_new, new = chunk_scores(query, pair[0, :keys], False, start, core)
            share = 1.0 / (
                jnp.sum(old, axis=-1, keepdims=True) + jnp.sum(new, axis=-1, keepdims=True)
            )
            total = jnp.zeros((chunk, HEAD_DIM), jnp.float32)
            for bent, powers, block, end, base in (
                (bent_old, old, behind, tokens, 0),
                (bent_new, new, pair, keys, 2),
            ):
                prob = powers * share
                grad_p = dot_nt(upstream, block[1, :end])
                grad_s = (prob * (grad_p - delta) * (1.0 - bent * bent)).astype(jnp.bfloat16)
                total += dot_nn(grad_s, block[0, :end])
                sums[base, :end, :] += dot_tn(grad_s, query)
                sums[base + 1, :end, :] += dot_tn(prob.astype(jnp.bfloat16), upstream)
            grad_q[rows, columns] = rope(total * scale, cos, -sin).astype(jnp.bfloat16)
    grad_old[0] = (sums[0] * scale).astype(jnp.bfloat16)
    grad_old[1] = sums[1].astype(jnp.bfloat16)
    grad_own[0] = sums[2] * scale
    grad_own[1] = sums[3]


def attend_back(place, queries, pair, behind, attended, grad_att, cosine, sine, *earlier):
    tokens, heads = queries.shape
    bf16 = jnp.bfloat16
    return pl.pallas_call(
        attend_back_kernel,
        in_specs=[spec_smem()] + [spec_vmem()] * 7 + [spec_any()] * len(earlier),
        out_specs=[spec_vmem()] * 3,
        out_shape=[
            shaped((tokens, heads), bf16),
            shaped((2, tokens, HEAD_DIM), jnp.float32),
            shaped((2, tokens, HEAD_DIM), bf16),
        ],
        scratch_shapes=[pltpu.VMEM((4, tokens, HEAD_DIM), jnp.float32)],
        compiler_params=kernel_params(),
        cost_estimate=cost(20 * tokens * 1024 * heads, 5_000_000),
        name="attend_back",
    )(place, queries, pair, behind, attended, grad_att, cosine, sine, *earlier)


def project_back_kernel(
    place, grad_q, grad_own, grad_ahead, cosine, sine, x, one, two, one_far, two_far, *rest
):
    proj, result, gain_out, weight, sems = rest[-5:]
    width = (GROUP + 2) * HEAD_DIM
    copies = fetch_rows(place, (one, two), (one_far, two_far), weight, sems, 0, width)
    for copy in copies:
        copy.start()
    heads = GROUP * HEAD_DIM
    proj[:, :heads] = grad_q[...]
    grad_key = grad_own[0] + grad_ahead[0].astype(jnp.float32)
    proj[:, heads : heads + HEAD_DIM] = rope(grad_key, cosine[...], -sine[...]).astype(jnp.bfloat16)
    proj[:, heads + HEAD_DIM :] = (grad_own[1] + grad_ahead[1].astype(jnp.float32)).astype(
        jnp.bfloat16
    )
    gain_out[...] = jnp.zeros_like(gain_out)
    for copy in copies:
        copy.wait()
    tile = 768
    for column in range(0, result.shape[1], tile):
        part = dot_nt(proj[...], weight[column : column + tile, :])
        result[:, column : column + tile] = part.astype(jnp.bfloat16)
    chunk = ROW_CHUNK

    @pl.loop(0, x.shape[0] // chunk, unroll=ROW_UNROLL)
    def _(step):
        rows = pl.ds(pl.multiple_of(step * chunk, chunk), chunk)
        stream = x[rows, :].astype(jnp.float32)
        product = result[rows, :].astype(jnp.float32) * (stream * row_scale(stream))
        gain_out[...] += fold_rows(product)


def project_back(place, grad_q, grad_own, grad_ahead, cosine, sine, x, near, far, *earlier):
    tokens, width = x.shape
    proj_width = (GROUP + 2) * HEAD_DIM
    bf16 = jnp.bfloat16
    return pl.pallas_call(
        project_back_kernel,
        in_specs=[spec_smem()]
        + [spec_vmem()] * 6
        + [spec_any()] * 4
        + [spec_any()] * len(earlier),
        out_specs=[spec_vmem()] * 3,
        out_shape=[
            shaped((tokens, proj_width), bf16),
            shaped((tokens, width), bf16),
            shaped((8, width), jnp.float32),
        ],
        scratch_shapes=[pltpu.VMEM((width, proj_width), bf16), pltpu.SemaphoreType.DMA((8,))],
        compiler_params=kernel_params(),
        cost_estimate=cost(2 * tokens * width * proj_width, 14_000_000),
        name="project_back",
    )(place, grad_q, grad_own, grad_ahead, cosine, sine, x, *near, *far, *earlier)


def stream_back_kernel(grad_in, x, gains, grad_mid, *rest):
    result = rest[-1]
    chunk = ROW_CHUNK

    @pl.loop(0, x.shape[0] // chunk, unroll=ROW_UNROLL)
    def _(step):
        rows = pl.ds(pl.multiple_of(step * chunk, chunk), chunk)
        stream = x[rows, :].astype(jnp.float32)
        upstream = grad_in[rows, :].astype(jnp.float32)
        pulled, _ = norm_pull(stream, row_scale(stream), gains[0:1, :], upstream)
        result[rows, :] = grad_mid[rows, :] + pulled


def stream_back(grad_in, x, gains, grad_mid, *earlier):
    tokens, width = x.shape
    tile = MID_ROWS
    rows = pl.BlockSpec((tile, width), lambda i: (i, 0))
    return pl.pallas_call(
        stream_back_kernel,
        grid=(tokens // tile,),
        in_specs=[rows, rows, whole((8, width)), rows] + [spec_any()] * len(earlier),
        out_specs=rows,
        out_shape=shaped((tokens, width), jnp.float32),
        compiler_params=kernel_params(),
        cost_estimate=cost(20 * tokens * width, 14_000_000),
        name="stream_back",
    )(grad_in, x, gains, grad_mid, *earlier)


def flat(values):
    rows, pair, width = values.shape
    lanes = width // 128
    if pair == 1:
        return values.reshape(rows * lanes, 128)
    tiles = with_layout_constraint(
        values.reshape(rows, pair, lanes, 128), Layout(major_to_minor=(0, 2, 1, 3))
    )
    return tiles.transpose(0, 2, 1, 3).reshape(rows * pair * lanes, 128)


def unflat(values, shape):
    rows, pair, width = shape
    lanes = width // 128
    if pair == 1:
        return values.reshape(shape)
    tiles = values.reshape(rows, lanes, pair, 128).transpose(0, 2, 1, 3)
    return with_layout_constraint(tiles, Layout(major_to_minor=(0, 2, 1, 3))).reshape(shape)


def join_kernel(*refs):
    result = refs[-1]
    for which in range(2):
        own, got, far = (refs[which * 3 + k][...].astype(jnp.float32) for k in range(3))
        result[:, which, :] = own + got + far


def join(gate, up):
    rows, width = gate[0].shape
    tile = 32
    block = pl.BlockSpec((tile, width), lambda i: (i, 0))
    return pl.pallas_call(
        join_kernel,
        grid=(rows // tile,),
        in_specs=[block] * 6,
        out_specs=pl.BlockSpec((tile, 2, width), lambda i: (i, 0, 0)),
        out_shape=shaped((rows, 2, width), jnp.float32),
        compiler_params=kernel_params(),
        cost_estimate=cost(0, 200_000_000),
        name="join",
    )(*gate, *up)


def adam_kernel(parts, decay, *refs):
    weight, first, second = (ref[...] for ref in refs[parts : parts + 3])
    outs = refs[parts + 3 :]
    grad = refs[0][...].astype(jnp.float32)
    for ref in refs[1:parts]:
        grad += ref[...].astype(jnp.float32)
    if parts > 1:
        outs[-1][...] = grad
    outs[0][...], outs[1][...], outs[2][...] = adam_step(weight, grad, first, second, decay)


def adam(grads, weight, first, second, decay):
    rows, width = weight.shape
    steps = 3 if rows * width < 1_000_000 else 6
    tile = rows // steps
    block = pl.BlockSpec((tile, width), lambda i: (i, 0))
    count = 3 if len(grads) == 1 else 4
    return pl.pallas_call(
        functools.partial(adam_kernel, len(grads), decay),
        grid=(steps,),
        in_specs=[block] * (len(grads) + 3),
        out_specs=[block] * count,
        out_shape=[shaped((rows, width), jnp.float32)] * count,
        compiler_params=kernel_params(),
        cost_estimate=cost(0, 200_000_000),
        name="adam",
    )(*grads, weight, first, second)


def on_square(
    layer_in,
    cotangent,
    qkv_weight,
    out_weight,
    gate_up_weight,
    down_weight,
    norm_gains,
    qkv_first,
    out_first,
    gate_up_first,
    down_first,
    gains_first,
    qkv_second,
    out_second,
    gate_up_second,
    down_second,
    gains_second,
):
    tok_rows = layer_in.shape[1]
    chip, core = lax.axis_index("batch"), lax.axis_index("seq")
    place = jnp.stack([chip, core]).astype(jnp.int32)
    plane = ("batch", "seq")
    stream, top = layer_in[0], cotangent[0]
    gains_cast = jnp.pad(norm_gains.T, ((0, 0), (0, 128 - norm_gains.shape[0])))
    attn_cast = jnp.concatenate([qkv_weight[:, 0], out_weight.T, gains_cast], axis=1)
    gate_cast = gate_up_weight[:, 0].astype(jnp.bfloat16)
    up_cast = gate_up_weight[:, 1].astype(jnp.bfloat16)
    down_cast = down_weight.T.astype(jnp.bfloat16)
    attn_cast = attn_cast.astype(jnp.bfloat16)
    first, gate_cast, up_cast, down_cast = lax.optimization_barrier(
        (trade(attn_cast, 0), gate_cast, up_cast, down_cast)
    )
    attn_pair = jnp.stack([attn_cast, first])
    near = (attn_pair, trade(attn_pair, 1))
    far = tuple(swap(part, "seq", 1) for part in near)
    down_one = trade(down_cast, 0)
    gate_one = trade(gate_cast, 0)
    down_pair, gate_pair = jnp.stack([down_cast, down_one]), jnp.stack([gate_cast, gate_one])
    down_pair_far, gate_pair_far = swap(down_pair, "seq", 1), swap(gate_pair, "seq", 1)
    down_two = trade(down_pair, 1)
    gate_two = trade(after(gate_pair, down_pair_far, gate_pair_far), 1)
    down_parts = (down_pair, down_two), (down_pair_far, swap(down_two, "seq", 1))
    gate_parts = (gate_pair, gate_two), (gate_pair_far, swap(gate_two, "seq", 1))
    up = lax.all_gather(up_cast, plane, axis=0, tiled=True)
    positions = core * tok_rows + jnp.arange(tok_rows, dtype=jnp.int32)
    cosine, sine = rope_tables(positions, HEAD_DIM)

    queries, pair, attn_in, gains = project(
        place, stream, near, far, cosine, sine, up_cast
    )
    behind = from_behind(pair, "seq", 1)
    attended, attn_part = attend(
        place, queries, pair, behind, near, far, stream.shape[1], down_one, gate_one
    )
    attn_out = tensor_sum(attn_part)
    ffn_in, hidden, by_gate, by_up, ffn_part = ffn_forward(
        place, attn_out, stream, gains, up, gate_parts, down_parts
    )
    ffn_out = tensor_sum(ffn_part)

    gate = arrange(place, *gate_parts)
    down = arrange(place, *down_parts)
    att_both = jnp.concatenate([attended, swap(attended, "seq", 1)], axis=0)
    attn_in_both = both_cores(attn_in)
    ffn_in_both = both_cores(ffn_in)
    hidden_both = jnp.concatenate([hidden, swap(hidden, "seq", 1)], axis=0)
    grad_ffn, grad_gate, grad_up, gain_ffn, grad_ffn_part = ffn_back(
        ffn_out, top, gains, gate, up, down, by_gate, by_up, att_both, attn_in_both, ffn_in_both,
        hidden_both
    )
    grad_ffn_in = tensor_sum(grad_ffn_part)
    grad_gate_both = jnp.concatenate([grad_gate, swap(grad_gate, "seq", 1)], axis=0)
    grad_up_both = jnp.concatenate([grad_up, swap(grad_up, "seq", 1)], axis=0)
    down_local = weight_local(both_cores(grad_ffn), hidden_both)
    gate_local = weight_local(ffn_in_both, grad_gate_both)
    up_local = weight_local(ffn_in_both, grad_up_both)
    down_state = scatter_begin(down_local)
    gate_state = scatter_begin(gate_local)
    up_got = trade(jnp.stack([up_local[1], up_local[3]]), 0)
    down_grad = scatter_end(down_state)

    grad_mid, grad_attn, grad_att, gain_mid = mid_back(
        place, grad_ffn_in, stream, attn_out, top, gains, near, far, down_state[2], gate_state[1]
    )
    gate_grad = scatter_end(gate_state)
    grad_q, grad_own, grad_old = attend_back(
        place, queries, pair, behind, attended, grad_att, cosine, sine
    )
    grad_ahead = from_behind(grad_old, "seq", -1)
    grad_proj, grad_attn_part, gain_attn = project_back(
        place, grad_q, grad_own, grad_ahead, cosine, sine, stream, near, far, down_grad[2], up_got
    )
    grad_attn_in = tensor_sum(grad_attn_part)
    grad_attn, gain_mid, up_got, down_grad = after(
        (grad_attn, gain_mid, up_got, down_grad), grad_attn_part
    )
    up_grad = scatter_end(scatter_begin(up_local, up_got))
    gate_up_grad = join(gate_grad, up_grad)

    out_local = weight_local(both_cores(grad_attn), att_both)
    out_grad = scatter_end(scatter_begin(out_local))
    proj_both = jnp.concatenate([grad_proj, swap(grad_proj, "seq", 1)], axis=0)
    qkv_local = weight_local(attn_in_both, proj_both)
    qkv_grad = sum(part.astype(jnp.float32) for part in scatter_end(scatter_begin(qkv_local)))[:, None]
    gains_rest = jnp.concatenate([gain_mid, gain_ffn[None]], axis=0).sum(axis=1)
    gains_rest = jnp.where(lax.axis_index("tensor") == 0, gains_rest, 0.0)
    gains_total = everywhere_sum(jnp.concatenate([gain_attn.sum(axis=0)[None], gains_rest], axis=0))
    own_columns = norm_gains.shape[1]
    gains_grad = lax.dynamic_slice_in_dim(
        gains_total, (chip * 2 + core) * own_columns, own_columns, axis=1
    )
    attn_float = attn_out.astype(jnp.float32)
    mid_stream = stream.astype(jnp.float32) + rms_norm(attn_float, gains[1])
    layer_out = (mid_stream + rms_norm(ffn_out.astype(jnp.float32), gains[3])).astype(jnp.bfloat16)
    qkv_shape, gate_up_shape = qkv_weight.shape, gate_up_weight.shape
    qkv_new, qkv_first_new, qkv_second_new = (
        unflat(value, qkv_shape)
        for value in adam(
            [flat(qkv_grad)], flat(qkv_weight), flat(qkv_first), flat(qkv_second), decay_rate
        )
    )
    out_new, out_first_new, out_second_new, out_grad = adam(
        out_grad, out_weight.T, out_first.T, out_second.T, decay_rate
    )
    gate_up_new, gate_up_first_new, gate_up_second_new = (
        unflat(value, gate_up_shape)
        for value in adam(
            [flat(gate_up_grad)],
            flat(gate_up_weight),
            flat(gate_up_first),
            flat(gate_up_second),
            decay_rate,
        )
    )
    down_new, down_first_new, down_second_new, down_grad = adam(
        down_grad, down_weight.T, down_first.T, down_second.T, decay_rate
    )
    gains_new, gains_first_new, gains_second_new = adam_step(
        norm_gains, gains_grad, gains_first, gains_second, 0.0
    )
    input_grad = stream_back(
        grad_attn_in, stream, gains, grad_mid, qkv_new, out_new, gate_up_new, down_new, gains_new
    )
    return (
        layer_out[None],
        input_grad[None],
        qkv_grad,
        out_grad.T,
        gate_up_grad,
        down_grad.T,
        gains_grad,
        qkv_new,
        out_new.T,
        gate_up_new,
        down_new.T,
        gains_new,
        qkv_first_new,
        out_first_new.T,
        gate_up_first_new,
        down_first_new.T,
        gains_first_new,
        qkv_second_new,
        out_second_new.T,
        gate_up_second_new,
        down_second_new.T,
        gains_second_new,
    )


def on_device(
    layer_in,
    cotangent,
    qkv_weight,
    out_weight,
    gate_up_weight,
    down_weight,
    norm_gains,
    qkv_first,
    out_first,
    gate_up_first,
    down_first,
    gains_first,
    qkv_second,
    out_second,
    gate_up_second,
    down_second,
    gains_second,
):
    tok_rows = layer_in.shape[1]
    seq_index = lax.axis_index("seq")
    collected = (
        lax.all_gather(qkv_weight.astype(jnp.bfloat16), ("batch", "seq"), axis=0, tiled=True),
        lax.all_gather(out_weight.astype(jnp.bfloat16), ("batch", "seq"), axis=1, tiled=True),
        lax.all_gather(gate_up_weight.astype(jnp.bfloat16), ("batch", "seq"), axis=0, tiled=True),
        lax.all_gather(down_weight.astype(jnp.bfloat16), ("batch", "seq"), axis=1, tiled=True),
        lax.all_gather(norm_gains.astype(jnp.bfloat16), ("batch", "seq"), axis=1, tiled=True),
    )
    qkv_full, out_full, gate_up_full, down_full, gains_full = collected
    model_width = qkv_full.shape[0]
    kv_local = qkv_full.shape[1]
    heads_local = kv_local * GROUP
    ffn_local = gate_up_full.shape[2]
    qkv_flat = qkv_full.reshape(model_width, kv_local * (GROUP + 2) * HEAD_DIM)
    gate_up_flat = gate_up_full.reshape(model_width, 2 * ffn_local)
    gains_float = gains_full.astype(jnp.float32)
    positions = seq_index * tok_rows + jnp.arange(tok_rows, dtype=jnp.int32)
    cosine, sine = rope_tables(positions, HEAD_DIM)
    key_positions = (seq_index - WIN_BLOCKS) * tok_rows + jnp.arange(
        (WIN_BLOCKS + 1) * tok_rows, dtype=jnp.int32
    )
    spread = positions[:, None] - key_positions[None, :]
    allowed = (spread >= 0) & (spread < WIN_BLOCKS * tok_rows) & (key_positions >= 0)[None, :]
    mask = allowed[None, None]
    stream = layer_in[0].astype(jnp.float32)
    attn_in = rms_norm(stream, gains_float[0]).astype(jnp.bfloat16)
    projected = jnp.dot(attn_in, qkv_flat, preferred_element_type=jnp.float32).reshape(
        tok_rows, kv_local, GROUP + 2, HEAD_DIM
    )
    queries = rotate(
        projected[:, :, :GROUP].reshape(tok_rows, heads_local, HEAD_DIM), cosine, sine
    ).astype(jnp.bfloat16)
    keys = rotate(projected[:, :, GROUP], cosine, sine).astype(jnp.bfloat16)
    values = projected[:, :, GROUP + 1].astype(jnp.bfloat16)
    kv_pair = jnp.stack([keys, values], axis=0)
    reach = min(WIN_BLOCKS, lax.axis_size("seq") - 1)
    pieces = []
    for distance in range(WIN_BLOCKS, 0, -1):
        if distance <= reach:
            pieces.append(from_behind(kv_pair, "seq", distance))
        else:
            pieces.append(jnp.zeros_like(kv_pair))
    pieces.append(kv_pair)
    extended = jnp.concatenate(pieces, axis=1)
    ext_keys = extended[0]
    ext_values = extended[1]
    query_groups = queries.reshape(tok_rows, kv_local, GROUP, HEAD_DIM)
    capped = capped_scores(query_groups, ext_keys)
    log_sums = jnp.log(jnp.sum(jnp.where(mask, jnp.exp(capped), 0.0), axis=-1))
    probs = jnp.where(mask, jnp.exp(capped - log_sums[..., None]), 0.0).astype(jnp.bfloat16)
    attended = jnp.einsum(
        "cgij,jcd->icgd", probs, ext_values, preferred_element_type=jnp.float32
    ).astype(jnp.bfloat16)
    att_flat = attended.reshape(tok_rows, heads_local * HEAD_DIM)
    attn_out = lax.psum(jnp.dot(att_flat, out_full, preferred_element_type=jnp.float32), "tensor")
    mid_stream = stream + rms_norm(attn_out, gains_float[1])
    ffn_in = rms_norm(mid_stream, gains_float[2]).astype(jnp.bfloat16)
    gate_up = jnp.dot(ffn_in, gate_up_flat, preferred_element_type=jnp.float32).reshape(
        tok_rows, 2, ffn_local
    )
    hidden = geglu(gate_up[:, 0], gate_up[:, 1]).astype(jnp.bfloat16)
    ffn_out = lax.psum(jnp.dot(hidden, down_full, preferred_element_type=jnp.float32), "tensor")
    layer_out = (mid_stream + rms_norm(ffn_out, gains_float[3])).astype(jnp.bfloat16)
    grad_top = cotangent[0].astype(jnp.float32)
    grad_ffn_out, gain_three = norm_back(ffn_out, gains_float[3], grad_top)
    grad_ffn = grad_ffn_out.astype(jnp.bfloat16)
    grad_hidden = cols_product(grad_ffn, down_full)
    _, geglu_pull = jax.vjp(geglu, gate_up[:, 0], gate_up[:, 1])
    grad_gate, grad_up = geglu_pull(grad_hidden)
    grad_gate_up = (
        jnp.stack([grad_gate, grad_up], axis=1)
        .reshape(tok_rows, 2 * ffn_local)
        .astype(jnp.bfloat16)
    )
    grad_ffn_in = lax.psum(cols_product(grad_gate_up, gate_up_flat), "tensor")
    grad_mid_norm, gain_two = norm_back(mid_stream, gains_float[2], grad_ffn_in)
    grad_mid = grad_top + grad_mid_norm
    grad_attn_out, gain_one = norm_back(attn_out, gains_float[1], grad_mid)
    grad_attn = grad_attn_out.astype(jnp.bfloat16)
    grad_att = (
        cols_product(grad_attn, out_full)
        .astype(jnp.bfloat16)
        .reshape(tok_rows, kv_local, GROUP, HEAD_DIM)
    )
    capped_again = capped_scores(query_groups, ext_keys)
    probs_float = jnp.where(mask, jnp.exp(capped_again - log_sums[..., None]), 0.0)
    probs_again = probs_float.astype(jnp.bfloat16)
    delta = jnp.einsum("icgd,icgd->cgi", grad_att, attended, preferred_element_type=jnp.float32)
    grad_probs = jnp.einsum(
        "icgd,jcd->cgij", grad_att, ext_values, preferred_element_type=jnp.float32
    )
    grad_scores = (
        probs_float * (grad_probs - delta[..., None]) * (1.0 - (capped_again / soft_cap) ** 2)
    ).astype(jnp.bfloat16)
    score_scale = HEAD_DIM ** (-0.5)
    grad_values_ext = jnp.einsum(
        "cgij,icgd->jcd", probs_again, grad_att, preferred_element_type=jnp.float32
    )
    grad_keys_ext = (
        jnp.einsum("cgij,icgd->jcd", grad_scores, query_groups, preferred_element_type=jnp.float32)
        * score_scale
    )
    grad_queries = (
        jnp.einsum("cgij,jcd->icgd", grad_scores, ext_keys, preferred_element_type=jnp.float32)
        * score_scale
    )
    grad_pair_ext = jnp.stack([grad_keys_ext, grad_values_ext], axis=0)
    grad_pair = grad_pair_ext[:, WIN_BLOCKS * tok_rows :]
    for distance in range(1, reach + 1):
        start = (WIN_BLOCKS - distance) * tok_rows
        piece = grad_pair_ext[:, start : start + tok_rows]
        grad_pair = grad_pair + from_behind(piece.astype(jnp.bfloat16), "seq", -distance).astype(
            piece.dtype
        )
    grad_queries = rotate(
        grad_queries.reshape(tok_rows, heads_local, HEAD_DIM), cosine, -sine
    ).reshape(tok_rows, kv_local, GROUP, HEAD_DIM)
    grad_keys = rotate(grad_pair[0], cosine, -sine)
    grad_values = grad_pair[1]
    grad_proj = (
        jnp.concatenate([grad_queries, grad_keys[:, :, None], grad_values[:, :, None]], axis=2)
        .reshape(tok_rows, kv_local * (GROUP + 2) * HEAD_DIM)
        .astype(jnp.bfloat16)
    )
    grad_attn_in = lax.psum(
        cols_product(grad_proj, qkv_flat).astype(jnp.bfloat16), "tensor"
    ).astype(jnp.float32)
    grad_stream_norm, gain_zero = norm_back(stream, gains_float[0], grad_attn_in)
    input_grad = grad_mid + grad_stream_norm
    qkv_local = rows_product(attn_in, grad_proj).reshape(
        model_width, kv_local, (GROUP + 2) * HEAD_DIM
    )
    out_local = rows_product(att_flat, grad_attn)
    gate_up_local = rows_product(ffn_in, grad_gate_up).reshape(model_width, 2, ffn_local)
    down_local = rows_product(hidden, grad_ffn)
    gains_local = jnp.stack([gain_zero, gain_one, gain_two, gain_three])
    summed = (
        lax.psum_scatter(
            qkv_local.astype(jnp.bfloat16), ("batch", "seq"), scatter_dimension=0, tiled=True
        ).astype(jnp.float32),
        lax.psum_scatter(
            out_local.astype(jnp.bfloat16), ("batch", "seq"), scatter_dimension=1, tiled=True
        ).astype(jnp.float32),
        lax.psum_scatter(
            gate_up_local.astype(jnp.bfloat16), ("batch", "seq"), scatter_dimension=0, tiled=True
        ).astype(jnp.float32),
        lax.psum_scatter(
            down_local.astype(jnp.bfloat16), ("batch", "seq"), scatter_dimension=1, tiled=True
        ).astype(jnp.float32),
        lax.psum_scatter(
            gains_local.astype(jnp.bfloat16), ("batch", "seq"), scatter_dimension=1, tiled=True
        ).astype(jnp.float32),
    )
    qkv_grad, out_grad, gate_up_grad, down_grad, gains_grad = summed
    qkv_new, qkv_first_new, qkv_second_new = adam_step(
        qkv_weight, qkv_grad, qkv_first, qkv_second, decay_rate
    )
    out_new, out_first_new, out_second_new = adam_step(
        out_weight, out_grad, out_first, out_second, decay_rate
    )
    gate_up_new, gate_up_first_new, gate_up_second_new = adam_step(
        gate_up_weight, gate_up_grad, gate_up_first, gate_up_second, decay_rate
    )
    down_new, down_first_new, down_second_new = adam_step(
        down_weight, down_grad, down_first, down_second, decay_rate
    )
    gains_new, gains_first_new, gains_second_new = adam_step(
        norm_gains, gains_grad, gains_first, gains_second, 0.0
    )
    return (
        layer_out[None],
        input_grad[None],
        qkv_grad,
        out_grad,
        gate_up_grad,
        down_grad,
        gains_grad,
        qkv_new,
        out_new,
        gate_up_new,
        down_new,
        gains_new,
        qkv_first_new,
        out_first_new,
        gate_up_first_new,
        down_first_new,
        gains_first_new,
        qkv_second_new,
        out_second_new,
        gate_up_second_new,
        down_second_new,
        gains_second_new,
    )


def solution(mesh):
    in_specs = (
        P("batch", "seq", None),
        P("batch", "seq", None),
        P(("batch", "seq"), "tensor", None),
        P("tensor", ("batch", "seq")),
        P(("batch", "seq"), None, "tensor"),
        P("tensor", ("batch", "seq")),
        P(None, ("batch", "seq")),
        P(("batch", "seq"), "tensor", None),
        P("tensor", ("batch", "seq")),
        P(("batch", "seq"), None, "tensor"),
        P("tensor", ("batch", "seq")),
        P(None, ("batch", "seq")),
        P(("batch", "seq"), "tensor", None),
        P("tensor", ("batch", "seq")),
        P(("batch", "seq"), None, "tensor"),
        P("tensor", ("batch", "seq")),
        P(None, ("batch", "seq")),
    )
    out_specs = (
        P("batch", "seq", None),
        P("batch", "seq", None),
        P(("batch", "seq"), "tensor", None),
        P("tensor", ("batch", "seq")),
        P(("batch", "seq"), None, "tensor"),
        P("tensor", ("batch", "seq")),
        P(None, ("batch", "seq")),
        P(("batch", "seq"), "tensor", None),
        P("tensor", ("batch", "seq")),
        P(("batch", "seq"), None, "tensor"),
        P("tensor", ("batch", "seq")),
        P(None, ("batch", "seq")),
        P(("batch", "seq"), "tensor", None),
        P("tensor", ("batch", "seq")),
        P(("batch", "seq"), None, "tensor"),
        P("tensor", ("batch", "seq")),
        P(None, ("batch", "seq")),
        P(("batch", "seq"), "tensor", None),
        P("tensor", ("batch", "seq")),
        P(("batch", "seq"), None, "tensor"),
        P("tensor", ("batch", "seq")),
        P(None, ("batch", "seq")),
    )
    sizes = tuple(mesh.shape[axis] for axis in ("batch", "seq", "tensor"))
    body = on_square if sizes == (4, 2, 4) else on_device
    return jax.shard_map(
        body, mesh=mesh, in_specs=in_specs, out_specs=out_specs, check_vma=False
    )
```

```python
import functools
import jax
import jax.numpy as jnp
from jax import lax
from jax.experimental.layout import Layout, with_layout_constraint
from jax.experimental import pallas as pl
from jax.experimental.pallas import tpu as pltpu
from jax.sharding import PartitionSpec as P

HEAD_DIM = 256
WIN_BLOCKS = 4
STEP = 10
GROUP = 2


norm_eps = 1e-06
soft_cap = 50.0
learn_rate = 0.02
decay_rate = 0.1
beta_first = 0.9
beta_second = 0.95
adam_eps = 1e-08
gelu_coef = 0.7978845608028654


def from_behind(value, axis, steps):
    count = lax.axis_size(axis)
    initial, last = (max(0, -steps), min(count, count - steps))
    return lax.ppermute(value, axis, [(source, source + steps) for source in range(initial, last)])


def rms_norm(values, gain):
    scale = lax.rsqrt(jnp.mean(values * values, axis=-1, keepdims=True) + norm_eps)
    return values * scale * (1.0 + gain)


def norm_back(values, gain, upstream):
    _, pullback = jax.vjp(rms_norm, values, gain)
    return pullback(upstream)


def gelu_tanh(values):
    inner = gelu_coef * (values + 0.044715 * values * values * values)
    return 0.5 * values * (1.0 + jnp.tanh(inner))


def geglu(gate, up_part):
    return gelu_tanh(gate) * up_part


def rope_tables(positions, head_size):
    half = head_size // 2
    exponent = jnp.arange(half, dtype=jnp.float32) * (2.0 / head_size)
    freqs = 10000.0 ** (-exponent)
    angles = positions.astype(jnp.float32)[:, None] * freqs[None, :]
    return (jnp.cos(angles), jnp.sin(angles))


def rotate(values, cosine, sine):
    half = values.shape[-1] // 2
    first = values[..., :half]
    second = values[..., half:]
    cosine = cosine[:, None, :]
    sine = sine[:, None, :]
    return jnp.concatenate(
        [first * cosine - second * sine, second * cosine + first * sine], axis=-1
    )


def adam_step(weight, grad, first, second, decay):
    first_new = beta_first * first + (1.0 - beta_first) * grad
    second_new = beta_second * second + (1.0 - beta_second) * grad * grad
    first_hat = first_new / (1.0 - beta_first**STEP)
    second_hat = second_new / (1.0 - beta_second**STEP)
    weight_new = weight - learn_rate * (
        first_hat / (jnp.sqrt(second_hat) + adam_eps) + decay * weight
    )
    return (weight_new, first_new, second_new)


def rows_product(left, right):
    return lax.dot_general(
        left, right, (((0,), (0,)), ((), ())), preferred_element_type=jnp.float32
    )


def cols_product(left, right):
    return lax.dot_general(
        left, right, (((1,), (1,)), ((), ())), preferred_element_type=jnp.float32
    )


def capped_scores(query_groups, ext_keys):
    raw = jnp.einsum(
        "icgd,jcd->cgij", query_groups, ext_keys, preferred_element_type=jnp.float32
    ) * query_groups.shape[-1] ** (-0.5)
    return soft_cap * jnp.tanh(raw / soft_cap)


def tensor_sum(part):
    return lax.psum(part, "tensor")


def swap(value, axis, bit):
    count = lax.axis_size(axis)
    return lax.ppermute(value, axis, [(source, source ^ bit) for source in range(count)])


def after(value, *earlier):
    return lax.optimization_barrier((value, earlier))[0]


def trade(value, turn):
    pairs = []
    for chip in range(4):
        for core in range(2):
            pairs.append((chip * 2 + core, (chip ^ (1 + (core ^ turn))) * 2 + core))
    return lax.ppermute(value, ("batch", "seq"), pairs)


def offsets(owner):
    return (0, 1 + owner, 2 - owner, 3)


def own_blocks(wide):
    tokens, width = wide.shape
    chip, core = lax.axis_index("batch"), lax.axis_index("seq")
    split = wide.reshape(tokens, 8, width // 8)
    halves = []
    for owner in (core, 1 - core):
        parts = [
            lax.dynamic_index_in_dim(split, (chip ^ offset) * 2 + owner, 1, keepdims=False)
            for offset in offsets(owner)
        ]
        halves.append(jnp.concatenate(parts, axis=1))
    return halves


def both_cores(wide):
    mine, theirs = own_blocks(wide)
    return jnp.concatenate([mine, swap(theirs, "seq", 1)], axis=0)


def weight_local(wide, narrow):
    local = rows_product(wide, narrow).astype(jnp.bfloat16)
    return local.reshape(4, -1, local.shape[1])


def scatter_begin(local, got=None):
    if got is None:
        got = trade(jnp.stack([local[1], local[3]]), 0)
    far = local[2].astype(jnp.float32) + got[1].astype(jnp.float32)
    return local, got, far.astype(jnp.bfloat16)


def scatter_end(state):
    local, got, far = state
    return local[0], got[0], trade(far, 1)


def everywhere_sum(value):
    for axis, bit in (("seq", 1), ("batch", 1), ("batch", 2), ("tensor", 1), ("tensor", 2)):
        value = value + swap(value, axis, bit)
    return value


FFN_TILE = 768
ROW_CHUNK = 16
ROW_UNROLL = 4
MID_ROWS = 128


def spec_any():
    return pl.BlockSpec(memory_space=pl.ANY)


def spec_vmem():
    return pl.BlockSpec(memory_space=pltpu.VMEM)


def spec_smem():
    return pl.BlockSpec(memory_space=pltpu.SMEM)


def kernel_params():
    return pltpu.CompilerParams(vmem_limit_bytes=56 * 1024 * 1024)


def cost(flops, moved):
    return pl.CostEstimate(flops=flops, bytes_accessed=moved, transcendentals=0)


def shaped(shape, kind):
    return jax.ShapeDtypeStruct(shape, kind)


def dot_nn(left, right):
    return lax.dot_general(
        left, right, (((1,), (0,)), ((), ())), preferred_element_type=jnp.float32
    )


def dot_nt(left, right):
    return lax.dot_general(
        left, right, (((1,), (1,)), ((), ())), preferred_element_type=jnp.float32
    )


def dot_tn(left, right):
    return lax.dot_general(
        left, right, (((0,), (0,)), ((), ())), preferred_element_type=jnp.float32
    )


def row_scale(values):
    return lax.rsqrt(jnp.mean(values * values, axis=-1, keepdims=True) + norm_eps)


def norm_pull(values, scale, gain, upstream):
    normed = values * scale
    inner = upstream * (1.0 + gain)
    pulled = scale * (inner - normed * jnp.mean(normed * inner, axis=-1, keepdims=True))
    return pulled, upstream * normed


def fold_rows(values):
    total = values[:8]
    for start in range(8, values.shape[0], 8):
        total += values[start : start + 8]
    return total


def fetch_rows(place, near, far, target, sems, column, columns):
    chip, core = place[0], place[1]
    rows = near[0].shape[1]
    copies = []
    for which, (one, two) in enumerate((near, far)):
        owner = which ^ core
        blocks = ((one.at[0], 0), (one.at[1], 1 + owner), (two.at[0], 2 - owner), (two.at[1], 3))
        for block, offset in blocks:
            row = ((offset ^ chip) * 2 + owner) * rows
            copies.append(
                pltpu.make_async_copy(
                    block.at[:, pl.ds(column, columns)],
                    target.at[pl.ds(pl.multiple_of(row, 16), rows), :],
                    sems.at[len(copies)],
                )
            )
    return copies


def rope(values, cosine, sine):
    half = HEAD_DIM // 2
    first, second = values[:, :half], values[:, half:]
    return jnp.concatenate(
        [first * cosine - second * sine, second * cosine + first * sine], axis=1
    )


def arrange_kernel(place, one, two, one_far, two_far, result, sems):
    copies = fetch_rows(place, (one, two), (one_far, two_far), result, sems, 0, result.shape[1])
    for copy in copies:
        copy.start()
    for copy in copies:
        copy.wait()


def arrange(place, near, far):
    return pl.pallas_call(
        arrange_kernel,
        in_specs=[spec_smem()] + [spec_any()] * 4,
        out_specs=spec_vmem(),
        out_shape=shaped((8 * near[0].shape[1], near[0].shape[2]), jnp.bfloat16),
        scratch_shapes=[pltpu.SemaphoreType.DMA((8,))],
        compiler_params=kernel_params(),
        cost_estimate=cost(0, 16 * near[0].size),
        name="arrange",
    )(place, *near, *far)


def project_kernel(place, x, one, two, one_far, two_far, cosine, sine, *rest):
    queries, pair, attn_in, gains, weight, sems = rest[-6:]
    copies = fetch_rows(place, (one, two), (one_far, two_far), weight, sems, 0, weight.shape[1])
    for copy in copies:
        copy.start()
    for copy in copies:
        copy.wait()
    width = (GROUP + 2) * HEAD_DIM
    tail = weight[:, width + GROUP * HEAD_DIM :].astype(jnp.float32)
    gains[...] = jnp.transpose(tail)[:8]
    gain = 1.0 + gains[0:1, :]
    chunk = ROW_CHUNK

    @pl.loop(0, x.shape[0] // chunk, unroll=ROW_UNROLL)
    def _(step):
        rows = pl.ds(pl.multiple_of(step * chunk, chunk), chunk)
        stream = x[rows, :].astype(jnp.float32)
        attn_in[rows, :] = (stream * row_scale(stream) * gain).astype(jnp.bfloat16)

    for member in range(GROUP + 2):
        columns = slice(member * HEAD_DIM, (member + 1) * HEAD_DIM)
        part = dot_nn(attn_in[...], weight[:, columns])
        if member < GROUP:
            queries[:, columns] = rope(part, cosine[...], sine[...]).astype(jnp.bfloat16)
        elif member == GROUP:
            pair[0] = rope(part, cosine[...], sine[...]).astype(jnp.bfloat16)
        else:
            pair[1] = part.astype(jnp.bfloat16)


def project(place, x, near, far, cosine, sine, *earlier):
    tokens, width = x.shape
    bf16 = jnp.bfloat16
    return pl.pallas_call(
        project_kernel,
        in_specs=[spec_smem(), spec_vmem()]
        + [spec_any()] * 4
        + [spec_vmem()] * 2
        + [spec_any()] * len(earlier),
        out_specs=[spec_vmem()] * 4,
        out_shape=[
            shaped((tokens, GROUP * HEAD_DIM), bf16),
            shaped((2, tokens, HEAD_DIM), bf16),
            shaped((tokens, width), bf16),
            shaped((8, width), jnp.float32),
        ],
        scratch_shapes=[pltpu.VMEM((width, near[0].shape[2]), bf16), pltpu.SemaphoreType.DMA((8,))],
        compiler_params=kernel_params(),
        cost_estimate=cost(2 * tokens * width * 1024, 12_000_000),
        name="project",
    )(place, x, *near, *far, cosine, sine, *earlier)


def chunk_scores(query, key, behind, row, core):
    raw = dot_nt(query, key) * (HEAD_DIM**-0.5 / soft_cap)
    bent = jnp.tanh(raw)
    powers = jnp.exp(soft_cap * bent)
    if behind:
        powers = jnp.where(core > 0, powers, 0.0)
    else:
        at = row + lax.broadcasted_iota(jnp.int32, powers.shape, 0)
        powers = jnp.where(at >= lax.broadcasted_iota(jnp.int32, powers.shape, 1), powers, 0.0)
    return bent, powers


def attend_kernel(place, queries, pair, behind, one, two, one_far, two_far, *rest):
    attended, result, weight, sems = rest[-4:]
    width = (GROUP + 2) * HEAD_DIM
    copies = fetch_rows(place, (one, two), (one_far, two_far), weight, sems, width, GROUP * HEAD_DIM)
    for copy in copies:
        copy.start()
    core = place[1]
    chunk = 128
    tokens = queries.shape[0]
    for start in range(0, tokens, chunk):
        rows = slice(start, start + chunk)
        keys = start + chunk
        for head in range(GROUP):
            columns = slice(head * HEAD_DIM, (head + 1) * HEAD_DIM)
            query = queries[rows, columns]
            _, old = chunk_scores(query, behind[0], True, start, core)
            _, new = chunk_scores(query, pair[0, :keys], False, start, core)
            total = jnp.sum(old, axis=-1, keepdims=True) + jnp.sum(new, axis=-1, keepdims=True)
            share = 1.0 / total
            value = dot_nn((old * share).astype(jnp.bfloat16), behind[1])
            value += dot_nn((new * share).astype(jnp.bfloat16), pair[1, :keys])
            attended[rows, columns] = value.astype(jnp.bfloat16)
    for copy in copies:
        copy.wait()
    tile = 768
    for column in range(0, result.shape[1], tile):
        part = dot_nt(attended[...], weight[column : column + tile, :])
        result[:, column : column + tile] = part.astype(jnp.bfloat16)


def attend(place, queries, pair, behind, near, far, width, *earlier):
    tokens = queries.shape[0]
    bf16 = jnp.bfloat16
    return pl.pallas_call(
        attend_kernel,
        in_specs=[spec_smem()] + [spec_vmem()] * 3 + [spec_any()] * (4 + len(earlier)),
        out_specs=[spec_vmem()] * 2,
        out_shape=[shaped((tokens, GROUP * HEAD_DIM), bf16), shaped((tokens, width), bf16)],
        scratch_shapes=[
            pltpu.VMEM((width, GROUP * HEAD_DIM), bf16),
            pltpu.SemaphoreType.DMA((8,)),
        ],
        compiler_params=kernel_params(),
        cost_estimate=cost(4 * tokens * width * 1024, 8_000_000),
        name="attend",
    )(place, queries, pair, behind, *near, *far, *earlier)


def whole(shape):
    return pl.BlockSpec(shape, lambda *_: (0,) * len(shape))


def ffn_params():
    return pltpu.CompilerParams(vmem_limit_bytes=58 * 1024 * 1024)


def move(source, target, sem):
    copy = pltpu.make_async_copy(source, target, sem)
    copy.start()
    return copy


def ffn_kernel(place, attn_out, x, gains, up_full, *rest):
    gate_near, gate_far, down_near, down_far = (rest[k : k + 2] for k in (0, 2, 4, 6))
    outs, (sides, gate_up_here, down_here, in_sems, down_sems, out_sems) = rest[-11:-6], rest[-6:]
    ffn_in, hidden, by_gate, by_up, result = (sides.at[k] for k in range(5))
    tokens, width = x.shape
    units = up_full.shape[1]
    tile = FFN_TILE
    steps, turns = units // tile, width // tile

    def load(step):
        columns = pl.ds(pl.multiple_of(step * tile, tile), tile)
        up_copy = pltpu.make_async_copy(
            up_full.at[:, columns], gate_up_here.at[1, :, columns], in_sems.at[step, 8]
        )
        target = gate_up_here.at[0, :, columns]
        return [up_copy] + fetch_rows(
            place, gate_near, gate_far, target, in_sems.at[step], columns.start, tile
        )

    down_copies = fetch_rows(place, down_near, down_far, down_here, down_sems, 0, units)
    for step in range(steps):
        for copy in load(step):
            copy.start()
    for copy in down_copies:
        copy.start()
    chunk = ROW_CHUNK

    @pl.loop(0, tokens // chunk, unroll=ROW_UNROLL)
    def _(step):
        rows = pl.ds(pl.multiple_of(step * chunk, chunk), chunk)
        out = attn_out[rows, :].astype(jnp.float32)
        mid = x[rows, :].astype(jnp.float32) + out * row_scale(out) * (1.0 + gains[1:2, :])
        ffn_in[rows, :] = (mid * row_scale(mid) * (1.0 + gains[2:3, :])).astype(jnp.bfloat16)

    stores = [move(ffn_in, outs[0], out_sems.at[0])]

    @pl.loop(0, steps)
    def _(step):
        for copy in load(step):
            copy.wait()
        columns = pl.ds(pl.multiple_of(step * tile, tile), tile)
        for rows in (slice(None),):
            value = ffn_in[...]
            gate = dot_nn(value, gate_up_here[0, :, columns])
            up = dot_nn(value, gate_up_here[1, :, columns])
            square_of = gate * gate
            bent = jnp.tanh(gate * (gelu_coef + gelu_coef * 0.044715 * square_of))
            half = 0.5 + 0.5 * bent
            curve = gate * half
            slope = half + curve * (1.0 - bent) * (
                gelu_coef + 3.0 * gelu_coef * 0.044715 * square_of
            )
            hidden[rows, columns] = (curve * up).astype(jnp.bfloat16)
            by_gate[rows, columns] = (slope * up).astype(jnp.bfloat16)
            by_up[rows, columns] = curve.astype(jnp.bfloat16)

    for k, side in ((1, hidden), (2, by_gate), (3, by_up)):
        stores.append(move(side, outs[k], out_sems.at[k]))

    def store(turn):
        columns = pl.ds(pl.multiple_of(turn * tile, tile), tile)
        return pltpu.make_async_copy(
            result.at[:, columns], outs[4].at[:, columns], out_sems.at[4 + turn]
        )

    for copy in down_copies:
        copy.wait()

    @pl.loop(0, turns)
    def _(turn):
        rows = pl.ds(pl.multiple_of(turn * tile, tile), tile)
        result[:, rows] = dot_nt(hidden[...], down_here[rows, :]).astype(jnp.bfloat16)
        store(turn).start()

    for copy in stores:
        copy.wait()
    for turn in range(turns):
        store(turn).wait()


def ffn_forward(place, attn_out, x, gains, up, gate, down):
    tokens, width = x.shape
    units = up.shape[1]
    bf16 = jnp.bfloat16
    return pl.pallas_call(
        ffn_kernel,
        in_specs=[spec_smem()] + [spec_vmem()] * 3 + [spec_any()] * 9,
        out_specs=[spec_any()] * 5,
        out_shape=[shaped((tokens, width), bf16)]
        + [shaped((tokens, units), bf16)] * 3
        + [shaped((tokens, width), bf16)],
        scratch_shapes=[
            pltpu.VMEM((5, tokens, width), bf16),
            pltpu.VMEM((2, width, units), bf16),
            pltpu.VMEM((width, units), bf16),
            pltpu.SemaphoreType.DMA((units // FFN_TILE, 9)),
            pltpu.SemaphoreType.DMA((8,)),
            pltpu.SemaphoreType.DMA((4 + width // FFN_TILE,)),
        ],
        compiler_params=ffn_params(),
        cost_estimate=cost(6 * tokens * width * units, 50_000_000),
        name="ffn_forward",
    )(place, attn_out, x, gains, up, *gate[0], *gate[1], *down[0], *down[1])


def ffn_back_kernel(ffn_out, top, gains, gate, up_full, down, by_gate, by_up, *rest):
    grad_out, gate_out, up_out, gain_out, result_out = rest[-13:-8]
    sides, grads, gate_up_here, down_here, in_sems, down_sems, gate_sems, out_sems = rest[-8:]
    grad_ffn, result = sides.at[0], sides.at[1]
    tokens, width = top.shape
    units = gate.shape[1]
    grad_gate, grad_up = grads.at[:, pl.ds(0, units)], grads.at[:, pl.ds(units, units)]
    tile = FFN_TILE
    steps, turns = units // tile, width // tile

    def load_down(step):
        columns = pl.ds(pl.multiple_of(step * tile, tile), tile)
        return pltpu.make_async_copy(
            down.at[:, columns], down_here.at[:, columns], down_sems.at[step]
        )

    def load(turn, which):
        rows = pl.ds(pl.multiple_of(turn * tile, tile), tile)
        return pltpu.make_async_copy(
            (gate, up_full)[which].at[rows, :],
            gate_up_here.at[rows, pl.ds(which * units, units)],
            gate_sems.at[turn, which],
        )

    load_down(0).start()
    factors = [
        move(by_gate, grad_gate, in_sems.at[0]),
        move(by_up, grad_up, in_sems.at[1]),
    ]
    load_down(1).start()
    gain_out[...] = jnp.zeros_like(gain_out)
    chunk = ROW_CHUNK

    @pl.loop(0, tokens // chunk, unroll=ROW_UNROLL)
    def _(step):
        rows = pl.ds(pl.multiple_of(step * chunk, chunk), chunk)
        out = ffn_out[rows, :].astype(jnp.float32)
        upstream = top[rows, :].astype(jnp.float32)
        pulled, product = norm_pull(out, row_scale(out), gains[3:4, :], upstream)
        grad_ffn[rows, :] = pulled.astype(jnp.bfloat16)
        gain_out[...] += fold_rows(product)

    stores = [move(grad_ffn, grad_out, out_sems.at[0])]
    for copy in factors:
        copy.wait()

    @pl.loop(0, steps)
    def _(step):
        load_down(step).wait()

        @pl.when(step + 2 < steps)
        def _():
            load_down(step + 2).start()

        @pl.when(step + 2 >= steps)
        def _():
            load(step + 2 - steps, 0).start()
            load(step + 2 - steps, 1).start()

        columns = pl.ds(pl.multiple_of(step * tile, tile), tile)
        for start in range(0, tokens, tokens // 2):
            rows = pl.ds(start, tokens // 2)
            grad_hidden = dot_nn(grad_ffn[rows, :], down_here[:, columns])
            one = grad_hidden * grad_gate[rows, columns].astype(jnp.float32)
            two = grad_hidden * grad_up[rows, columns].astype(jnp.float32)
            grad_gate[rows, columns] = one.astype(jnp.bfloat16)
            grad_up[rows, columns] = two.astype(jnp.bfloat16)

    stores.append(move(grad_gate, gate_out, out_sems.at[1]))
    stores.append(move(grad_up, up_out, out_sems.at[2]))

    def store(turn):
        columns = pl.ds(pl.multiple_of(turn * tile, tile), tile)
        return pltpu.make_async_copy(
            result.at[:, columns], result_out.at[:, columns], out_sems.at[3 + turn]
        )

    @pl.loop(0, turns)
    def _(turn):
        load(turn, 0).wait()
        load(turn, 1).wait()

        @pl.when(turn + 2 < turns)
        def _():
            load(turn + 2, 0).start()
            load(turn + 2, 1).start()

        rows = pl.ds(pl.multiple_of(turn * tile, tile), tile)
        part = dot_nt(grads[...], gate_up_here[rows, :])
        result[:, rows] = part.astype(jnp.bfloat16)
        store(turn).start()

    for copy in stores:
        copy.wait()
    for turn in range(turns):
        store(turn).wait()


def ffn_back(ffn_out, top, gains, gate, up, down, by_gate, by_up, *earlier):
    tokens, width = top.shape
    units = by_up.shape[1]
    bf16 = jnp.bfloat16
    return pl.pallas_call(
        ffn_back_kernel,
        in_specs=[spec_vmem()] * 3 + [spec_any()] * (5 + len(earlier)),
        out_specs=[spec_any()] * 3 + [spec_vmem(), spec_any()],
        out_shape=[
            shaped((tokens, width), bf16),
            shaped((tokens, units), bf16),
            shaped((tokens, units), bf16),
            shaped((8, width), jnp.float32),
            shaped((tokens, width), bf16),
        ],
        scratch_shapes=[
            pltpu.VMEM((2, tokens, width), bf16),
            pltpu.VMEM((tokens, 2 * units), bf16),
            pltpu.VMEM((width, 2 * units), bf16),
            pltpu.VMEM((width, units), bf16),
            pltpu.SemaphoreType.DMA((2,)),
            pltpu.SemaphoreType.DMA((units // FFN_TILE,)),
            pltpu.SemaphoreType.DMA((width // FFN_TILE, 2)),
            pltpu.SemaphoreType.DMA((3 + width // FFN_TILE,)),
        ],
        compiler_params=ffn_params(),
        cost_estimate=cost(6 * tokens * width * units, 55_000_000),
        name="ffn_back",
    )(ffn_out, top, gains, gate, up, down, by_gate, by_up, *earlier)


def mid_back_kernel(place, grad_in, x, attn_out, top, gains, one, two, one_far, two_far, *rest):
    grad_mid, grad_attn, grad_att, gain_out, weight, sems = rest[-6:]
    width = (GROUP + 2) * HEAD_DIM
    first = pl.program_id(0) == 0

    def fetch():
        return fetch_rows(place, (one, two), (one_far, two_far), weight, sems, width, GROUP * HEAD_DIM)

    @pl.when(first)
    def _():
        gain_out[...] = jnp.zeros_like(gain_out)
        for copy in fetch():
            copy.start()

    chunk = ROW_CHUNK

    @pl.loop(0, x.shape[0] // chunk, unroll=ROW_UNROLL)
    def _(step):
        rows = pl.ds(pl.multiple_of(step * chunk, chunk), chunk)
        out = attn_out[rows, :].astype(jnp.float32)
        out_scale = row_scale(out)
        mid = x[rows, :].astype(jnp.float32) + out * out_scale * (1.0 + gains[1:2, :])
        upstream = grad_in[rows, :].astype(jnp.float32)
        pulled, product = norm_pull(mid, row_scale(mid), gains[2:3, :], upstream)
        gain_out[1] += fold_rows(product)
        at_mid = top[rows, :].astype(jnp.float32) + pulled
        grad_mid[rows, :] = at_mid
        pulled, product = norm_pull(out, out_scale, gains[1:2, :], at_mid)
        gain_out[0] += fold_rows(product)
        grad_attn[rows, :] = pulled.astype(jnp.bfloat16)

    @pl.when(first)
    def _():
        for copy in fetch():
            copy.wait()

    grad_att[...] = dot_nn(grad_attn[...], weight[...]).astype(jnp.bfloat16)


def mid_back(place, grad_in, x, attn_out, top, gains, near, far, *earlier):
    tokens, width = x.shape
    heads = GROUP * HEAD_DIM
    bf16 = jnp.bfloat16
    rows = pl.BlockSpec((MID_ROWS, width), lambda i: (i, 0))
    return pl.pallas_call(
        mid_back_kernel,
        grid=(tokens // MID_ROWS,),
        in_specs=[spec_smem()]
        + [rows] * 4
        + [whole((8, width))]
        + [spec_any()] * (4 + len(earlier)),
        out_specs=[
            rows,
            rows,
            pl.BlockSpec((MID_ROWS, heads), lambda i: (i, 0)),
            whole((2, 8, width)),
        ],
        out_shape=[
            shaped((tokens, width), jnp.float32),
            shaped((tokens, width), bf16),
            shaped((tokens, heads), bf16),
            shaped((2, 8, width), jnp.float32),
        ],
        scratch_shapes=[pltpu.VMEM((width, heads), bf16), pltpu.SemaphoreType.DMA((8,))],
        compiler_params=kernel_params(),
        cost_estimate=cost(2 * tokens * width * heads, 24_000_000),
        name="mid_back",
    )(place, grad_in, x, attn_out, top, gains, *near, *far, *earlier)


def attend_back_kernel(
    place, queries, pair, behind, attended, grad_att, cosine, sine, *rest
):
    grad_q, grad_own, grad_old, sums = rest[-4:]
    core = place[1]
    chunk = 128
    tokens = queries.shape[0]
    scale = HEAD_DIM**-0.5
    sums[...] = jnp.zeros_like(sums)
    for start in range(0, tokens, chunk):
        rows = slice(start, start + chunk)
        keys = start + chunk
        cos, sin = cosine[rows, :], sine[rows, :]
        for head in range(GROUP):
            columns = slice(head * HEAD_DIM, (head + 1) * HEAD_DIM)
            query, upstream = queries[rows, columns], grad_att[rows, columns]
            delta = jnp.sum(
                upstream.astype(jnp.float32) * attended[rows, columns].astype(jnp.float32),
                axis=-1,
                keepdims=True,
            )
            bent_old, old = chunk_scores(query, behind[0], True, start, core)
            bent_new, new = chunk_scores(query, pair[0, :keys], False, start, core)
            share = 1.0 / (
                jnp.sum(old, axis=-1, keepdims=True) + jnp.sum(new, axis=-1, keepdims=True)
            )
            total = jnp.zeros((chunk, HEAD_DIM), jnp.float32)
            for bent, powers, block, end, base in (
                (bent_old, old, behind, tokens, 0),
                (bent_new, new, pair, keys, 2),
            ):
                prob = powers * share
                grad_p = dot_nt(upstream, block[1, :end])
                grad_s = (prob * (grad_p - delta) * (1.0 - bent * bent)).astype(jnp.bfloat16)
                total += dot_nn(grad_s, block[0, :end])
                sums[base, :end, :] += dot_tn(grad_s, query)
                sums[base + 1, :end, :] += dot_tn(prob.astype(jnp.bfloat16), upstream)
            grad_q[rows, columns] = rope(total * scale, cos, -sin).astype(jnp.bfloat16)
    grad_old[0] = (sums[0] * scale).astype(jnp.bfloat16)
    grad_old[1] = sums[1].astype(jnp.bfloat16)
    grad_own[0] = sums[2] * scale
    grad_own[1] = sums[3]


def attend_back(place, queries, pair, behind, attended, grad_att, cosine, sine, *earlier):
    tokens, heads = queries.shape
    bf16 = jnp.bfloat16
    return pl.pallas_call(
        attend_back_kernel,
        in_specs=[spec_smem()] + [spec_vmem()] * 7 + [spec_any()] * len(earlier),
        out_specs=[spec_vmem()] * 3,
        out_shape=[
            shaped((tokens, heads), bf16),
            shaped((2, tokens, HEAD_DIM), jnp.float32),
            shaped((2, tokens, HEAD_DIM), bf16),
        ],
        scratch_shapes=[pltpu.VMEM((4, tokens, HEAD_DIM), jnp.float32)],
        compiler_params=kernel_params(),
        cost_estimate=cost(20 * tokens * 1024 * heads, 5_000_000),
        name="attend_back",
    )(place, queries, pair, behind, attended, grad_att, cosine, sine, *earlier)


def project_back_kernel(
    place, grad_q, grad_own, grad_ahead, cosine, sine, x, one, two, one_far, two_far, *rest
):
    proj, result, gain_out, weight, sems = rest[-5:]
    width = (GROUP + 2) * HEAD_DIM
    copies = fetch_rows(place, (one, two), (one_far, two_far), weight, sems, 0, width)
    for copy in copies:
        copy.start()
    heads = GROUP * HEAD_DIM
    proj[:, :heads] = grad_q[...]
    grad_key = grad_own[0] + grad_ahead[0].astype(jnp.float32)
    proj[:, heads : heads + HEAD_DIM] = rope(grad_key, cosine[...], -sine[...]).astype(jnp.bfloat16)
    proj[:, heads + HEAD_DIM :] = (grad_own[1] + grad_ahead[1].astype(jnp.float32)).astype(
        jnp.bfloat16
    )
    gain_out[...] = jnp.zeros_like(gain_out)
    for copy in copies:
        copy.wait()
    tile = 768
    for column in range(0, result.shape[1], tile):
        part = dot_nt(proj[...], weight[column : column + tile, :])
        result[:, column : column + tile] = part.astype(jnp.bfloat16)
    chunk = ROW_CHUNK

    @pl.loop(0, x.shape[0] // chunk, unroll=ROW_UNROLL)
    def _(step):
        rows = pl.ds(pl.multiple_of(step * chunk, chunk), chunk)
        stream = x[rows, :].astype(jnp.float32)
        product = result[rows, :].astype(jnp.float32) * (stream * row_scale(stream))
        gain_out[...] += fold_rows(product)


def project_back(place, grad_q, grad_own, grad_ahead, cosine, sine, x, near, far, *earlier):
    tokens, width = x.shape
    proj_width = (GROUP + 2) * HEAD_DIM
    bf16 = jnp.bfloat16
    return pl.pallas_call(
        project_back_kernel,
        in_specs=[spec_smem()]
        + [spec_vmem()] * 6
        + [spec_any()] * 4
        + [spec_any()] * len(earlier),
        out_specs=[spec_vmem()] * 3,
        out_shape=[
            shaped((tokens, proj_width), bf16),
            shaped((tokens, width), bf16),
            shaped((8, width), jnp.float32),
        ],
        scratch_shapes=[pltpu.VMEM((width, proj_width), bf16), pltpu.SemaphoreType.DMA((8,))],
        compiler_params=kernel_params(),
        cost_estimate=cost(2 * tokens * width * proj_width, 14_000_000),
        name="project_back",
    )(place, grad_q, grad_own, grad_ahead, cosine, sine, x, *near, *far, *earlier)


def stream_back_kernel(grad_in, x, gains, grad_mid, *rest):
    result = rest[-1]
    chunk = ROW_CHUNK

    @pl.loop(0, x.shape[0] // chunk, unroll=ROW_UNROLL)
    def _(step):
        rows = pl.ds(pl.multiple_of(step * chunk, chunk), chunk)
        stream = x[rows, :].astype(jnp.float32)
        upstream = grad_in[rows, :].astype(jnp.float32)
        pulled, _ = norm_pull(stream, row_scale(stream), gains[0:1, :], upstream)
        result[rows, :] = grad_mid[rows, :] + pulled


def stream_back(grad_in, x, gains, grad_mid, *earlier):
    tokens, width = x.shape
    tile = MID_ROWS
    rows = pl.BlockSpec((tile, width), lambda i: (i, 0))
    return pl.pallas_call(
        stream_back_kernel,
        grid=(tokens // tile,),
        in_specs=[rows, rows, whole((8, width)), rows] + [spec_any()] * len(earlier),
        out_specs=rows,
        out_shape=shaped((tokens, width), jnp.float32),
        compiler_params=kernel_params(),
        cost_estimate=cost(20 * tokens * width, 14_000_000),
        name="stream_back",
    )(grad_in, x, gains, grad_mid, *earlier)


def flat(values):
    rows, pair, width = values.shape
    lanes = width // 128
    if pair == 1:
        return values.reshape(rows * lanes, 128)
    tiles = with_layout_constraint(
        values.reshape(rows, pair, lanes, 128), Layout(major_to_minor=(0, 2, 1, 3))
    )
    return tiles.transpose(0, 2, 1, 3).reshape(rows * pair * lanes, 128)


def unflat(values, shape):
    rows, pair, width = shape
    lanes = width // 128
    if pair == 1:
        return values.reshape(shape)
    tiles = values.reshape(rows, lanes, pair, 128).transpose(0, 2, 1, 3)
    return with_layout_constraint(tiles, Layout(major_to_minor=(0, 2, 1, 3))).reshape(shape)


def join_kernel(*refs):
    result = refs[-1]
    for which in range(2):
        own, got, far = (refs[which * 3 + k][...].astype(jnp.float32) for k in range(3))
        result[:, which, :] = own + got + far


def join(gate, up):
    rows, width = gate[0].shape
    tile = 32
    block = pl.BlockSpec((tile, width), lambda i: (i, 0))
    return pl.pallas_call(
        join_kernel,
        grid=(rows // tile,),
        in_specs=[block] * 6,
        out_specs=pl.BlockSpec((tile, 2, width), lambda i: (i, 0, 0)),
        out_shape=shaped((rows, 2, width), jnp.float32),
        compiler_params=kernel_params(),
        cost_estimate=cost(0, 200_000_000),
        name="join",
    )(*gate, *up)


def adam_kernel(parts, decay, *refs):
    weight, first, second = (ref[...] for ref in refs[parts : parts + 3])
    outs = refs[parts + 3 :]
    grad = refs[0][...].astype(jnp.float32)
    for ref in refs[1:parts]:
        grad += ref[...].astype(jnp.float32)
    if parts > 1:
        outs[-1][...] = grad
    outs[0][...], outs[1][...], outs[2][...] = adam_step(weight, grad, first, second, decay)


def adam(grads, weight, first, second, decay):
    rows, width = weight.shape
    steps = 3 if rows * width < 1_000_000 else 6
    tile = rows // steps
    block = pl.BlockSpec((tile, width), lambda i: (i, 0))
    count = 3 if len(grads) == 1 else 4
    return pl.pallas_call(
        functools.partial(adam_kernel, len(grads), decay),
        grid=(steps,),
        in_specs=[block] * (len(grads) + 3),
        out_specs=[block] * count,
        out_shape=[shaped((rows, width), jnp.float32)] * count,
        compiler_params=kernel_params(),
        cost_estimate=cost(0, 200_000_000),
        name="adam",
    )(*grads, weight, first, second)


def on_square(
    layer_in,
    cotangent,
    qkv_weight,
    out_weight,
    gate_up_weight,
    down_weight,
    norm_gains,
    qkv_first,
    out_first,
    gate_up_first,
    down_first,
    gains_first,
    qkv_second,
    out_second,
    gate_up_second,
    down_second,
    gains_second,
):
    tok_rows = layer_in.shape[1]
    chip, core = lax.axis_index("batch"), lax.axis_index("seq")
    place = jnp.stack([chip, core]).astype(jnp.int32)
    plane = ("batch", "seq")
    stream, top = layer_in[0], cotangent[0]
    gains_cast = jnp.pad(norm_gains.T, ((0, 0), (0, 128 - norm_gains.shape[0])))
    attn_cast = jnp.concatenate([qkv_weight[:, 0], out_weight.T, gains_cast], axis=1)
    gate_cast = gate_up_weight[:, 0].astype(jnp.bfloat16)
    up_cast = gate_up_weight[:, 1].astype(jnp.bfloat16)
    down_cast = down_weight.T.astype(jnp.bfloat16)
    attn_cast = attn_cast.astype(jnp.bfloat16)
    first, gate_cast, up_cast, down_cast = lax.optimization_barrier(
        (trade(attn_cast, 0), gate_cast, up_cast, down_cast)
    )
    attn_pair = jnp.stack([attn_cast, first])
    near = (attn_pair, trade(attn_pair, 1))
    far = tuple(swap(part, "seq", 1) for part in near)
    down_one = trade(down_cast, 0)
    gate_one = trade(gate_cast, 0)
    down_pair, gate_pair = jnp.stack([down_cast, down_one]), jnp.stack([gate_cast, gate_one])
    down_pair_far, gate_pair_far = swap(down_pair, "seq", 1), swap(gate_pair, "seq", 1)
    down_two = trade(down_pair, 1)
    gate_two = trade(after(gate_pair, down_pair_far, gate_pair_far), 1)
    down_parts = (down_pair, down_two), (down_pair_far, swap(down_two, "seq", 1))
    gate_parts = (gate_pair, gate_two), (gate_pair_far, swap(gate_two, "seq", 1))
    up = lax.all_gather(up_cast, plane, axis=0, tiled=True)
    positions = core * tok_rows + jnp.arange(tok_rows, dtype=jnp.int32)
    cosine, sine = rope_tables(positions, HEAD_DIM)

    queries, pair, attn_in, gains = project(
        place, stream, near, far, cosine, sine, up_cast
    )
    behind = from_behind(pair, "seq", 1)
    attended, attn_part = attend(
        place, queries, pair, behind, near, far, stream.shape[1], down_one
    )
    attn_out = tensor_sum(attn_part)
    ffn_in, hidden, by_gate, by_up, ffn_part = ffn_forward(
        place, attn_out, stream, gains, up, gate_parts, down_parts
    )
    ffn_out = tensor_sum(ffn_part)

    gate = arrange(place, *gate_parts)
    down = arrange(place, *down_parts)
    att_both = jnp.concatenate([attended, swap(attended, "seq", 1)], axis=0)
    attn_in_both = both_cores(attn_in)
    ffn_in_both = both_cores(ffn_in)
    hidden_both = jnp.concatenate([hidden, swap(hidden, "seq", 1)], axis=0)
    grad_ffn, grad_gate, grad_up, gain_ffn, grad_ffn_part = ffn_back(
        ffn_out, top, gains, gate, up, down, by_gate, by_up, att_both, attn_in_both, ffn_in_both,
        hidden_both
    )
    grad_ffn_in = tensor_sum(grad_ffn_part)
    grad_gate_both = jnp.concatenate([grad_gate, swap(grad_gate, "seq", 1)], axis=0)
    grad_up_both = jnp.concatenate([grad_up, swap(grad_up, "seq", 1)], axis=0)
    down_local = weight_local(both_cores(grad_ffn), hidden_both)
    gate_local = weight_local(ffn_in_both, grad_gate_both)
    up_local = weight_local(ffn_in_both, grad_up_both)
    down_state = scatter_begin(down_local)
    gate_state = scatter_begin(gate_local)
    up_got = trade(jnp.stack([up_local[1], up_local[3]]), 0)
    down_grad = scatter_end(down_state)

    grad_mid, grad_attn, grad_att, gain_mid = mid_back(
        place, grad_ffn_in, stream, attn_out, top, gains, near, far, down_state[2], gate_state[1]
    )
    gate_grad = scatter_end(gate_state)
    grad_q, grad_own, grad_old = attend_back(
        place, queries, pair, behind, attended, grad_att, cosine, sine
    )
    grad_ahead = from_behind(grad_old, "seq", -1)
    grad_proj, grad_attn_part, gain_attn = project_back(
        place, grad_q, grad_own, grad_ahead, cosine, sine, stream, near, far, down_grad[2], up_got
    )
    grad_attn_in = tensor_sum(grad_attn_part)
    grad_attn, gain_mid, up_got, down_grad = after(
        (grad_attn, gain_mid, up_got, down_grad), grad_attn_part
    )
    up_grad = scatter_end(scatter_begin(up_local, up_got))
    gate_up_grad = join(gate_grad, up_grad)

    out_local = weight_local(both_cores(grad_attn), att_both)
    out_grad = scatter_end(scatter_begin(out_local))
    proj_both = jnp.concatenate([grad_proj, swap(grad_proj, "seq", 1)], axis=0)
    qkv_local = weight_local(attn_in_both, proj_both)
    qkv_grad = sum(part.astype(jnp.float32) for part in scatter_end(scatter_begin(qkv_local)))[:, None]
    gains_rest = jnp.concatenate([gain_mid, gain_ffn[None]], axis=0).sum(axis=1)
    gains_rest = jnp.where(lax.axis_index("tensor") == 0, gains_rest, 0.0)
    gains_total = everywhere_sum(jnp.concatenate([gain_attn.sum(axis=0)[None], gains_rest], axis=0))
    own_columns = norm_gains.shape[1]
    gains_grad = lax.dynamic_slice_in_dim(
        gains_total, (chip * 2 + core) * own_columns, own_columns, axis=1
    )
    attn_float = attn_out.astype(jnp.float32)
    mid_stream = stream.astype(jnp.float32) + rms_norm(attn_float, gains[1])
    layer_out = (mid_stream + rms_norm(ffn_out.astype(jnp.float32), gains[3])).astype(jnp.bfloat16)
    qkv_shape, gate_up_shape = qkv_weight.shape, gate_up_weight.shape
    qkv_new, qkv_first_new, qkv_second_new = (
        unflat(value, qkv_shape)
        for value in adam(
            [flat(qkv_grad)], flat(qkv_weight), flat(qkv_first), flat(qkv_second), decay_rate
        )
    )
    out_new, out_first_new, out_second_new, out_grad = adam(
        out_grad, out_weight.T, out_first.T, out_second.T, decay_rate
    )
    gate_up_new, gate_up_first_new, gate_up_second_new = (
        unflat(value, gate_up_shape)
        for value in adam(
            [flat(gate_up_grad)],
            flat(gate_up_weight),
            flat(gate_up_first),
            flat(gate_up_second),
            decay_rate,
        )
    )
    down_new, down_first_new, down_second_new, down_grad = adam(
        down_grad, down_weight.T, down_first.T, down_second.T, decay_rate
    )
    gains_new, gains_first_new, gains_second_new = adam_step(
        norm_gains, gains_grad, gains_first, gains_second, 0.0
    )
    input_grad = stream_back(
        grad_attn_in, stream, gains, grad_mid, qkv_new, out_new, gate_up_new, down_new, gains_new
    )
    return (
        layer_out[None],
        input_grad[None],
        qkv_grad,
        out_grad.T,
        gate_up_grad,
        down_grad.T,
        gains_grad,
        qkv_new,
        out_new.T,
        gate_up_new,
        down_new.T,
        gains_new,
        qkv_first_new,
        out_first_new.T,
        gate_up_first_new,
        down_first_new.T,
        gains_first_new,
        qkv_second_new,
        out_second_new.T,
        gate_up_second_new,
        down_second_new.T,
        gains_second_new,
    )


def on_device(
    layer_in,
    cotangent,
    qkv_weight,
    out_weight,
    gate_up_weight,
    down_weight,
    norm_gains,
    qkv_first,
    out_first,
    gate_up_first,
    down_first,
    gains_first,
    qkv_second,
    out_second,
    gate_up_second,
    down_second,
    gains_second,
):
    tok_rows = layer_in.shape[1]
    seq_index = lax.axis_index("seq")
    collected = (
        lax.all_gather(qkv_weight.astype(jnp.bfloat16), ("batch", "seq"), axis=0, tiled=True),
        lax.all_gather(out_weight.astype(jnp.bfloat16), ("batch", "seq"), axis=1, tiled=True),
        lax.all_gather(gate_up_weight.astype(jnp.bfloat16), ("batch", "seq"), axis=0, tiled=True),
        lax.all_gather(down_weight.astype(jnp.bfloat16), ("batch", "seq"), axis=1, tiled=True),
        lax.all_gather(norm_gains.astype(jnp.bfloat16), ("batch", "seq"), axis=1, tiled=True),
    )
    qkv_full, out_full, gate_up_full, down_full, gains_full = collected
    model_width = qkv_full.shape[0]
    kv_local = qkv_full.shape[1]
    heads_local = kv_local * GROUP
    ffn_local = gate_up_full.shape[2]
    qkv_flat = qkv_full.reshape(model_width, kv_local * (GROUP + 2) * HEAD_DIM)
    gate_up_flat = gate_up_full.reshape(model_width, 2 * ffn_local)
    gains_float = gains_full.astype(jnp.float32)
    positions = seq_index * tok_rows + jnp.arange(tok_rows, dtype=jnp.int32)
    cosine, sine = rope_tables(positions, HEAD_DIM)
    key_positions = (seq_index - WIN_BLOCKS) * tok_rows + jnp.arange(
        (WIN_BLOCKS + 1) * tok_rows, dtype=jnp.int32
    )
    spread = positions[:, None] - key_positions[None, :]
    allowed = (spread >= 0) & (spread < WIN_BLOCKS * tok_rows) & (key_positions >= 0)[None, :]
    mask = allowed[None, None]
    stream = layer_in[0].astype(jnp.float32)
    attn_in = rms_norm(stream, gains_float[0]).astype(jnp.bfloat16)
    projected = jnp.dot(attn_in, qkv_flat, preferred_element_type=jnp.float32).reshape(
        tok_rows, kv_local, GROUP + 2, HEAD_DIM
    )
    queries = rotate(
        projected[:, :, :GROUP].reshape(tok_rows, heads_local, HEAD_DIM), cosine, sine
    ).astype(jnp.bfloat16)
    keys = rotate(projected[:, :, GROUP], cosine, sine).astype(jnp.bfloat16)
    values = projected[:, :, GROUP + 1].astype(jnp.bfloat16)
    kv_pair = jnp.stack([keys, values], axis=0)
    reach = min(WIN_BLOCKS, lax.axis_size("seq") - 1)
    pieces = []
    for distance in range(WIN_BLOCKS, 0, -1):
        if distance <= reach:
            pieces.append(from_behind(kv_pair, "seq", distance))
        else:
            pieces.append(jnp.zeros_like(kv_pair))
    pieces.append(kv_pair)
    extended = jnp.concatenate(pieces, axis=1)
    ext_keys = extended[0]
    ext_values = extended[1]
    query_groups = queries.reshape(tok_rows, kv_local, GROUP, HEAD_DIM)
    capped = capped_scores(query_groups, ext_keys)
    log_sums = jnp.log(jnp.sum(jnp.where(mask, jnp.exp(capped), 0.0), axis=-1))
    probs = jnp.where(mask, jnp.exp(capped - log_sums[..., None]), 0.0).astype(jnp.bfloat16)
    attended = jnp.einsum(
        "cgij,jcd->icgd", probs, ext_values, preferred_element_type=jnp.float32
    ).astype(jnp.bfloat16)
    att_flat = attended.reshape(tok_rows, heads_local * HEAD_DIM)
    attn_out = lax.psum(jnp.dot(att_flat, out_full, preferred_element_type=jnp.float32), "tensor")
    mid_stream = stream + rms_norm(attn_out, gains_float[1])
    ffn_in = rms_norm(mid_stream, gains_float[2]).astype(jnp.bfloat16)
    gate_up = jnp.dot(ffn_in, gate_up_flat, preferred_element_type=jnp.float32).reshape(
        tok_rows, 2, ffn_local
    )
    hidden = geglu(gate_up[:, 0], gate_up[:, 1]).astype(jnp.bfloat16)
    ffn_out = lax.psum(jnp.dot(hidden, down_full, preferred_element_type=jnp.float32), "tensor")
    layer_out = (mid_stream + rms_norm(ffn_out, gains_float[3])).astype(jnp.bfloat16)
    grad_top = cotangent[0].astype(jnp.float32)
    grad_ffn_out, gain_three = norm_back(ffn_out, gains_float[3], grad_top)
    grad_ffn = grad_ffn_out.astype(jnp.bfloat16)
    grad_hidden = cols_product(grad_ffn, down_full)
    _, geglu_pull = jax.vjp(geglu, gate_up[:, 0], gate_up[:, 1])
    grad_gate, grad_up = geglu_pull(grad_hidden)
    grad_gate_up = (
        jnp.stack([grad_gate, grad_up], axis=1)
        .reshape(tok_rows, 2 * ffn_local)
        .astype(jnp.bfloat16)
    )
    grad_ffn_in = lax.psum(cols_product(grad_gate_up, gate_up_flat), "tensor")
    grad_mid_norm, gain_two = norm_back(mid_stream, gains_float[2], grad_ffn_in)
    grad_mid = grad_top + grad_mid_norm
    grad_attn_out, gain_one = norm_back(attn_out, gains_float[1], grad_mid)
    grad_attn = grad_attn_out.astype(jnp.bfloat16)
    grad_att = (
        cols_product(grad_attn, out_full)
        .astype(jnp.bfloat16)
        .reshape(tok_rows, kv_local, GROUP, HEAD_DIM)
    )
    capped_again = capped_scores(query_groups, ext_keys)
    probs_float = jnp.where(mask, jnp.exp(capped_again - log_sums[..., None]), 0.0)
    probs_again = probs_float.astype(jnp.bfloat16)
    delta = jnp.einsum("icgd,icgd->cgi", grad_att, attended, preferred_element_type=jnp.float32)
    grad_probs = jnp.einsum(
        "icgd,jcd->cgij", grad_att, ext_values, preferred_element_type=jnp.float32
    )
    grad_scores = (
        probs_float * (grad_probs - delta[..., None]) * (1.0 - (capped_again / soft_cap) ** 2)
    ).astype(jnp.bfloat16)
    score_scale = HEAD_DIM ** (-0.5)
    grad_values_ext = jnp.einsum(
        "cgij,icgd->jcd", probs_again, grad_att, preferred_element_type=jnp.float32
    )
    grad_keys_ext = (
        jnp.einsum("cgij,icgd->jcd", grad_scores, query_groups, preferred_element_type=jnp.float32)
        * score_scale
    )
    grad_queries = (
        jnp.einsum("cgij,jcd->icgd", grad_scores, ext_keys, preferred_element_type=jnp.float32)
        * score_scale
    )
    grad_pair_ext = jnp.stack([grad_keys_ext, grad_values_ext], axis=0)
    grad_pair = grad_pair_ext[:, WIN_BLOCKS * tok_rows :]
    for distance in range(1, reach + 1):
        start = (WIN_BLOCKS - distance) * tok_rows
        piece = grad_pair_ext[:, start : start + tok_rows]
        grad_pair = grad_pair + from_behind(piece.astype(jnp.bfloat16), "seq", -distance).astype(
            piece.dtype
        )
    grad_queries = rotate(
        grad_queries.reshape(tok_rows, heads_local, HEAD_DIM), cosine, -sine
    ).reshape(tok_rows, kv_local, GROUP, HEAD_DIM)
    grad_keys = rotate(grad_pair[0], cosine, -sine)
    grad_values = grad_pair[1]
    grad_proj = (
        jnp.concatenate([grad_queries, grad_keys[:, :, None], grad_values[:, :, None]], axis=2)
        .reshape(tok_rows, kv_local * (GROUP + 2) * HEAD_DIM)
        .astype(jnp.bfloat16)
    )
    grad_attn_in = lax.psum(
        cols_product(grad_proj, qkv_flat).astype(jnp.bfloat16), "tensor"
    ).astype(jnp.float32)
    grad_stream_norm, gain_zero = norm_back(stream, gains_float[0], grad_attn_in)
    input_grad = grad_mid + grad_stream_norm
    qkv_local = rows_product(attn_in, grad_proj).reshape(
        model_width, kv_local, (GROUP + 2) * HEAD_DIM
    )
    out_local = rows_product(att_flat, grad_attn)
    gate_up_local = rows_product(ffn_in, grad_gate_up).reshape(model_width, 2, ffn_local)
    down_local = rows_product(hidden, grad_ffn)
    gains_local = jnp.stack([gain_zero, gain_one, gain_two, gain_three])
    summed = (
        lax.psum_scatter(
            qkv_local.astype(jnp.bfloat16), ("batch", "seq"), scatter_dimension=0, tiled=True
        ).astype(jnp.float32),
        lax.psum_scatter(
            out_local.astype(jnp.bfloat16), ("batch", "seq"), scatter_dimension=1, tiled=True
        ).astype(jnp.float32),
        lax.psum_scatter(
            gate_up_local.astype(jnp.bfloat16), ("batch", "seq"), scatter_dimension=0, tiled=True
        ).astype(jnp.float32),
        lax.psum_scatter(
            down_local.astype(jnp.bfloat16), ("batch", "seq"), scatter_dimension=1, tiled=True
        ).astype(jnp.float32),
        lax.psum_scatter(
            gains_local.astype(jnp.bfloat16), ("batch", "seq"), scatter_dimension=1, tiled=True
        ).astype(jnp.float32),
    )
    qkv_grad, out_grad, gate_up_grad, down_grad, gains_grad = summed
    qkv_new, qkv_first_new, qkv_second_new = adam_step(
        qkv_weight, qkv_grad, qkv_first, qkv_second, decay_rate
    )
    out_new, out_first_new, out_second_new = adam_step(
        out_weight, out_grad, out_first, out_second, decay_rate
    )
    gate_up_new, gate_up_first_new, gate_up_second_new = adam_step(
        gate_up_weight, gate_up_grad, gate_up_first, gate_up_second, decay_rate
    )
    down_new, down_first_new, down_second_new = adam_step(
        down_weight, down_grad, down_first, down_second, decay_rate
    )
    gains_new, gains_first_new, gains_second_new = adam_step(
        norm_gains, gains_grad, gains_first, gains_second, 0.0
    )
    return (
        layer_out[None],
        input_grad[None],
        qkv_grad,
        out_grad,
        gate_up_grad,
        down_grad,
        gains_grad,
        qkv_new,
        out_new,
        gate_up_new,
        down_new,
        gains_new,
        qkv_first_new,
        out_first_new,
        gate_up_first_new,
        down_first_new,
        gains_first_new,
        qkv_second_new,
        out_second_new,
        gate_up_second_new,
        down_second_new,
        gains_second_new,
    )


def solution(mesh):
    in_specs = (
        P("batch", "seq", None),
        P("batch", "seq", None),
        P(("batch", "seq"), "tensor", None),
        P("tensor", ("batch", "seq")),
        P(("batch", "seq"), None, "tensor"),
        P("tensor", ("batch", "seq")),
        P(None, ("batch", "seq")),
        P(("batch", "seq"), "tensor", None),
        P("tensor", ("batch", "seq")),
        P(("batch", "seq"), None, "tensor"),
        P("tensor", ("batch", "seq")),
        P(None, ("batch", "seq")),
        P(("batch", "seq"), "tensor", None),
        P("tensor", ("batch", "seq")),
        P(("batch", "seq"), None, "tensor"),
        P("tensor", ("batch", "seq")),
        P(None, ("batch", "seq")),
    )
    out_specs = (
        P("batch", "seq", None),
        P("batch", "seq", None),
        P(("batch", "seq"), "tensor", None),
        P("tensor", ("batch", "seq")),
        P(("batch", "seq"), None, "tensor"),
        P("tensor", ("batch", "seq")),
        P(None, ("batch", "seq")),
        P(("batch", "seq"), "tensor", None),
        P("tensor", ("batch", "seq")),
        P(("batch", "seq"), None, "tensor"),
        P("tensor", ("batch", "seq")),
        P(None, ("batch", "seq")),
        P(("batch", "seq"), "tensor", None),
        P("tensor", ("batch", "seq")),
        P(("batch", "seq"), None, "tensor"),
        P("tensor", ("batch", "seq")),
        P(None, ("batch", "seq")),
        P(("batch", "seq"), "tensor", None),
        P("tensor", ("batch", "seq")),
        P(("batch", "seq"), None, "tensor"),
        P("tensor", ("batch", "seq")),
        P(None, ("batch", "seq")),
    )
    sizes = tuple(mesh.shape[axis] for axis in ("batch", "seq", "tensor"))
    body = on_square if sizes == (4, 2, 4) else on_device
    return jax.shard_map(
        body, mesh=mesh, in_specs=in_specs, out_specs=out_specs, check_vma=False
    )
```

```python
import functools
import jax
import jax.numpy as jnp
from jax import lax
from jax.experimental.layout import Layout, with_layout_constraint
from jax.experimental import pallas as pl
from jax.experimental.pallas import tpu as pltpu
from jax.sharding import PartitionSpec as P

HEAD_DIM = 256
WIN_BLOCKS = 4
STEP = 10
GROUP = 2


norm_eps = 1e-06
soft_cap = 50.0
learn_rate = 0.02
decay_rate = 0.1
beta_first = 0.9
beta_second = 0.95
adam_eps = 1e-08
gelu_coef = 0.7978845608028654


def from_behind(value, axis, steps):
    count = lax.axis_size(axis)
    initial, last = (max(0, -steps), min(count, count - steps))
    return lax.ppermute(value, axis, [(source, source + steps) for source in range(initial, last)])


def rms_norm(values, gain):
    scale = lax.rsqrt(jnp.mean(values * values, axis=-1, keepdims=True) + norm_eps)
    return values * scale * (1.0 + gain)


def norm_back(values, gain, upstream):
    _, pullback = jax.vjp(rms_norm, values, gain)
    return pullback(upstream)


def gelu_tanh(values):
    inner = gelu_coef * (values + 0.044715 * values * values * values)
    return 0.5 * values * (1.0 + jnp.tanh(inner))


def geglu(gate, up_part):
    return gelu_tanh(gate) * up_part


def rope_tables(positions, head_size):
    half = head_size // 2
    exponent = jnp.arange(half, dtype=jnp.float32) * (2.0 / head_size)
    freqs = 10000.0 ** (-exponent)
    angles = positions.astype(jnp.float32)[:, None] * freqs[None, :]
    return (jnp.cos(angles), jnp.sin(angles))


def rotate(values, cosine, sine):
    half = values.shape[-1] // 2
    first = values[..., :half]
    second = values[..., half:]
    cosine = cosine[:, None, :]
    sine = sine[:, None, :]
    return jnp.concatenate(
        [first * cosine - second * sine, second * cosine + first * sine], axis=-1
    )


def adam_step(weight, grad, first, second, decay):
    first_new = beta_first * first + (1.0 - beta_first) * grad
    second_new = beta_second * second + (1.0 - beta_second) * grad * grad
    first_hat = first_new / (1.0 - beta_first**STEP)
    second_hat = second_new / (1.0 - beta_second**STEP)
    weight_new = weight - learn_rate * (
        first_hat / (jnp.sqrt(second_hat) + adam_eps) + decay * weight
    )
    return (weight_new, first_new, second_new)


def rows_product(left, right):
    return lax.dot_general(
        left, right, (((0,), (0,)), ((), ())), preferred_element_type=jnp.float32
    )


def cols_product(left, right):
    return lax.dot_general(
        left, right, (((1,), (1,)), ((), ())), preferred_element_type=jnp.float32
    )


def capped_scores(query_groups, ext_keys):
    raw = jnp.einsum(
        "icgd,jcd->cgij", query_groups, ext_keys, preferred_element_type=jnp.float32
    ) * query_groups.shape[-1] ** (-0.5)
    return soft_cap * jnp.tanh(raw / soft_cap)


def tensor_sum(part):
    return lax.psum(part, "tensor")


def swap(value, axis, bit):
    count = lax.axis_size(axis)
    return lax.ppermute(value, axis, [(source, source ^ bit) for source in range(count)])


def after(value, *earlier):
    return lax.optimization_barrier((value, earlier))[0]


def trade(value, turn):
    pairs = []
    for chip in range(4):
        for core in range(2):
            pairs.append((chip * 2 + core, (chip ^ (1 + (core ^ turn))) * 2 + core))
    return lax.ppermute(value, ("batch", "seq"), pairs)


def offsets(owner):
    return (0, 1 + owner, 2 - owner, 3)


def own_blocks(wide):
    tokens, width = wide.shape
    chip, core = lax.axis_index("batch"), lax.axis_index("seq")
    split = wide.reshape(tokens, 8, width // 8)
    halves = []
    for owner in (core, 1 - core):
        parts = [
            lax.dynamic_index_in_dim(split, (chip ^ offset) * 2 + owner, 1, keepdims=False)
            for offset in offsets(owner)
        ]
        halves.append(jnp.concatenate(parts, axis=1))
    return halves


def both_cores(wide):
    mine, theirs = own_blocks(wide)
    return jnp.concatenate([mine, swap(theirs, "seq", 1)], axis=0)


def weight_local(wide, narrow):
    local = rows_product(wide, narrow).astype(jnp.bfloat16)
    return local.reshape(4, -1, local.shape[1])


def scatter_begin(local, got=None):
    if got is None:
        got = trade(jnp.stack([local[1], local[3]]), 0)
    far = local[2].astype(jnp.float32) + got[1].astype(jnp.float32)
    return local, got, far.astype(jnp.bfloat16)


def scatter_end(state):
    local, got, far = state
    return local[0], got[0], trade(far, 1)


def everywhere_sum(value):
    for axis, bit in (("seq", 1), ("batch", 1), ("batch", 2), ("tensor", 1), ("tensor", 2)):
        value = value + swap(value, axis, bit)
    return value


FFN_TILE = 768
ROW_CHUNK = 16
ROW_UNROLL = 4
MID_ROWS = 128


def spec_any():
    return pl.BlockSpec(memory_space=pl.ANY)


def spec_vmem():
    return pl.BlockSpec(memory_space=pltpu.VMEM)


def spec_smem():
    return pl.BlockSpec(memory_space=pltpu.SMEM)


def kernel_params():
    return pltpu.CompilerParams(vmem_limit_bytes=56 * 1024 * 1024)


def cost(flops, moved):
    return pl.CostEstimate(flops=flops, bytes_accessed=moved, transcendentals=0)


def shaped(shape, kind):
    return jax.ShapeDtypeStruct(shape, kind)


def dot_nn(left, right):
    return lax.dot_general(
        left, right, (((1,), (0,)), ((), ())), preferred_element_type=jnp.float32
    )


def dot_nt(left, right):
    return lax.dot_general(
        left, right, (((1,), (1,)), ((), ())), preferred_element_type=jnp.float32
    )


def dot_tn(left, right):
    return lax.dot_general(
        left, right, (((0,), (0,)), ((), ())), preferred_element_type=jnp.float32
    )


def row_scale(values):
    return lax.rsqrt(jnp.mean(values * values, axis=-1, keepdims=True) + norm_eps)


def norm_pull(values, scale, gain, upstream):
    normed = values * scale
    inner = upstream * (1.0 + gain)
    pulled = scale * (inner - normed * jnp.mean(normed * inner, axis=-1, keepdims=True))
    return pulled, upstream * normed


def fold_rows(values):
    total = values[:8]
    for start in range(8, values.shape[0], 8):
        total += values[start : start + 8]
    return total


def fetch_rows(place, near, far, target, sems, column, columns):
    chip, core = place[0], place[1]
    rows = near[0].shape[1]
    copies = []
    for which, (one, two) in enumerate((near, far)):
        owner = which ^ core
        blocks = ((one.at[0], 0), (one.at[1], 1 + owner), (two.at[0], 2 - owner), (two.at[1], 3))
        for block, offset in blocks:
            row = ((offset ^ chip) * 2 + owner) * rows
            copies.append(
                pltpu.make_async_copy(
                    block.at[:, pl.ds(column, columns)],
                    target.at[pl.ds(pl.multiple_of(row, 16), rows), :],
                    sems.at[len(copies)],
                )
            )
    return copies


def rope(values, cosine, sine):
    half = HEAD_DIM // 2
    first, second = values[:, :half], values[:, half:]
    return jnp.concatenate(
        [first * cosine - second * sine, second * cosine + first * sine], axis=1
    )


def arrange_kernel(place, one, two, one_far, two_far, result, sems):
    copies = fetch_rows(place, (one, two), (one_far, two_far), result, sems, 0, result.shape[1])
    for copy in copies:
        copy.start()
    for copy in copies:
        copy.wait()


def arrange(place, near, far):
    return pl.pallas_call(
        arrange_kernel,
        in_specs=[spec_smem()] + [spec_any()] * 4,
        out_specs=spec_vmem(),
        out_shape=shaped((8 * near[0].shape[1], near[0].shape[2]), jnp.bfloat16),
        scratch_shapes=[pltpu.SemaphoreType.DMA((8,))],
        compiler_params=kernel_params(),
        cost_estimate=cost(0, 16 * near[0].size),
        name="arrange",
    )(place, *near, *far)


def project_kernel(place, x, one, two, one_far, two_far, cosine, sine, *rest):
    queries, pair, attn_in, gains, weight, tail, sems, tail_sems = rest[-8:]
    parts = (one, two), (one_far, two_far)
    width = (GROUP + 2) * HEAD_DIM
    tail_copies = fetch_rows(
        place, *parts, tail, tail_sems, width + GROUP * HEAD_DIM, tail.shape[1]
    )
    copies = fetch_rows(place, *parts, weight, sems, 0, width)
    for copy in tail_copies + copies:
        copy.start()
    for copy in tail_copies:
        copy.wait()
    gains[...] = jnp.transpose(tail[...].astype(jnp.float32))[:8]
    gain = 1.0 + gains[0:1, :]
    chunk = ROW_CHUNK

    @pl.loop(0, x.shape[0] // chunk, unroll=ROW_UNROLL)
    def _(step):
        rows = pl.ds(pl.multiple_of(step * chunk, chunk), chunk)
        stream = x[rows, :].astype(jnp.float32)
        attn_in[rows, :] = (stream * row_scale(stream) * gain).astype(jnp.bfloat16)

    for copy in copies:
        copy.wait()
    for member in range(GROUP + 2):
        columns = slice(member * HEAD_DIM, (member + 1) * HEAD_DIM)
        part = dot_nn(attn_in[...], weight[:, columns])
        if member < GROUP:
            queries[:, columns] = rope(part, cosine[...], sine[...]).astype(jnp.bfloat16)
        elif member == GROUP:
            pair[0] = rope(part, cosine[...], sine[...]).astype(jnp.bfloat16)
        else:
            pair[1] = part.astype(jnp.bfloat16)


def project(place, x, near, far, cosine, sine, *earlier):
    tokens, width = x.shape
    bf16 = jnp.bfloat16
    return pl.pallas_call(
        project_kernel,
        in_specs=[spec_smem(), spec_vmem()]
        + [spec_any()] * 4
        + [spec_vmem()] * 2
        + [spec_any()] * len(earlier),
        out_specs=[spec_vmem()] * 4,
        out_shape=[
            shaped((tokens, GROUP * HEAD_DIM), bf16),
            shaped((2, tokens, HEAD_DIM), bf16),
            shaped((tokens, width), bf16),
            shaped((8, width), jnp.float32),
        ],
        scratch_shapes=[
            pltpu.VMEM((width, (GROUP + 2) * HEAD_DIM), bf16),
            pltpu.VMEM((width, near[0].shape[2] - (2 * GROUP + 2) * HEAD_DIM), bf16),
            pltpu.SemaphoreType.DMA((8,)),
            pltpu.SemaphoreType.DMA((8,)),
        ],
        compiler_params=kernel_params(),
        cost_estimate=cost(2 * tokens * width * 1024, 12_000_000),
        name="project",
    )(place, x, *near, *far, cosine, sine, *earlier)


def chunk_scores(query, key, behind, row, core):
    raw = dot_nt(query, key) * (HEAD_DIM**-0.5 / soft_cap)
    bent = jnp.tanh(raw)
    powers = jnp.exp(soft_cap * bent)
    if behind:
        powers = jnp.where(core > 0, powers, 0.0)
    else:
        at = row + lax.broadcasted_iota(jnp.int32, powers.shape, 0)
        powers = jnp.where(at >= lax.broadcasted_iota(jnp.int32, powers.shape, 1), powers, 0.0)
    return bent, powers


def attend_kernel(place, queries, pair, behind, one, two, one_far, two_far, *rest):
    attended, result, weight, sems = rest[-4:]
    width = (GROUP + 2) * HEAD_DIM
    copies = fetch_rows(place, (one, two), (one_far, two_far), weight, sems, width, GROUP * HEAD_DIM)
    for copy in copies:
        copy.start()
    core = place[1]
    chunk = 128
    tokens = queries.shape[0]
    for start in range(0, tokens, chunk):
        rows = slice(start, start + chunk)
        keys = start + chunk
        for head in range(GROUP):
            columns = slice(head * HEAD_DIM, (head + 1) * HEAD_DIM)
            query = queries[rows, columns]
            _, old = chunk_scores(query, behind[0], True, start, core)
            _, new = chunk_scores(query, pair[0, :keys], False, start, core)
            total = jnp.sum(old, axis=-1, keepdims=True) + jnp.sum(new, axis=-1, keepdims=True)
            share = 1.0 / total
            value = dot_nn((old * share).astype(jnp.bfloat16), behind[1])
            value += dot_nn((new * share).astype(jnp.bfloat16), pair[1, :keys])
            attended[rows, columns] = value.astype(jnp.bfloat16)
    for copy in copies:
        copy.wait()
    tile = 768
    for column in range(0, result.shape[1], tile):
        part = dot_nt(attended[...], weight[column : column + tile, :])
        result[:, column : column + tile] = part.astype(jnp.bfloat16)


def attend(place, queries, pair, behind, near, far, width, *earlier):
    tokens = queries.shape[0]
    bf16 = jnp.bfloat16
    return pl.pallas_call(
        attend_kernel,
        in_specs=[spec_smem()] + [spec_vmem()] * 3 + [spec_any()] * (4 + len(earlier)),
        out_specs=[spec_vmem()] * 2,
        out_shape=[shaped((tokens, GROUP * HEAD_DIM), bf16), shaped((tokens, width), bf16)],
        scratch_shapes=[
            pltpu.VMEM((width, GROUP * HEAD_DIM), bf16),
            pltpu.SemaphoreType.DMA((8,)),
        ],
        compiler_params=kernel_params(),
        cost_estimate=cost(4 * tokens * width * 1024, 8_000_000),
        name="attend",
    )(place, queries, pair, behind, *near, *far, *earlier)


def whole(shape):
    return pl.BlockSpec(shape, lambda *_: (0,) * len(shape))


def ffn_params():
    return pltpu.CompilerParams(vmem_limit_bytes=58 * 1024 * 1024)


def move(source, target, sem):
    copy = pltpu.make_async_copy(source, target, sem)
    copy.start()
    return copy


def ffn_kernel(place, attn_out, x, gains, up_full, *rest):
    gate_near, gate_far, down_near, down_far = (rest[k : k + 2] for k in (0, 2, 4, 6))
    outs, (sides, gate_up_here, down_here, in_sems, down_sems, out_sems) = rest[-11:-6], rest[-6:]
    ffn_in, hidden, by_gate, by_up, result = (sides.at[k] for k in range(5))
    tokens, width = x.shape
    units = up_full.shape[1]
    tile = FFN_TILE
    steps, turns = units // tile, width // tile

    def load(step):
        columns = pl.ds(pl.multiple_of(step * tile, tile), tile)
        up_copy = pltpu.make_async_copy(
            up_full.at[:, columns], gate_up_here.at[1, :, columns], in_sems.at[step, 8]
        )
        target = gate_up_here.at[0, :, columns]
        return [up_copy] + fetch_rows(
            place, gate_near, gate_far, target, in_sems.at[step], columns.start, tile
        )

    down_copies = fetch_rows(place, down_near, down_far, down_here, down_sems, 0, units)
    for step in range(steps):
        for copy in load(step):
            copy.start()
    for copy in down_copies:
        copy.start()
    chunk = ROW_CHUNK

    @pl.loop(0, tokens // chunk, unroll=ROW_UNROLL)
    def _(step):
        rows = pl.ds(pl.multiple_of(step * chunk, chunk), chunk)
        out = attn_out[rows, :].astype(jnp.float32)
        mid = x[rows, :].astype(jnp.float32) + out * row_scale(out) * (1.0 + gains[1:2, :])
        ffn_in[rows, :] = (mid * row_scale(mid) * (1.0 + gains[2:3, :])).astype(jnp.bfloat16)

    stores = [move(ffn_in, outs[0], out_sems.at[0])]

    @pl.loop(0, steps)
    def _(step):
        for copy in load(step):
            copy.wait()
        columns = pl.ds(pl.multiple_of(step * tile, tile), tile)
        for rows in (slice(None),):
            value = ffn_in[...]
            gate = dot_nn(value, gate_up_here[0, :, columns])
            up = dot_nn(value, gate_up_here[1, :, columns])
            square_of = gate * gate
            bent = jnp.tanh(gate * (gelu_coef + gelu_coef * 0.044715 * square_of))
            half = 0.5 + 0.5 * bent
            curve = gate * half
            slope = half + curve * (1.0 - bent) * (
                gelu_coef + 3.0 * gelu_coef * 0.044715 * square_of
            )
            hidden[rows, columns] = (curve * up).astype(jnp.bfloat16)
            by_gate[rows, columns] = (slope * up).astype(jnp.bfloat16)
            by_up[rows, columns] = curve.astype(jnp.bfloat16)

    for k, side in ((1, hidden), (2, by_gate), (3, by_up)):
        stores.append(move(side, outs[k], out_sems.at[k]))

    def store(turn):
        columns = pl.ds(pl.multiple_of(turn * tile, tile), tile)
        return pltpu.make_async_copy(
            result.at[:, columns], outs[4].at[:, columns], out_sems.at[4 + turn]
        )

    for copy in down_copies:
        copy.wait()

    @pl.loop(0, turns)
    def _(turn):
        rows = pl.ds(pl.multiple_of(turn * tile, tile), tile)
        result[:, rows] = dot_nt(hidden[...], down_here[rows, :]).astype(jnp.bfloat16)
        store(turn).start()

    for copy in stores:
        copy.wait()
    for turn in range(turns):
        store(turn).wait()


def ffn_forward(place, attn_out, x, gains, up, gate, down):
    tokens, width = x.shape
    units = up.shape[1]
    bf16 = jnp.bfloat16
    return pl.pallas_call(
        ffn_kernel,
        in_specs=[spec_smem()] + [spec_vmem()] * 3 + [spec_any()] * 9,
        out_specs=[spec_any()] * 5,
        out_shape=[shaped((tokens, width), bf16)]
        + [shaped((tokens, units), bf16)] * 3
        + [shaped((tokens, width), bf16)],
        scratch_shapes=[
            pltpu.VMEM((5, tokens, width), bf16),
            pltpu.VMEM((2, width, units), bf16),
            pltpu.VMEM((width, units), bf16),
            pltpu.SemaphoreType.DMA((units // FFN_TILE, 9)),
            pltpu.SemaphoreType.DMA((8,)),
            pltpu.SemaphoreType.DMA((4 + width // FFN_TILE,)),
        ],
        compiler_params=ffn_params(),
        cost_estimate=cost(6 * tokens * width * units, 50_000_000),
        name="ffn_forward",
    )(place, attn_out, x, gains, up, *gate[0], *gate[1], *down[0], *down[1])


def ffn_back_kernel(ffn_out, top, gains, gate, up_full, down, by_gate, by_up, *rest):
    grad_out, gate_out, up_out, gain_out, result_out = rest[-13:-8]
    sides, grads, gate_up_here, down_here, in_sems, down_sems, gate_sems, out_sems = rest[-8:]
    grad_ffn, result = sides.at[0], sides.at[1]
    tokens, width = top.shape
    units = gate.shape[1]
    grad_gate, grad_up = grads.at[:, pl.ds(0, units)], grads.at[:, pl.ds(units, units)]
    tile = FFN_TILE
    steps, turns = units // tile, width // tile

    def load_down(step):
        columns = pl.ds(pl.multiple_of(step * tile, tile), tile)
        return pltpu.make_async_copy(
            down.at[:, columns], down_here.at[:, columns], down_sems.at[step]
        )

    def load(turn, which):
        rows = pl.ds(pl.multiple_of(turn * tile, tile), tile)
        return pltpu.make_async_copy(
            (gate, up_full)[which].at[rows, :],
            gate_up_here.at[rows, pl.ds(which * units, units)],
            gate_sems.at[turn, which],
        )

    load_down(0).start()
    factors = [
        move(by_gate, grad_gate, in_sems.at[0]),
        move(by_up, grad_up, in_sems.at[1]),
    ]
    load_down(1).start()
    gain_out[...] = jnp.zeros_like(gain_out)
    chunk = ROW_CHUNK

    @pl.loop(0, tokens // chunk, unroll=ROW_UNROLL)
    def _(step):
        rows = pl.ds(pl.multiple_of(step * chunk, chunk), chunk)
        out = ffn_out[rows, :].astype(jnp.float32)
        upstream = top[rows, :].astype(jnp.float32)
        pulled, product = norm_pull(out, row_scale(out), gains[3:4, :], upstream)
        grad_ffn[rows, :] = pulled.astype(jnp.bfloat16)
        gain_out[...] += fold_rows(product)

    stores = [move(grad_ffn, grad_out, out_sems.at[0])]
    for copy in factors:
        copy.wait()

    @pl.loop(0, steps)
    def _(step):
        load_down(step).wait()

        @pl.when(step + 2 < steps)
        def _():
            load_down(step + 2).start()

        @pl.when(step + 2 >= steps)
        def _():
            load(step + 2 - steps, 0).start()
            load(step + 2 - steps, 1).start()

        columns = pl.ds(pl.multiple_of(step * tile, tile), tile)
        for start in range(0, tokens, tokens // 2):
            rows = pl.ds(start, tokens // 2)
            grad_hidden = dot_nn(grad_ffn[rows, :], down_here[:, columns])
            one = grad_hidden * grad_gate[rows, columns].astype(jnp.float32)
            two = grad_hidden * grad_up[rows, columns].astype(jnp.float32)
            grad_gate[rows, columns] = one.astype(jnp.bfloat16)
            grad_up[rows, columns] = two.astype(jnp.bfloat16)

    stores.append(move(grad_gate, gate_out, out_sems.at[1]))
    stores.append(move(grad_up, up_out, out_sems.at[2]))

    def store(turn):
        columns = pl.ds(pl.multiple_of(turn * tile, tile), tile)
        return pltpu.make_async_copy(
            result.at[:, columns], result_out.at[:, columns], out_sems.at[3 + turn]
        )

    @pl.loop(0, turns)
    def _(turn):
        load(turn, 0).wait()
        load(turn, 1).wait()

        @pl.when(turn + 2 < turns)
        def _():
            load(turn + 2, 0).start()
            load(turn + 2, 1).start()

        rows = pl.ds(pl.multiple_of(turn * tile, tile), tile)
        part = dot_nt(grads[...], gate_up_here[rows, :])
        result[:, rows] = part.astype(jnp.bfloat16)
        store(turn).start()

    for copy in stores:
        copy.wait()
    for turn in range(turns):
        store(turn).wait()


def ffn_back(ffn_out, top, gains, gate, up, down, by_gate, by_up, *earlier):
    tokens, width = top.shape
    units = by_up.shape[1]
    bf16 = jnp.bfloat16
    return pl.pallas_call(
        ffn_back_kernel,
        in_specs=[spec_vmem()] * 3 + [spec_any()] * (5 + len(earlier)),
        out_specs=[spec_any()] * 3 + [spec_vmem(), spec_any()],
        out_shape=[
            shaped((tokens, width), bf16),
            shaped((tokens, units), bf16),
            shaped((tokens, units), bf16),
            shaped((8, width), jnp.float32),
            shaped((tokens, width), bf16),
        ],
        scratch_shapes=[
            pltpu.VMEM((2, tokens, width), bf16),
            pltpu.VMEM((tokens, 2 * units), bf16),
            pltpu.VMEM((width, 2 * units), bf16),
            pltpu.VMEM((width, units), bf16),
            pltpu.SemaphoreType.DMA((2,)),
            pltpu.SemaphoreType.DMA((units // FFN_TILE,)),
            pltpu.SemaphoreType.DMA((width // FFN_TILE, 2)),
            pltpu.SemaphoreType.DMA((3 + width // FFN_TILE,)),
        ],
        compiler_params=ffn_params(),
        cost_estimate=cost(6 * tokens * width * units, 55_000_000),
        name="ffn_back",
    )(ffn_out, top, gains, gate, up, down, by_gate, by_up, *earlier)


def mid_back_kernel(place, grad_in, x, attn_out, top, gains, one, two, one_far, two_far, *rest):
    grad_mid, grad_attn, grad_att, gain_out, weight, sems = rest[-6:]
    width = (GROUP + 2) * HEAD_DIM
    first = pl.program_id(0) == 0

    def fetch():
        return fetch_rows(place, (one, two), (one_far, two_far), weight, sems, width, GROUP * HEAD_DIM)

    @pl.when(first)
    def _():
        gain_out[...] = jnp.zeros_like(gain_out)
        for copy in fetch():
            copy.start()

    chunk = ROW_CHUNK

    @pl.loop(0, x.shape[0] // chunk, unroll=ROW_UNROLL)
    def _(step):
        rows = pl.ds(pl.multiple_of(step * chunk, chunk), chunk)
        out = attn_out[rows, :].astype(jnp.float32)
        out_scale = row_scale(out)
        mid = x[rows, :].astype(jnp.float32) + out * out_scale * (1.0 + gains[1:2, :])
        upstream = grad_in[rows, :].astype(jnp.float32)
        pulled, product = norm_pull(mid, row_scale(mid), gains[2:3, :], upstream)
        gain_out[1] += fold_rows(product)
        at_mid = top[rows, :].astype(jnp.float32) + pulled
        grad_mid[rows, :] = at_mid.astype(jnp.bfloat16)
        pulled, product = norm_pull(out, out_scale, gains[1:2, :], at_mid)
        gain_out[0] += fold_rows(product)
        grad_attn[rows, :] = pulled.astype(jnp.bfloat16)

    @pl.when(first)
    def _():
        for copy in fetch():
            copy.wait()

    grad_att[...] = dot_nn(grad_attn[...], weight[...]).astype(jnp.bfloat16)


def mid_back(place, grad_in, x, attn_out, top, gains, near, far, *earlier):
    tokens, width = x.shape
    heads = GROUP * HEAD_DIM
    bf16 = jnp.bfloat16
    rows = pl.BlockSpec((MID_ROWS, width), lambda i: (i, 0))
    return pl.pallas_call(
        mid_back_kernel,
        grid=(tokens // MID_ROWS,),
        in_specs=[spec_smem()]
        + [rows] * 4
        + [whole((8, width))]
        + [spec_any()] * (4 + len(earlier)),
        out_specs=[
            rows,
            rows,
            pl.BlockSpec((MID_ROWS, heads), lambda i: (i, 0)),
            whole((2, 8, width)),
        ],
        out_shape=[
            shaped((tokens, width), bf16),
            shaped((tokens, width), bf16),
            shaped((tokens, heads), bf16),
            shaped((2, 8, width), jnp.float32),
        ],
        scratch_shapes=[pltpu.VMEM((width, heads), bf16), pltpu.SemaphoreType.DMA((8,))],
        compiler_params=kernel_params(),
        cost_estimate=cost(2 * tokens * width * heads, 24_000_000),
        name="mid_back",
    )(place, grad_in, x, attn_out, top, gains, *near, *far, *earlier)


def attend_back_kernel(
    place, queries, pair, behind, attended, grad_att, cosine, sine, *rest
):
    grad_q, grad_own, grad_old, sums = rest[-4:]
    core = place[1]
    chunk = 128
    tokens = queries.shape[0]
    scale = HEAD_DIM**-0.5
    sums[...] = jnp.zeros_like(sums)
    for start in range(0, tokens, chunk):
        rows = slice(start, start + chunk)
        keys = start + chunk
        cos, sin = cosine[rows, :], sine[rows, :]
        for head in range(GROUP):
            columns = slice(head * HEAD_DIM, (head + 1) * HEAD_DIM)
            query, upstream = queries[rows, columns], grad_att[rows, columns]
            delta = jnp.sum(
                upstream.astype(jnp.float32) * attended[rows, columns].astype(jnp.float32),
                axis=-1,
                keepdims=True,
            )
            bent_old, old = chunk_scores(query, behind[0], True, start, core)
            bent_new, new = chunk_scores(query, pair[0, :keys], False, start, core)
            share = 1.0 / (
                jnp.sum(old, axis=-1, keepdims=True) + jnp.sum(new, axis=-1, keepdims=True)
            )
            total = jnp.zeros((chunk, HEAD_DIM), jnp.float32)
            for bent, powers, block, end, base in (
                (bent_old, old, behind, tokens, 0),
                (bent_new, new, pair, keys, 2),
            ):
                prob = powers * share
                grad_p = dot_nt(upstream, block[1, :end])
                grad_s = (prob * (grad_p - delta) * (1.0 - bent * bent)).astype(jnp.bfloat16)
                total += dot_nn(grad_s, block[0, :end])
                sums[base, :end, :] += dot_tn(grad_s, query)
                sums[base + 1, :end, :] += dot_tn(prob.astype(jnp.bfloat16), upstream)
            grad_q[rows, columns] = rope(total * scale, cos, -sin).astype(jnp.bfloat16)
    grad_old[0] = (sums[0] * scale).astype(jnp.bfloat16)
    grad_old[1] = sums[1].astype(jnp.bfloat16)
    grad_own[0] = sums[2] * scale
    grad_own[1] = sums[3]


def attend_back(place, queries, pair, behind, attended, grad_att, cosine, sine, *earlier):
    tokens, heads = queries.shape
    bf16 = jnp.bfloat16
    return pl.pallas_call(
        attend_back_kernel,
        in_specs=[spec_smem()] + [spec_vmem()] * 7 + [spec_any()] * len(earlier),
        out_specs=[spec_vmem()] * 3,
        out_shape=[
            shaped((tokens, heads), bf16),
            shaped((2, tokens, HEAD_DIM), jnp.float32),
            shaped((2, tokens, HEAD_DIM), bf16),
        ],
        scratch_shapes=[pltpu.VMEM((4, tokens, HEAD_DIM), jnp.float32)],
        compiler_params=kernel_params(),
        cost_estimate=cost(20 * tokens * 1024 * heads, 5_000_000),
        name="attend_back",
    )(place, queries, pair, behind, attended, grad_att, cosine, sine, *earlier)


def project_back_kernel(
    place, grad_q, grad_own, grad_ahead, cosine, sine, x, one, two, one_far, two_far, *rest
):
    proj, result, gain_out, weight, sems = rest[-5:]
    width = (GROUP + 2) * HEAD_DIM
    copies = fetch_rows(place, (one, two), (one_far, two_far), weight, sems, 0, width)
    for copy in copies:
        copy.start()
    heads = GROUP * HEAD_DIM
    proj[:, :heads] = grad_q[...]
    grad_key = grad_own[0] + grad_ahead[0].astype(jnp.float32)
    proj[:, heads : heads + HEAD_DIM] = rope(grad_key, cosine[...], -sine[...]).astype(jnp.bfloat16)
    proj[:, heads + HEAD_DIM :] = (grad_own[1] + grad_ahead[1].astype(jnp.float32)).astype(
        jnp.bfloat16
    )
    gain_out[...] = jnp.zeros_like(gain_out)
    for copy in copies:
        copy.wait()
    tile = 768
    for column in range(0, result.shape[1], tile):
        part = dot_nt(proj[...], weight[column : column + tile, :])
        result[:, column : column + tile] = part.astype(jnp.bfloat16)
    chunk = ROW_CHUNK

    @pl.loop(0, x.shape[0] // chunk, unroll=ROW_UNROLL)
    def _(step):
        rows = pl.ds(pl.multiple_of(step * chunk, chunk), chunk)
        stream = x[rows, :].astype(jnp.float32)
        product = result[rows, :].astype(jnp.float32) * (stream * row_scale(stream))
        gain_out[...] += fold_rows(product)


def project_back(place, grad_q, grad_own, grad_ahead, cosine, sine, x, near, far, *earlier):
    tokens, width = x.shape
    proj_width = (GROUP + 2) * HEAD_DIM
    bf16 = jnp.bfloat16
    return pl.pallas_call(
        project_back_kernel,
        in_specs=[spec_smem()]
        + [spec_vmem()] * 6
        + [spec_any()] * 4
        + [spec_any()] * len(earlier),
        out_specs=[spec_vmem()] * 3,
        out_shape=[
            shaped((tokens, proj_width), bf16),
            shaped((tokens, width), bf16),
            shaped((8, width), jnp.float32),
        ],
        scratch_shapes=[pltpu.VMEM((width, proj_width), bf16), pltpu.SemaphoreType.DMA((8,))],
        compiler_params=kernel_params(),
        cost_estimate=cost(2 * tokens * width * proj_width, 14_000_000),
        name="project_back",
    )(place, grad_q, grad_own, grad_ahead, cosine, sine, x, *near, *far, *earlier)


def stream_back_kernel(grad_in, x, gains, grad_mid, *rest):
    result = rest[-1]
    chunk = ROW_CHUNK

    @pl.loop(0, x.shape[0] // chunk, unroll=ROW_UNROLL)
    def _(step):
        rows = pl.ds(pl.multiple_of(step * chunk, chunk), chunk)
        stream = x[rows, :].astype(jnp.float32)
        upstream = grad_in[rows, :].astype(jnp.float32)
        pulled, _ = norm_pull(stream, row_scale(stream), gains[0:1, :], upstream)
        result[rows, :] = grad_mid[rows, :].astype(jnp.float32) + pulled


def stream_back(grad_in, x, gains, grad_mid, *earlier):
    tokens, width = x.shape
    tile = MID_ROWS
    rows = pl.BlockSpec((tile, width), lambda i: (i, 0))
    return pl.pallas_call(
        stream_back_kernel,
        grid=(tokens // tile,),
        in_specs=[rows, rows, whole((8, width)), rows] + [spec_any()] * len(earlier),
        out_specs=rows,
        out_shape=shaped((tokens, width), jnp.float32),
        compiler_params=kernel_params(),
        cost_estimate=cost(20 * tokens * width, 14_000_000),
        name="stream_back",
    )(grad_in, x, gains, grad_mid, *earlier)


def flat(values):
    rows, pair, width = values.shape
    lanes = width // 128
    if pair == 1:
        return values.reshape(rows * lanes, 128)
    tiles = with_layout_constraint(
        values.reshape(rows, pair, lanes, 128), Layout(major_to_minor=(0, 2, 1, 3))
    )
    return tiles.transpose(0, 2, 1, 3).reshape(rows * pair * lanes, 128)


def unflat(values, shape):
    rows, pair, width = shape
    lanes = width // 128
    if pair == 1:
        return values.reshape(shape)
    tiles = values.reshape(rows, lanes, pair, 128).transpose(0, 2, 1, 3)
    return with_layout_constraint(tiles, Layout(major_to_minor=(0, 2, 1, 3))).reshape(shape)


def join_kernel(*refs):
    result = refs[-1]
    for which in range(2):
        own, got, far = (refs[which * 3 + k][...].astype(jnp.float32) for k in range(3))
        result[:, which, :] = own + got + far


def join(gate, up):
    rows, width = gate[0].shape
    tile = 32
    block = pl.BlockSpec((tile, width), lambda i: (i, 0))
    return pl.pallas_call(
        join_kernel,
        grid=(rows // tile,),
        in_specs=[block] * 6,
        out_specs=pl.BlockSpec((tile, 2, width), lambda i: (i, 0, 0)),
        out_shape=shaped((rows, 2, width), jnp.float32),
        compiler_params=kernel_params(),
        cost_estimate=cost(0, 200_000_000),
        name="join",
    )(*gate, *up)


def adam_kernel(parts, decay, *refs):
    weight, first, second = (ref[...] for ref in refs[parts : parts + 3])
    outs = refs[parts + 3 :]
    grad = refs[0][...].astype(jnp.float32)
    for ref in refs[1:parts]:
        grad += ref[...].astype(jnp.float32)
    if parts > 1:
        outs[-1][...] = grad
    outs[0][...], outs[1][...], outs[2][...] = adam_step(weight, grad, first, second, decay)


def adam(grads, weight, first, second, decay):
    rows, width = weight.shape
    steps = 3 if rows * width < 1_000_000 else 6
    tile = rows // steps
    block = pl.BlockSpec((tile, width), lambda i: (i, 0))
    count = 3 if len(grads) == 1 else 4
    return pl.pallas_call(
        functools.partial(adam_kernel, len(grads), decay),
        grid=(steps,),
        in_specs=[block] * (len(grads) + 3),
        out_specs=[block] * count,
        out_shape=[shaped((rows, width), jnp.float32)] * count,
        compiler_params=kernel_params(),
        cost_estimate=cost(0, 200_000_000),
        name="adam",
    )(*grads, weight, first, second)


def on_square(
    layer_in,
    cotangent,
    qkv_weight,
    out_weight,
    gate_up_weight,
    down_weight,
    norm_gains,
    qkv_first,
    out_first,
    gate_up_first,
    down_first,
    gains_first,
    qkv_second,
    out_second,
    gate_up_second,
    down_second,
    gains_second,
):
    tok_rows = layer_in.shape[1]
    chip, core = lax.axis_index("batch"), lax.axis_index("seq")
    place = jnp.stack([chip, core]).astype(jnp.int32)
    plane = ("batch", "seq")
    stream, top = layer_in[0], cotangent[0]
    gains_cast = jnp.pad(norm_gains.T, ((0, 0), (0, 128 - norm_gains.shape[0])))
    attn_cast = jnp.concatenate([qkv_weight[:, 0], out_weight.T, gains_cast], axis=1)
    gate_cast = gate_up_weight[:, 0].astype(jnp.bfloat16)
    up_cast = gate_up_weight[:, 1].astype(jnp.bfloat16)
    down_cast = down_weight.T.astype(jnp.bfloat16)
    attn_cast = attn_cast.astype(jnp.bfloat16)
    first, gate_cast, up_cast, down_cast = lax.optimization_barrier(
        (trade(attn_cast, 0), gate_cast, up_cast, down_cast)
    )
    attn_pair = jnp.stack([attn_cast, first])
    near = (attn_pair, trade(attn_pair, 1))
    far = tuple(swap(part, "seq", 1) for part in near)
    down_one = trade(down_cast, 0)
    gate_one = trade(gate_cast, 0)
    down_pair, gate_pair = jnp.stack([down_cast, down_one]), jnp.stack([gate_cast, gate_one])
    down_pair_far, gate_pair_far = swap(down_pair, "seq", 1), swap(gate_pair, "seq", 1)
    down_two = trade(down_pair, 1)
    gate_two = trade(after(gate_pair, down_pair_far, gate_pair_far), 1)
    down_parts = (down_pair, down_two), (down_pair_far, swap(down_two, "seq", 1))
    gate_parts = (gate_pair, gate_two), (gate_pair_far, swap(gate_two, "seq", 1))
    up = lax.all_gather(up_cast, plane, axis=0, tiled=True)
    positions = core * tok_rows + jnp.arange(tok_rows, dtype=jnp.int32)
    cosine, sine = rope_tables(positions, HEAD_DIM)

    queries, pair, attn_in, gains = project(
        place, stream, near, far, cosine, sine, up_cast
    )
    behind = from_behind(pair, "seq", 1)
    attended, attn_part = attend(
        place, queries, pair, behind, near, far, stream.shape[1], down_one
    )
    attn_out = tensor_sum(attn_part)
    ffn_in, hidden, by_gate, by_up, ffn_part = ffn_forward(
        place, attn_out, stream, gains, up, gate_parts, down_parts
    )
    ffn_out = tensor_sum(ffn_part)

    gate = arrange(place, *gate_parts)
    down = arrange(place, *down_parts)
    att_both = jnp.concatenate([attended, swap(attended, "seq", 1)], axis=0)
    attn_in_both = both_cores(attn_in)
    ffn_in_both = both_cores(ffn_in)
    hidden_both = jnp.concatenate([hidden, swap(hidden, "seq", 1)], axis=0)
    grad_ffn, grad_gate, grad_up, gain_ffn, grad_ffn_part = ffn_back(
        ffn_out, top, gains, gate, up, down, by_gate, by_up, att_both, attn_in_both, ffn_in_both,
        hidden_both
    )
    grad_ffn_in = tensor_sum(grad_ffn_part)
    grad_gate_both = jnp.concatenate([grad_gate, swap(grad_gate, "seq", 1)], axis=0)
    grad_up_both = jnp.concatenate([grad_up, swap(grad_up, "seq", 1)], axis=0)
    down_local = weight_local(both_cores(grad_ffn), hidden_both)
    gate_local = weight_local(ffn_in_both, grad_gate_both)
    up_local = weight_local(ffn_in_both, grad_up_both)
    down_state = scatter_begin(down_local)
    gate_state = scatter_begin(gate_local)
    up_got = trade(jnp.stack([up_local[1], up_local[3]]), 0)
    down_grad = scatter_end(down_state)

    grad_mid, grad_attn, grad_att, gain_mid = mid_back(
        place, grad_ffn_in, stream, attn_out, top, gains, near, far, down_state[2], gate_state[1]
    )
    gate_grad = scatter_end(gate_state)
    grad_q, grad_own, grad_old = attend_back(
        place, queries, pair, behind, attended, grad_att, cosine, sine
    )
    grad_ahead = from_behind(grad_old, "seq", -1)
    grad_proj, grad_attn_part, gain_attn = project_back(
        place, grad_q, grad_own, grad_ahead, cosine, sine, stream, near, far, down_grad[2], up_got
    )
    grad_attn_in = tensor_sum(grad_attn_part)
    grad_attn, gain_mid, up_got, down_grad = after(
        (grad_attn, gain_mid, up_got, down_grad), grad_attn_part
    )
    up_grad = scatter_end(scatter_begin(up_local, up_got))
    gate_up_grad = join(gate_grad, up_grad)

    out_local = weight_local(both_cores(grad_attn), att_both)
    out_grad = scatter_end(scatter_begin(out_local))
    proj_both = jnp.concatenate([grad_proj, swap(grad_proj, "seq", 1)], axis=0)
    qkv_local = weight_local(attn_in_both, proj_both)
    qkv_grad = sum(part.astype(jnp.float32) for part in scatter_end(scatter_begin(qkv_local)))[:, None]
    gains_rest = jnp.concatenate([gain_mid, gain_ffn[None]], axis=0).sum(axis=1)
    gains_rest = jnp.where(lax.axis_index("tensor") == 0, gains_rest, 0.0)
    gains_total = everywhere_sum(jnp.concatenate([gain_attn.sum(axis=0)[None], gains_rest], axis=0))
    own_columns = norm_gains.shape[1]
    gains_grad = lax.dynamic_slice_in_dim(
        gains_total, (chip * 2 + core) * own_columns, own_columns, axis=1
    )
    attn_float = attn_out.astype(jnp.float32)
    mid_stream = stream.astype(jnp.float32) + rms_norm(attn_float, gains[1])
    layer_out = (mid_stream + rms_norm(ffn_out.astype(jnp.float32), gains[3])).astype(jnp.bfloat16)
    qkv_shape, gate_up_shape = qkv_weight.shape, gate_up_weight.shape
    qkv_new, qkv_first_new, qkv_second_new = (
        unflat(value, qkv_shape)
        for value in adam(
            [flat(qkv_grad)], flat(qkv_weight), flat(qkv_first), flat(qkv_second), decay_rate
        )
    )
    out_new, out_first_new, out_second_new, out_grad = adam(
        out_grad, out_weight.T, out_first.T, out_second.T, decay_rate
    )
    gate_up_new, gate_up_first_new, gate_up_second_new = (
        unflat(value, gate_up_shape)
        for value in adam(
            [flat(gate_up_grad)],
            flat(gate_up_weight),
            flat(gate_up_first),
            flat(gate_up_second),
            decay_rate,
        )
    )
    down_new, down_first_new, down_second_new, down_grad = adam(
        down_grad, down_weight.T, down_first.T, down_second.T, decay_rate
    )
    gains_new, gains_first_new, gains_second_new = adam_step(
        norm_gains, gains_grad, gains_first, gains_second, 0.0
    )
    input_grad = stream_back(
        grad_attn_in, stream, gains, grad_mid, qkv_new, out_new, gate_up_new, down_new, gains_new
    )
    return (
        layer_out[None],
        input_grad[None],
        qkv_grad,
        out_grad.T,
        gate_up_grad,
        down_grad.T,
        gains_grad,
        qkv_new,
        out_new.T,
        gate_up_new,
        down_new.T,
        gains_new,
        qkv_first_new,
        out_first_new.T,
        gate_up_first_new,
        down_first_new.T,
        gains_first_new,
        qkv_second_new,
        out_second_new.T,
        gate_up_second_new,
        down_second_new.T,
        gains_second_new,
    )


def on_device(
    layer_in,
    cotangent,
    qkv_weight,
    out_weight,
    gate_up_weight,
    down_weight,
    norm_gains,
    qkv_first,
    out_first,
    gate_up_first,
    down_first,
    gains_first,
    qkv_second,
    out_second,
    gate_up_second,
    down_second,
    gains_second,
):
    tok_rows = layer_in.shape[1]
    seq_index = lax.axis_index("seq")
    collected = (
        lax.all_gather(qkv_weight.astype(jnp.bfloat16), ("batch", "seq"), axis=0, tiled=True),
        lax.all_gather(out_weight.astype(jnp.bfloat16), ("batch", "seq"), axis=1, tiled=True),
        lax.all_gather(gate_up_weight.astype(jnp.bfloat16), ("batch", "seq"), axis=0, tiled=True),
        lax.all_gather(down_weight.astype(jnp.bfloat16), ("batch", "seq"), axis=1, tiled=True),
        lax.all_gather(norm_gains.astype(jnp.bfloat16), ("batch", "seq"), axis=1, tiled=True),
    )
    qkv_full, out_full, gate_up_full, down_full, gains_full = collected
    model_width = qkv_full.shape[0]
    kv_local = qkv_full.shape[1]
    heads_local = kv_local * GROUP
    ffn_local = gate_up_full.shape[2]
    qkv_flat = qkv_full.reshape(model_width, kv_local * (GROUP + 2) * HEAD_DIM)
    gate_up_flat = gate_up_full.reshape(model_width, 2 * ffn_local)
    gains_float = gains_full.astype(jnp.float32)
    positions = seq_index * tok_rows + jnp.arange(tok_rows, dtype=jnp.int32)
    cosine, sine = rope_tables(positions, HEAD_DIM)
    key_positions = (seq_index - WIN_BLOCKS) * tok_rows + jnp.arange(
        (WIN_BLOCKS + 1) * tok_rows, dtype=jnp.int32
    )
    spread = positions[:, None] - key_positions[None, :]
    allowed = (spread >= 0) & (spread < WIN_BLOCKS * tok_rows) & (key_positions >= 0)[None, :]
    mask = allowed[None, None]
    stream = layer_in[0].astype(jnp.float32)
    attn_in = rms_norm(stream, gains_float[0]).astype(jnp.bfloat16)
    projected = jnp.dot(attn_in, qkv_flat, preferred_element_type=jnp.float32).reshape(
        tok_rows, kv_local, GROUP + 2, HEAD_DIM
    )
    queries = rotate(
        projected[:, :, :GROUP].reshape(tok_rows, heads_local, HEAD_DIM), cosine, sine
    ).astype(jnp.bfloat16)
    keys = rotate(projected[:, :, GROUP], cosine, sine).astype(jnp.bfloat16)
    values = projected[:, :, GROUP + 1].astype(jnp.bfloat16)
    kv_pair = jnp.stack([keys, values], axis=0)
    reach = min(WIN_BLOCKS, lax.axis_size("seq") - 1)
    pieces = []
    for distance in range(WIN_BLOCKS, 0, -1):
        if distance <= reach:
            pieces.append(from_behind(kv_pair, "seq", distance))
        else:
            pieces.append(jnp.zeros_like(kv_pair))
    pieces.append(kv_pair)
    extended = jnp.concatenate(pieces, axis=1)
    ext_keys = extended[0]
    ext_values = extended[1]
    query_groups = queries.reshape(tok_rows, kv_local, GROUP, HEAD_DIM)
    capped = capped_scores(query_groups, ext_keys)
    log_sums = jnp.log(jnp.sum(jnp.where(mask, jnp.exp(capped), 0.0), axis=-1))
    probs = jnp.where(mask, jnp.exp(capped - log_sums[..., None]), 0.0).astype(jnp.bfloat16)
    attended = jnp.einsum(
        "cgij,jcd->icgd", probs, ext_values, preferred_element_type=jnp.float32
    ).astype(jnp.bfloat16)
    att_flat = attended.reshape(tok_rows, heads_local * HEAD_DIM)
    attn_out = lax.psum(jnp.dot(att_flat, out_full, preferred_element_type=jnp.float32), "tensor")
    mid_stream = stream + rms_norm(attn_out, gains_float[1])
    ffn_in = rms_norm(mid_stream, gains_float[2]).astype(jnp.bfloat16)
    gate_up = jnp.dot(ffn_in, gate_up_flat, preferred_element_type=jnp.float32).reshape(
        tok_rows, 2, ffn_local
    )
    hidden = geglu(gate_up[:, 0], gate_up[:, 1]).astype(jnp.bfloat16)
    ffn_out = lax.psum(jnp.dot(hidden, down_full, preferred_element_type=jnp.float32), "tensor")
    layer_out = (mid_stream + rms_norm(ffn_out, gains_float[3])).astype(jnp.bfloat16)
    grad_top = cotangent[0].astype(jnp.float32)
    grad_ffn_out, gain_three = norm_back(ffn_out, gains_float[3], grad_top)
    grad_ffn = grad_ffn_out.astype(jnp.bfloat16)
    grad_hidden = cols_product(grad_ffn, down_full)
    _, geglu_pull = jax.vjp(geglu, gate_up[:, 0], gate_up[:, 1])
    grad_gate, grad_up = geglu_pull(grad_hidden)
    grad_gate_up = (
        jnp.stack([grad_gate, grad_up], axis=1)
        .reshape(tok_rows, 2 * ffn_local)
        .astype(jnp.bfloat16)
    )
    grad_ffn_in = lax.psum(cols_product(grad_gate_up, gate_up_flat), "tensor")
    grad_mid_norm, gain_two = norm_back(mid_stream, gains_float[2], grad_ffn_in)
    grad_mid = grad_top + grad_mid_norm
    grad_attn_out, gain_one = norm_back(attn_out, gains_float[1], grad_mid)
    grad_attn = grad_attn_out.astype(jnp.bfloat16)
    grad_att = (
        cols_product(grad_attn, out_full)
        .astype(jnp.bfloat16)
        .reshape(tok_rows, kv_local, GROUP, HEAD_DIM)
    )
    capped_again = capped_scores(query_groups, ext_keys)
    probs_float = jnp.where(mask, jnp.exp(capped_again - log_sums[..., None]), 0.0)
    probs_again = probs_float.astype(jnp.bfloat16)
    delta = jnp.einsum("icgd,icgd->cgi", grad_att, attended, preferred_element_type=jnp.float32)
    grad_probs = jnp.einsum(
        "icgd,jcd->cgij", grad_att, ext_values, preferred_element_type=jnp.float32
    )
    grad_scores = (
        probs_float * (grad_probs - delta[..., None]) * (1.0 - (capped_again / soft_cap) ** 2)
    ).astype(jnp.bfloat16)
    score_scale = HEAD_DIM ** (-0.5)
    grad_values_ext = jnp.einsum(
        "cgij,icgd->jcd", probs_again, grad_att, preferred_element_type=jnp.float32
    )
    grad_keys_ext = (
        jnp.einsum("cgij,icgd->jcd", grad_scores, query_groups, preferred_element_type=jnp.float32)
        * score_scale
    )
    grad_queries = (
        jnp.einsum("cgij,jcd->icgd", grad_scores, ext_keys, preferred_element_type=jnp.float32)
        * score_scale
    )
    grad_pair_ext = jnp.stack([grad_keys_ext, grad_values_ext], axis=0)
    grad_pair = grad_pair_ext[:, WIN_BLOCKS * tok_rows :]
    for distance in range(1, reach + 1):
        start = (WIN_BLOCKS - distance) * tok_rows
        piece = grad_pair_ext[:, start : start + tok_rows]
        grad_pair = grad_pair + from_behind(piece.astype(jnp.bfloat16), "seq", -distance).astype(
            piece.dtype
        )
    grad_queries = rotate(
        grad_queries.reshape(tok_rows, heads_local, HEAD_DIM), cosine, -sine
    ).reshape(tok_rows, kv_local, GROUP, HEAD_DIM)
    grad_keys = rotate(grad_pair[0], cosine, -sine)
    grad_values = grad_pair[1]
    grad_proj = (
        jnp.concatenate([grad_queries, grad_keys[:, :, None], grad_values[:, :, None]], axis=2)
        .reshape(tok_rows, kv_local * (GROUP + 2) * HEAD_DIM)
        .astype(jnp.bfloat16)
    )
    grad_attn_in = lax.psum(
        cols_product(grad_proj, qkv_flat).astype(jnp.bfloat16), "tensor"
    ).astype(jnp.float32)
    grad_stream_norm, gain_zero = norm_back(stream, gains_float[0], grad_attn_in)
    input_grad = grad_mid + grad_stream_norm
    qkv_local = rows_product(attn_in, grad_proj).reshape(
        model_width, kv_local, (GROUP + 2) * HEAD_DIM
    )
    out_local = rows_product(att_flat, grad_attn)
    gate_up_local = rows_product(ffn_in, grad_gate_up).reshape(model_width, 2, ffn_local)
    down_local = rows_product(hidden, grad_ffn)
    gains_local = jnp.stack([gain_zero, gain_one, gain_two, gain_three])
    summed = (
        lax.psum_scatter(
            qkv_local.astype(jnp.bfloat16), ("batch", "seq"), scatter_dimension=0, tiled=True
        ).astype(jnp.float32),
        lax.psum_scatter(
            out_local.astype(jnp.bfloat16), ("batch", "seq"), scatter_dimension=1, tiled=True
        ).astype(jnp.float32),
        lax.psum_scatter(
            gate_up_local.astype(jnp.bfloat16), ("batch", "seq"), scatter_dimension=0, tiled=True
        ).astype(jnp.float32),
        lax.psum_scatter(
            down_local.astype(jnp.bfloat16), ("batch", "seq"), scatter_dimension=1, tiled=True
        ).astype(jnp.float32),
        lax.psum_scatter(
            gains_local.astype(jnp.bfloat16), ("batch", "seq"), scatter_dimension=1, tiled=True
        ).astype(jnp.float32),
    )
    qkv_grad, out_grad, gate_up_grad, down_grad, gains_grad = summed
    qkv_new, qkv_first_new, qkv_second_new = adam_step(
        qkv_weight, qkv_grad, qkv_first, qkv_second, decay_rate
    )
    out_new, out_first_new, out_second_new = adam_step(
        out_weight, out_grad, out_first, out_second, decay_rate
    )
    gate_up_new, gate_up_first_new, gate_up_second_new = adam_step(
        gate_up_weight, gate_up_grad, gate_up_first, gate_up_second, decay_rate
    )
    down_new, down_first_new, down_second_new = adam_step(
        down_weight, down_grad, down_first, down_second, decay_rate
    )
    gains_new, gains_first_new, gains_second_new = adam_step(
        norm_gains, gains_grad, gains_first, gains_second, 0.0
    )
    return (
        layer_out[None],
        input_grad[None],
        qkv_grad,
        out_grad,
        gate_up_grad,
        down_grad,
        gains_grad,
        qkv_new,
        out_new,
        gate_up_new,
        down_new,
        gains_new,
        qkv_first_new,
        out_first_new,
        gate_up_first_new,
        down_first_new,
        gains_first_new,
        qkv_second_new,
        out_second_new,
        gate_up_second_new,
        down_second_new,
        gains_second_new,
    )


def solution(mesh):
    in_specs = (
        P("batch", "seq", None),
        P("batch", "seq", None),
        P(("batch", "seq"), "tensor", None),
        P("tensor", ("batch", "seq")),
        P(("batch", "seq"), None, "tensor"),
        P("tensor", ("batch", "seq")),
        P(None, ("batch", "seq")),
        P(("batch", "seq"), "tensor", None),
        P("tensor", ("batch", "seq")),
        P(("batch", "seq"), None, "tensor"),
        P("tensor", ("batch", "seq")),
        P(None, ("batch", "seq")),
        P(("batch", "seq"), "tensor", None),
        P("tensor", ("batch", "seq")),
        P(("batch", "seq"), None, "tensor"),
        P("tensor", ("batch", "seq")),
        P(None, ("batch", "seq")),
    )
    out_specs = (
        P("batch", "seq", None),
        P("batch", "seq", None),
        P(("batch", "seq"), "tensor", None),
        P("tensor", ("batch", "seq")),
        P(("batch", "seq"), None, "tensor"),
        P("tensor", ("batch", "seq")),
        P(None, ("batch", "seq")),
        P(("batch", "seq"), "tensor", None),
        P("tensor", ("batch", "seq")),
        P(("batch", "seq"), None, "tensor"),
        P("tensor", ("batch", "seq")),
        P(None, ("batch", "seq")),
        P(("batch", "seq"), "tensor", None),
        P("tensor", ("batch", "seq")),
        P(("batch", "seq"), None, "tensor"),
        P("tensor", ("batch", "seq")),
        P(None, ("batch", "seq")),
        P(("batch", "seq"), "tensor", None),
        P("tensor", ("batch", "seq")),
        P(("batch", "seq"), None, "tensor"),
        P("tensor", ("batch", "seq")),
        P(None, ("batch", "seq")),
    )
    sizes = tuple(mesh.shape[axis] for axis in ("batch", "seq", "tensor"))
    body = on_square if sizes == (4, 2, 4) else on_device
    return jax.shard_map(
        body, mesh=mesh, in_specs=in_specs, out_specs=out_specs, check_vma=False
    )
```
